256 devices in a mesh: owner: 16 (over y_hi, x, core), rep: 16 (over z, y_lo).
Axes of the slice: x: 4, y: 4 (y_hi: 2, y_lo: 2; y = y_hi * 2 + y_lo), z: 8, core: 2. Of those that a mesh axis runs over, the one named last changes fastest.
Arguments:
- shots: bfloat16 [65536, 768], P(('owner', 'rep'))
- basis: float32 [65536, 64], P(('owner', 'rep'))
- round_masks: int32 [3], replicated, may hold values from 1 to 15, as said below
Outputs:
- iterate: float32 [65536, 64], P(('owner', 'rep'))
- ritz: float32 [64, 64], replicated
The draws below stay inside these ranges and needn't reach their ends.
Inputs may be any that keep to these rules, and one draw needn't show every extreme that they name: `round_masks`: the masks are distinct, so every round pairs every block with a different block.
All inputs are finite; a program needn't handle non-finite values.
Results may differ from the reference program's by a relative error of at most 0.0039.
Values may be sent and summed in bfloat16 or wider, within the bound.
A program may use at most 64 MiB of HBM per device.

```python
import math
import jax
import jax.numpy as jnp
from jax import lax

E = 768
K = 64
ROUNDS = 3
BLK = 4096
NROWS = 65536


def draw_shots(key, part):
    key = jax.random.fold_in(key, 11)
    key_scene, key_center, key_noise, key_column, key_row = jax.random.split(key, 5)
    scene = jax.random.randint(key_scene, (NROWS,), 0, 64)
    centers = jax.random.normal(key_center, (64, E), jnp.float32)
    share = 0.08
    noise = jax.random.normal(key_noise, (NROWS, E), jnp.float32)
    column_scale = jnp.exp(jax.random.uniform(key_column, (E,), jnp.float32, 0.0, math.log(10.0)))
    row_scale = jnp.exp(jax.random.uniform(key_row, (NROWS, 1), jnp.float32, 0.0, math.log(10.0)))
    values = math.sqrt(share) * jnp.take(centers, scene, axis=0) + math.sqrt(1.0 - share) * noise
    return (values * column_scale[None, :] * row_scale).astype(jnp.bfloat16)


def draw_basis(key, part):
    key = jax.random.fold_in(key, 12)
    key_main = jax.random.fold_in(key, 0)
    ramp = jnp.exp(math.log(3.0) * jnp.arange(NROWS, dtype=jnp.float32) / NROWS)[:, None]
    values = jax.random.normal(key_main, (NROWS, K), jnp.float32)
    return (values * ramp).astype(jnp.float32)


def draw_round_masks(key, part):
    key = jax.random.fold_in(key, 13)
    key_order, key_place = jax.random.split(key, 2)
    owner_count = NROWS // BLK
    others = jax.random.permutation(key_order, max(owner_count - 2, 1)) + 1
    place = jax.random.randint(key_place, (), 0, ROUNDS)
    slots = jnp.arange(ROUNDS, dtype=jnp.int32)
    index = jnp.clip(slots - (slots > place).astype(jnp.int32), 0, max(owner_count - 3, 0))
    masks = jnp.where(slots == place, owner_count - 1, others[index])
    return masks.astype(jnp.int32)


def setup_inputs(seed: int = 0) -> dict:
    key_of = jax.random.split(jax.random.key(seed), 4)
    return {
        "shots": draw_shots(jax.random.fold_in(key_of[3], 71), 0),
        "basis": draw_basis(jax.random.fold_in(key_of[3], 71), 0),
        "round_masks": draw_round_masks(jax.random.fold_in(key_of[3], 71), 0),
    }


sharpness = 1.6

def normalize(shots):
    values = shots.astype(jnp.float32)
    scale = lax.rsqrt(lax.optimization_barrier(jnp.mean(values * values, axis=-1, keepdims=True)) + 1e-06)
    return (values * scale).astype(jnp.bfloat16)

def apply_inverse(lower_factor, values):
    return lax.linalg.triangular_solve(lower_factor, values, left_side=False, lower=True, transpose_a=True)

def reference(shots, basis, round_masks):
    owner_count = NROWS // BLK
    unit_blocks = normalize(shots).reshape(owner_count, BLK, E)
    owners = jnp.arange(owner_count, dtype=jnp.int32)
    iterate = basis
    ritz_sum = jnp.zeros((K, K), jnp.float32)
    for round_index in range(ROUNDS):
        partners = jnp.bitwise_xor(owners, round_masks[round_index]).astype(jnp.int32)
        iter_blocks = iterate.reshape(owner_count, BLK, K)

        def one_block(owner):
            mine = unit_blocks[owner]
            theirs = unit_blocks[partners[owner]]
            their_values = iter_blocks[partners[owner]]
            scores = lax.dot_general(mine.astype(jnp.float32), theirs.astype(jnp.float32), (((1,), (1,)), ((), ())), preferred_element_type=jnp.float32)
            affinity = jnp.exp(scores * (sharpness / math.sqrt(E)))
            totals = lax.optimization_barrier(jnp.sum(affinity, axis=1))
            product = jnp.dot(affinity.astype(jnp.float32), their_values.astype(jnp.float32), precision=lax.Precision.HIGHEST, preferred_element_type=jnp.float32)
            return product / totals[:, None]
        carried = lax.map(one_block, owners).reshape(NROWS, K)
        grown_rows = iterate + carried
        gram_sum = lax.dot_general(grown_rows.astype(jnp.float32), grown_rows.astype(jnp.float32), (((0,), (0,)), ((), ())), precision=lax.Precision.HIGHEST, preferred_element_type=jnp.float32) / NROWS
        ritz_sum = lax.dot_general(iterate.astype(jnp.float32), grown_rows.astype(jnp.float32), (((0,), (0,)), ((), ())), precision=lax.Precision.HIGHEST, preferred_element_type=jnp.float32) / NROWS
        lower_factor = jnp.linalg.cholesky(gram_sum)
        iterate = apply_inverse(lower_factor, grown_rows)
    return (iterate, ritz_sum)
```

```python
import math

import jax
import jax.numpy as jnp
from jax import lax
from jax.sharding import PartitionSpec as P

ROUNDS = 3


sharpness = 1.6


def swapped_2(shard, axis, distance):
    return lax.ppermute(shard, axis, [(i, i ^ 1 << distance) for i in range(lax.axis_size(axis))])


def normalize(shots):
    values = shots.astype(jnp.float32)
    scale = lax.rsqrt(jnp.mean(values * values, axis=-1, keepdims=True) + 1e-06)
    return (values * scale).astype(jnp.bfloat16)


def to_partner(values, mask, owner_bits):
    for bit in range(owner_bits):
        flag = mask // 2**bit % 2 == 1
        values = jnp.where(flag, swapped_2(values, "owner", bit), values)
    return values


def dot_tn(a, b):
    return lax.dot_general(
        a, b, (((0,), (0,)), ((), ())), precision=lax.Precision.HIGHEST, preferred_element_type=jnp.float32
    )


def shards(shots, basis, round_masks):
    row_count, feature_count = shots.shape
    owner_bits = lax.axis_size("owner").bit_length() - 1
    total_rows = float(lax.axis_size("owner") * lax.axis_size("rep") * row_count)
    score_scale = sharpness / math.sqrt(feature_count)
    unit_rows = normalize(shots)
    own_units = lax.all_gather(unit_rows, "rep", axis=0, tiled=True)
    affinities = []
    for t in range(ROUNDS):
        theirs = to_partner(unit_rows, round_masks[t], owner_bits)
        scores = lax.dot_general(
            theirs, own_units, (((1,), (1,)), ((), ())), preferred_element_type=jnp.float32
        )
        affinities.append(jnp.exp(scores * score_scale).astype(jnp.bfloat16))
    grown = basis
    before = basis
    for t in range(ROUNDS):
        before = grown
        whole = lax.all_gather(grown.astype(jnp.bfloat16), "rep", axis=0, tiled=True)
        totals = jnp.sum(affinities[t].astype(jnp.float32), axis=1, keepdims=True)
        carried = jnp.dot(affinities[t], whole, preferred_element_type=jnp.float32) / totals
        grown = before + to_partner(carried, round_masks[t], owner_bits)
    both = jnp.concatenate([before, grown], axis=1)
    k = basis.shape[1]
    sums = lax.psum(dot_tn(both, both), ("owner", "rep")) / total_rows
    lower = jnp.linalg.cholesky(jnp.stack([sums[:k, :k], sums[k:, k:]]))
    iterate = lax.linalg.triangular_solve(lower[1], grown, left_side=False, lower=True, transpose_a=True)
    half = lax.linalg.triangular_solve(lower[0], sums[:k, k:], left_side=True, lower=True)
    ritz = lax.linalg.triangular_solve(lower[0], half, left_side=False, lower=True, transpose_a=True)
    return (iterate, ritz)


def solution(mesh):
    in_specs = (P(("owner", "rep"), None), P(("owner", "rep"), None), P())
    out_specs = (P(("owner", "rep"), None), P())
    return jax.shard_map(shards, mesh=mesh, in_specs=in_specs, out_specs=out_specs, check_vma=False)
```

```python
import functools
import math

import jax
import jax.numpy as jnp
from jax import lax
from jax.experimental import pallas as pl
from jax.experimental.pallas import tpu as pltpu
from jax.sharding import PartitionSpec as P

ROUNDS = 3
SHARPNESS = 1.6
MESH = pl.DeviceIdType.MESH
NT = (((1,), (1,)), ((), ()))
TN = (((0,), (0,)), ((), ()))
NX, NZ = 4, 8


def dot32(a, b, dims):
    return lax.dot_general(a, b, dims, precision=lax.Precision.HIGHEST, preferred_element_type=jnp.float32)


def pack(rows):
    half = rows.shape[0] // 2
    return jnp.concatenate([rows[:half], rows[half:]], axis=1)


def rounds_kernel(
    scale, masks, shots, basis, grown_out, sums_out,
    own, oth, stage, sib_stage, theirs, aff, gpart, gfull, xbufs, ybufs, rs, ys, zs, fin, prod,
    s1, r1, sg, rg, sc, rc, sa, ra,
):
    n, feat = shots.shape
    half, quarter = n // 2, n // 4
    k = basis.shape[1]
    o, r = lax.axis_index("owner"), lax.axis_index("rep")
    c, x, yh = o % 2, (o // 2) % NX, o // (2 * NX)
    z, yl = r // 2, r % 2
    y, q = yh * 2 + yl, o % (2 * NX)

    def dev(yh=yh, x=x, c=c, z=z, yl=yl):
        return ((yh * NX + x) * 2 + c, z * 2 + yl)

    sibling = dev(yl=1 - yl)

    bar = pltpu.get_barrier_semaphore()

    def hello(device):
        pl.semaphore_signal(bar, inc=1, device_id=device, device_id_type=MESH)

    @pl.loop(1, NZ)
    def _(i):
        hello((o, ((z + i) % NZ) * 2 + yl))

    @pl.loop(1, 2 * NX)
    def _(i):
        hello((yh * 2 * NX + (q + i) % (2 * NX), r))

    @pl.loop(1, 4)
    def _(i):
        there = (y + i) % 4
        hello(((there // 2) * 2 * NX + q, z * 2 + there % 2))

    hello(dev(yh=1 - yh, c=1 - c))

    values = shots[...].astype(jnp.float32)
    inv = lax.rsqrt(jnp.mean(values * values, axis=-1, keepdims=True) + 1e-06)
    units = (values * inv).astype(jnp.bfloat16)
    own[r] = units
    oth[yh, x] = units
    g0 = pack(basis[...])
    gpart[0, r] = g0.astype(jnp.bfloat16)
    pl.semaphore_wait(bar, (NZ - 1) + (2 * NX - 1) + 3 + 1)

    def send(src, dst, ssem, rsem, device):
        return pltpu.make_async_remote_copy(
            src_ref=src, dst_ref=dst, send_sem=ssem, recv_sem=rsem, device_id=device, device_id_type=MESH
        )

    pending = []

    def same(ref, number, device):
        copy = send(ref, ref, s1.at[number], r1.at[number], device)
        pending.append(copy)
        copy.start()

    def landed(ref, number):
        send(ref, ref, s1.at[number], r1.at[number], sibling).wait_recv()

    full, low, high = pl.ds(0, n), pl.ds(0, half), pl.ds(half, half)
    low_a, low_b = pl.ds(0, quarter), pl.ds(quarter, quarter)

    def col(distance, column):
        return ((z + NZ + distance) % NZ) * 2 + column

    YH, XR, XL, XR2, XL2, HR, HL, HR2, HL2 = range(9)
    SIB0 = 9
    UP, DN, UPS, DNS = 18, 22, 26, 30
    CORE = 34
    up, down = dev(z=(z + 1) % NZ), dev(z=(z + NZ - 1) % NZ)
    right, left = dev(x=(x + 1) % NX), dev(x=(x + NX - 1) % NX)

    def g_send(t):
        mine = gpart.at[t, r]

        @pl.loop(1, NZ)
        def _(i):
            send(mine, mine, sg.at[t, i], rg.at[t, i], (o, ((z + i) % NZ) * 2 + yl)).start()

        send(mine, mine, sg.at[t, 8], rg.at[t, 8], sibling).start()

    lane = lax.broadcasted_iota(jnp.int32, (half, 128), 1)

    def unpack(t, item):
        p = gpart[t, item].astype(jnp.float32)
        tail = jnp.where(lane == k, 1.0, 0.0)
        at = pl.multiple_of(item * n, n)
        gfull[pl.ds(at, half), :] = jnp.where(lane < k, p, tail).astype(jnp.bfloat16)
        gfull[pl.ds(at + half, half), :] = jnp.where(lane < k, pltpu.roll(p, 128 - k, 1), tail).astype(jnp.bfloat16)

    def near(j):
        return (NZ + (1 - 2 * ((j + 1) % 2)) * ((j + 1) // 2)) % NZ

    def g_receive(t):
        unpack(t, r)

        @pl.loop(1, NZ)
        def _(j):
            i = near(j)
            item = col(-i, yl)
            ref = gpart.at[t, item]
            send(ref, ref, sg.at[t, i], rg.at[t, i], sibling).wait_recv()
            send(ref, ref, sg.at[t, 8 + i], rg.at[t, 8 + i], sibling).start()
            unpack(t, item)

        @pl.loop(0, NZ)
        def _(j):
            i = near(j)
            item = col(-i, 1 - yl)
            ref = gpart.at[t, item]
            send(ref, ref, sg.at[t, 8 + i], rg.at[t, 8 + i], sibling).wait_recv()
            unpack(t, item)

        @pl.loop(1, 2 * NZ)
        def _(i):
            ref = gpart.at[t, r]
            send(ref, ref, sg.at[t, i], rg.at[t, i], sibling).wait_send()

    mine, other = oth.at[yh, x], oth.at[1 - yh, x]
    same(mine, YH, dev(yh=1 - yh))
    same(mine, XR, right)
    same(mine, XL, left)
    same(own.at[r, low], SIB0 + 8, sibling)
    same(own.at[r], UP, up)
    same(own.at[r], DN, down)
    g_send(0)

    landed(own.at[col(0, 1 - yl), low], SIB0 + 8)
    same(own.at[col(0, 1 - yl), low], UPS, up)
    same(own.at[col(0, 1 - yl), low], DNS, down)
    same(own.at[r, high], SIB0, sibling)

    xl, xr, xo = (x + NX - 1) % NX, (x + 1) % NX, (x + 2) % NX

    def x_first(hi, a, b, a2, b2):
        landed(oth.at[hi, xl], a)
        same(oth.at[hi, xl, low], a2, right)
        landed(oth.at[hi, xr], b)
        same(oth.at[hi, xr, high], b2, left)

    def x_last(hi, a2, b2):
        landed(oth.at[hi, xo, low], a2)
        landed(oth.at[hi, xo, high], b2)

    def z_own(s):
        a, b = col(-s, yl), col(s, yl)
        if s < 4:
            landed(own.at[a], UP + s - 1)
            same(own.at[a] if s < 3 else own.at[a, low], UP + s, up)
            same(own.at[a, high], SIB0 + s, sibling)
            landed(own.at[b], DN + s - 1)
            same(own.at[b] if s < 3 else own.at[b, high], DN + s, down)
            same(own.at[b, high], SIB0 + NZ - s, sibling)
        else:
            landed(own.at[a, high], DN + 3)
            same(own.at[a, high], SIB0 + 4, sibling)
            landed(own.at[a, low], UP + 3)

    def z_sib(s):
        a, b = col(-s, 1 - yl), col(s, 1 - yl)
        if s < 4:
            landed(own.at[a, low], UPS + s - 1)
            same(own.at[a, low if s < 3 else low_a], UPS + s, up)
            landed(own.at[b, low], DNS + s - 1)
            same(own.at[b, low if s < 3 else low_b], DNS + s, down)
        else:
            landed(own.at[a, low_a], UPS + 3)
            landed(own.at[a, low_b], DNS + 3)

    x_first(yh, XR, XL, XR2, XL2)
    z_own(1)
    landed(other, YH)
    same(other, HR, right)
    same(other, HL, left)
    z_sib(1)
    x_last(yh, XR2, XL2)
    z_own(2)
    x_first(1 - yh, HR, HL, HR2, HL2)
    z_sib(2)
    x_last(1 - yh, HR2, HL2)

    for t in range(ROUNDS):
        m = masks[t]
        stage[t] = oth[yh ^ (m // 8), x ^ ((m // 2) % 4)]
    core_copy = send(stage, sib_stage, s1.at[CORE], r1.at[CORE], dev(c=1 - c))
    pending.append(core_copy)
    core_copy.start()
    core_copy.wait_recv()
    for t in range(ROUNDS):
        crossed = masks[t] % 2 == 1
        theirs[t] = jnp.where(crossed, sib_stage[t].astype(jnp.float32), stage[t].astype(jnp.float32)).astype(jnp.bfloat16)

    def affinity(item):
        rows = own[item]
        at = pl.multiple_of(item * n, n)
        for t in range(ROUNDS):
            scores = lax.dot_general(theirs[t], rows, NT, preferred_element_type=jnp.float32)
            aff[t, :, pl.ds(at, n)] = jnp.exp(scores * scale).astype(jnp.bfloat16)

    def own_range(lo, hi):
        @pl.loop(lo, hi)
        def _(j):
            affinity(col(near(j), yl))

    def sib_range(lo, hi):
        @pl.loop(lo, hi)
        def _(j):
            i = near(j)
            item = col(-i, 1 - yl)
            landed(own.at[item, high], SIB0 + i)
            affinity(item)

    own_range(0, 5)
    z_own(3)
    z_sib(3)
    own_range(5, 7)
    sib_range(0, 5)
    z_own(4)
    own_range(7, 8)
    sib_range(5, 7)
    z_sib(4)
    sib_range(7, 8)

    before, grown = g0, g0
    for t in range(ROUNDS):
        if t > 0:
            gpart[t, r] = grown.astype(jnp.bfloat16)
            g_send(t)
        g_receive(t)
        product = lax.dot_general(aff[t], gfull[...], (((1,), (0,)), ((), ())), preferred_element_type=jnp.float32)
        carried = product[:, :k] / product[:, k:k + 1]
        xbufs[t][x] = pack(carried).astype(jnp.bfloat16)
        for i in range(1, NX):
            ref = xbufs[t].at[x]
            send(ref, ref, sc.at[t, i - 1], rc.at[t, i - 1], dev(x=(x + i) % NX)).start()
        for i in range(1, NX):
            ref = xbufs[t].at[(x + NX - i) % NX]
            send(ref, ref, sc.at[t, i - 1], rc.at[t, i - 1], sibling).wait_recv()
        m = masks[t]
        ybufs[t][yh * 2 + c] = xbufs[t][x ^ ((m // 2) % 4)]
        for i in range(1, 4):
            ref = ybufs[t].at[yh * 2 + c]
            device = dev(yh=(yh + i // 2) % 2, c=(c + i % 2) % 2)
            send(ref, ref, sc.at[t, 2 + i], rc.at[t, 2 + i], device).start()
        for i in range(1, 4):
            ref = ybufs[t].at[((yh + i // 2) % 2) * 2 + (c + i % 2) % 2]
            send(ref, ref, sc.at[t, 2 + i], rc.at[t, 2 + i], sibling).wait_recv()
        came = ybufs[t][(yh ^ (m // 8)) * 2 + (c ^ (m % 2))].astype(jnp.float32)
        before, grown = grown, grown + came
    grown_out[...] = grown

    top = jnp.where(lane < k, before, pltpu.roll(grown, k, 1))
    bottom = jnp.where(lane < k, pltpu.roll(before, k, 1), grown)
    prod[...] = (dot32(top, top, TN) + dot32(bottom, bottom, TN)).reshape(prod.shape)

    def total(ref, count):
        value = ref[0]
        for i in range(1, count):
            value = value + ref[i]
        return value

    def q_dev(i):
        return (yh * 2 * NX + (q + i) % (2 * NX), r)

    nq = 2 * NX

    @pl.loop(1, nq)
    def _(i):
        send(prod.at[(q + i) % nq], rs.at[q], sa.at[i], ra.at[i], q_dev(i)).start()

    rs[q] = prod[q]

    @pl.loop(1, nq)
    def _(i):
        send(prod.at[0], rs.at[(q + nq - i) % nq], sa.at[i], ra.at[i], sibling).wait_recv()

    ys[y] = total(rs, nq)

    @pl.loop(1, 4)
    def _(i):
        there = (y + i) % 4
        device = ((there // 2) * nq + q, z * 2 + there % 2)
        send(ys.at[y], ys.at[y], sa.at[8 + i], ra.at[8 + i], device).start()

    @pl.loop(1, 4)
    def _(i):
        ref = ys.at[(y + 4 - i) % 4]
        send(ref, ref, sa.at[8 + i], ra.at[8 + i], sibling).wait_recv()

    zs[z] = total(ys, 4)

    @pl.loop(1, NZ)
    def _(i):
        send(zs.at[z], zs.at[z], sa.at[12 + i], ra.at[12 + i], (o, ((z + i) % NZ) * 2 + yl)).start()

    @pl.loop(1, NZ)
    def _(i):
        ref = zs.at[(z + NZ - i) % NZ]
        send(ref, ref, sa.at[12 + i], ra.at[12 + i], sibling).wait_recv()

    fin[q] = total(zs, NZ)

    @pl.loop(1, nq)
    def _(i):
        send(fin.at[q], fin.at[q], sa.at[20 + i], ra.at[20 + i], q_dev(i)).start()

    @pl.loop(1, nq)
    def _(i):
        ref = fin.at[(q + nq - i) % nq]
        send(ref, ref, sa.at[20 + i], ra.at[20 + i], sibling).wait_recv()

    sums_out[...] = fin[...].reshape(sums_out.shape)

    for copy in pending:
        copy.wait_send()
    for t in range(ROUNDS):
        for i in range(6):
            ref = xbufs[t].at[x]
            send(ref, ref, sc.at[t, i], rc.at[t, i], sibling).wait_send()

    @pl.loop(1, nq)
    def _(i):
        send(fin.at[q], fin.at[q], sa.at[i], ra.at[i], sibling).wait_send()
        send(fin.at[q], fin.at[q], sa.at[12 + i], ra.at[12 + i], sibling).wait_send()
        send(fin.at[q], fin.at[q], sa.at[20 + i], ra.at[20 + i], sibling).wait_send()

    @pl.loop(1, 4)
    def _(i):
        send(fin.at[q], fin.at[q], sa.at[8 + i], ra.at[8 + i], sibling).wait_send()


def inverse_factor(gram):
    k = gram.shape[0]
    row = lax.broadcasted_iota(jnp.int32, (k, 2 * k), 0)
    lane = lax.broadcasted_iota(jnp.int32, (k, 2 * k), 1)
    rows = lax.broadcasted_iota(jnp.int32, (k, 1), 0)
    work = jnp.concatenate([gram, jnp.where(lane == row, 1.0, 0.0)[:, :k]], axis=1)
    for i in range(k - 1):
        first = (i + 1) // 8 * 8
        pivot = work[i:i + 1, :] * (1.0 / work[i:i + 1, i:i + 1])
        rest = work[first:, :]
        factor = jnp.where(rows[first:] > i, rest[:, i:i + 1], 0.0)
        rest = rest - factor * pivot
        work = rest if first == 0 else jnp.concatenate([work[:first], rest], axis=0)
    diagonal = jnp.sum(jnp.where(lane == row, work, 0.0), axis=1, keepdims=True)
    return work[:, k:] * (1.0 / jnp.sqrt(diagonal))


def finish_kernel(total_rows, grown, sums, iterate, ritz):
    k = ritz.shape[0]
    half = grown.shape[0]
    every = sums[...] * (1.0 / total_rows)
    inv_before = inverse_factor(every[:k, :k])
    inv_last = inverse_factor(every[k:, k:])
    packed = grown[...]
    iterate[:half, :] = dot32(packed[:, :k], inv_last, NT)
    iterate[half:, :] = dot32(packed[:, k:], inv_last, NT)
    left = dot32(inv_before, every[:k, k:], (((1,), (0,)), ((), ())))
    ritz[...] = dot32(left, inv_before, NT)


def shards(shots, basis, round_masks):
    n, feat = shots.shape
    k = basis.shape[1]
    nrep, nown = lax.axis_size("rep"), lax.axis_size("owner")
    half = n // 2
    bf, f32 = jnp.bfloat16, jnp.float32
    vmem = pl.BlockSpec(memory_space=pltpu.VMEM)
    slab = (2 * k) // (2 * NX)
    dma = pltpu.SemaphoreType.DMA
    grown, sums = pl.pallas_call(
        functools.partial(rounds_kernel, SHARPNESS / math.sqrt(feat)),
        out_shape=(jax.ShapeDtypeStruct((half, 2 * k), f32), jax.ShapeDtypeStruct((2 * k, 2 * k), f32)),
        in_specs=[pl.BlockSpec(memory_space=pltpu.SMEM), vmem, vmem],
        out_specs=(vmem, vmem),
        scratch_shapes=[
            pltpu.VMEM((nrep, n, feat), bf),
            pltpu.VMEM((2, NX, n, feat), bf),
            pltpu.VMEM((ROUNDS, n, feat), bf),
            pltpu.VMEM((ROUNDS, n, feat), bf),
            pltpu.VMEM((ROUNDS, n, feat), bf),
            pltpu.VMEM((ROUNDS, n, nrep * n), bf),
            pltpu.VMEM((ROUNDS, nrep, half, 2 * k), bf),
            pltpu.VMEM((nrep * n, 2 * k), bf),
            [pltpu.VMEM((NX, half, 2 * k), bf)] * ROUNDS,
            [pltpu.VMEM((4, half, 2 * k), bf)] * ROUNDS,
            pltpu.VMEM((2 * NX, slab, 2 * k), f32),
            pltpu.VMEM((4, slab, 2 * k), f32),
            pltpu.VMEM((NZ, slab, 2 * k), f32),
            pltpu.VMEM((2 * NX, slab, 2 * k), f32),
            pltpu.VMEM((2 * NX, slab, 2 * k), f32),
            dma((35,)), dma((35,)),
            dma((ROUNDS, 16)), dma((ROUNDS, 16)),
            dma((ROUNDS, 6)), dma((ROUNDS, 6)),
            dma((28,)), dma((28,)),
        ],
        compiler_params=pltpu.CompilerParams(
            collective_id=0, has_side_effects=True, vmem_limit_bytes=48 * 1024 * 1024
        ),
        name="rounds",
    )(round_masks, shots, basis)
    return pl.pallas_call(
        functools.partial(finish_kernel, float(nown * nrep * n)),
        out_shape=(jax.ShapeDtypeStruct((n, k), f32), jax.ShapeDtypeStruct((k, k), f32)),
        in_specs=[vmem, vmem],
        out_specs=(vmem, vmem),
        name="finish",
    )(grown, sums)


def solution(mesh):
    in_specs = (P(("owner", "rep"), None), P(("owner", "rep"), None), P())
    out_specs = (P(("owner", "rep"), None), P())
    return jax.shard_map(shards, mesh=mesh, in_specs=in_specs, out_specs=out_specs, check_vma=False)
```

```python
import functools
import math

import jax
import jax.numpy as jnp
from jax import lax
from jax.experimental import pallas as pl
from jax.experimental.pallas import tpu as pltpu
from jax.sharding import PartitionSpec as P

ROUNDS = 3
SHARPNESS = 1.6
MESH = pl.DeviceIdType.MESH
NT = (((1,), (1,)), ((), ()))
TN = (((0,), (0,)), ((), ()))
NX, NY, NZ = 4, 4, 8


def dot32(a, b, dims):
    return lax.dot_general(a, b, dims, precision=lax.Precision.HIGHEST, preferred_element_type=jnp.float32)


def pack(rows):
    half = rows.shape[0] // 2
    return jnp.concatenate([rows[:half], rows[half:]], axis=1)


def rounds_kernel(
    scale, masks, shots, basis_t, grown_out, sums_out,
    unit, oth, own, stage, sib_stage, aff, gpart, gfull, wsend, wrecv, xbufs, ybufs, homeward, ghome, gsend, gback, gx, gy,
    rs, ys, zs, fin, prod,
    s1, r1, sg, rg, sc, rc, sw, rw, sa, ra,
):
    n, feat = shots.shape
    half, quarter = n // 2, n // 4
    k = basis_t.shape[0]
    o, r = lax.axis_index("owner"), lax.axis_index("rep")
    c, x, yh = o % 2, (o // 2) % NX, o // (2 * NX)
    z, yl = r // 2, r % 2
    y = yh * 2 + yl
    nq = 2 * NX
    q = x * 2 + c

    def dev(y=y, x=x, c=c, z=z):
        return (((y // 2) * NX + x) * 2 + c, z * 2 + y % 2)

    twin_y = yh * 2 + c
    twin = dev(y=twin_y, c=yl)
    other_core = dev(c=1 - c)
    moved = c != yl
    stays = c == yl

    bar = pltpu.get_barrier_semaphore()

    def hello(device):
        pl.semaphore_signal(bar, inc=1, device_id=device, device_id_type=MESH)

    @pl.loop(1, NZ)
    def _(i):
        hello(dev(z=(z + i) % NZ))

    @pl.loop(1, NX)
    def _(i):
        for core in range(2):
            hello(dev(x=(x + i) % NX, c=core))
            hello(dev(y=(y + i) % NY, c=core))

    hello(other_core)

    values = shots[...].astype(jnp.float32)
    inv = lax.rsqrt(jnp.mean(values * values, axis=-1, keepdims=True) + 1e-06)
    units = (values * inv).astype(jnp.bfloat16)
    g0 = pack(basis_t[...].T)

    @pl.when(stays)
    def _():
        oth[y, x] = units
        ghome[...] = g0

    @pl.when(moved)
    def _():
        unit[...] = units
        gsend[0] = g0

    pl.semaphore_wait(bar, (NZ - 1) + 2 * (NX - 1) + 2 * (NY - 1) + 1)

    def send(src, dst, ssem, rsem, device):
        return pltpu.make_async_remote_copy(
            src_ref=src, dst_ref=dst, send_sem=ssem, recv_sem=rsem, device_id=device, device_id_type=MESH
        )

    pending = []

    def move(src, dst, number, device):
        copy = send(src, dst, s1.at[number], r1.at[number], device)
        pending.append(copy)
        copy.start()

    def same(ref, number, device):
        move(ref, ref, number, device)

    def landed(ref, number):
        send(ref, ref, s1.at[number], r1.at[number], other_core).wait_recv()

    halves = (pl.ds(0, half), pl.ds(half, half))
    quarters = tuple((pl.ds(i * half, quarter), pl.ds(i * half + quarter, quarter)) for i in range(2))

    RING, UP, DN, CORE, TRADE = 0, 40, 47, 54, 57

    trades = [
        send(unit.at[halves[0]], oth.at[twin_y, x, halves[0]], s1.at[TRADE], r1.at[TRADE], twin),
        send(unit.at[halves[1]], oth.at[twin_y, x, halves[1]], s1.at[TRADE + 1], r1.at[TRADE + 1], twin),
        send(gsend.at[0], ghome, s1.at[TRADE + 2], r1.at[TRADE + 2], twin),
    ]

    @pl.when(moved)
    def _():
        for copy in trades:
            copy.start()

    def step(axis, i):
        return dev(x=(x + i) % NX) if axis == 0 else dev(y=(y + i) % NY)

    def at(axis, i, j):
        dx, dy = (i, j) if axis == 0 else (j, i)
        return (y + dy) % NY, (x + dx) % NX

    def ring(axis, h, j, first):
        return RING + 4 * ((5 * h) + (0 if first else 1 + j % 4))

    def begin(axis, h, j, first=False):
        number = ring(axis, h, j, first)
        ref = oth.at[(*at(axis, 0, j), halves[h])]
        same(ref, number, step(axis, 1))
        same(ref, number + 1, step(axis, -1 % 4))

    def onward(axis, h, j, first=False):
        number = ring(axis, h, j, first)
        landed(oth.at[(*at(axis, 3, j), halves[h])], number)
        same(oth.at[(*at(axis, 3, j), quarters[h][0])], number + 2, step(axis, 1))
        landed(oth.at[(*at(axis, 1, j), halves[h])], number + 1)
        same(oth.at[(*at(axis, 1, j), quarters[h][1])], number + 3, step(axis, 3))

    def last(axis, h, j, first=False):
        number = ring(axis, h, j, first)
        landed(oth.at[(*at(axis, 2, j), quarters[h][0])], number + 2)
        landed(oth.at[(*at(axis, 2, j), quarters[h][1])], number + 3)

    up, down = dev(z=(z + 1) % NZ), dev(z=(z + NZ - 1) % NZ)

    def z_begin(h):
        move(oth.at[y, x, halves[h]], own.at[z, halves[h]], UP + h, up)
        move(oth.at[y, x, halves[h]], own.at[z, halves[h]], DN + h, down)

    def z_on(s, h):
        a, b = (z + NZ - s) % NZ, (z + s) % NZ
        landed(own.at[a, halves[h]], UP + 2 * (s - 1) + h)
        if s < 3 or h == 0:
            same(own.at[a, halves[h]], UP + 2 * s + (h if s < 3 else 0), up)
        landed(own.at[b, halves[h]], DN + 2 * (s - 1) + h)
        if s < 3 or h == 1:
            same(own.at[b, halves[h]], DN + 2 * s + (h if s < 3 else 0), down)

    def z_last():
        a = (z + 4) % NZ
        landed(own.at[a, halves[0]], UP + 6)
        landed(own.at[a, halves[1]], DN + 6)

    for h in range(2):
        @pl.when(moved)
        def _(h=h):
            send(unit.at[halves[h]], oth.at[y, x, halves[h]], s1.at[TRADE + h], r1.at[TRADE + h], twin).wait_recv()

        begin(h, h, 0, first=True)
        z_begin(h)
        begin(1 - h, h, 0)

    onward(0, 0, 0, first=True)
    begin(1, 0, 3)
    begin(1, 0, 1)
    z_on(1, 0)
    onward(1, 1, 0, first=True)
    begin(0, 1, 3)
    begin(0, 1, 1)
    z_on(1, 1)
    onward(1, 0, 0)
    onward(0, 1, 0)
    last(0, 0, 0, first=True)
    begin(1, 0, 2)
    last(1, 1, 0, first=True)
    begin(0, 1, 2)
    z_on(2, 0)
    own[z] = oth[y, x]
    z_on(2, 1)
    onward(1, 0, 3)
    onward(0, 1, 3)
    last(1, 0, 0)
    last(0, 1, 0)
    onward(1, 0, 1)
    onward(0, 1, 1)
    z_on(3, 0)
    z_on(3, 1)

    @pl.when(moved)
    def _():
        send(gsend.at[0], ghome, s1.at[TRADE + 2], r1.at[TRADE + 2], twin).wait_recv()

    def g_send(t, value):
        gpart[t, z] = value.astype(jnp.bfloat16)

        @pl.loop(1, NZ)
        def _(i):
            send(gpart.at[t, z], gpart.at[t, z], sg.at[t, i], rg.at[t, i], dev(z=(z + i) % NZ)).start()

    grown = ghome[...]
    g_send(0, grown)

    onward(1, 0, 2)
    onward(0, 1, 2)
    last(1, 0, 3)
    last(0, 1, 3)
    last(1, 0, 1)
    last(0, 1, 1)
    last(1, 0, 2)
    last(0, 1, 2)

    def partner(t):
        m = masks[t]
        return y ^ ((m // 8) * 2 + m % 2), x ^ ((m // 2) % 4)

    for t in range(ROUNDS):
        py, px = partner(t)
        stage[t] = oth[py, px]
        move(stage.at[t], sib_stage.at[t], CORE + t, other_core)

    def affinity(t, rows, item, part):
        scores = lax.dot_general(rows, own[item], NT, preferred_element_type=jnp.float32)
        columns = pl.ds(pl.multiple_of(item * n, n), n)
        aff[t, part * n:(part + 1) * n, columns] = jnp.exp(scores * scale).astype(jnp.bfloat16)

    def affinities(t):
        @pl.loop(0, NZ)
        def _(item):
            affinity(t, stage[t], item, 0)

        landed(sib_stage.at[t], CORE + t)

        @pl.loop(0, NZ)
        def _(item):
            affinity(t, sib_stage[t], item, 1)

    z_last()
    affinities(0)

    lane = lax.broadcasted_iota(jnp.int32, (half, 2 * k), 1)
    tail = jnp.where(lane == k, 1.0, 0.0)

    def unpack(t, item):
        p = gpart[t, item].astype(jnp.float32)
        start = pl.multiple_of(item * n, n)
        gfull[pl.ds(start, half), :] = jnp.where(lane < k, p, tail).astype(jnp.bfloat16)
        gfull[pl.ds(start + half, half), :] = jnp.where(lane < k, pltpu.roll(p, k, 1), tail).astype(jnp.bfloat16)

    def near(j):
        return (NZ + (1 - 2 * ((j + 1) % 2)) * ((j + 1) // 2)) % NZ

    def carried(t):
        unpack(t, z)

        @pl.loop(1, NZ)
        def _(j):
            i = near(j)
            item = (z + NZ - i) % NZ
            ref = gpart.at[t, item]
            send(ref, ref, sg.at[t, i], rg.at[t, i], other_core).wait_recv()
            unpack(t, item)

        wsend[t] = jnp.dot(aff[t, n:, :], gfull[...], preferred_element_type=jnp.float32)
        copy = send(wsend.at[t], wrecv.at[t], sw.at[t], rw.at[t], other_core)
        copy.start()
        mine = jnp.dot(aff[t, :n, :], gfull[...], preferred_element_type=jnp.float32)
        copy.wait_recv()
        product = mine + wrecv[t]
        return pack(product[:, :k] / product[:, k:k + 1]).astype(jnp.bfloat16)

    def x_send(ref, sems, t, base):
        for i in range(1, NX):
            send(ref, ref, sems[0].at[t, base + i], sems[1].at[t, base + i], dev(x=(x + i) % NX)).start()

    def x_wait(buf, sems, t, base):
        for i in range(1, NX):
            ref = buf.at[(x + NX - i) % NX]
            send(ref, ref, sems[0].at[t, base + i], sems[1].at[t, base + i], other_core).wait_recv()

    def y_send(ref, sems, t, base):
        for i in range(1, NY):
            send(ref, ref, sems[0].at[t, base + i], sems[1].at[t, base + i], dev(y=(y + i) % NY)).start()

    def y_wait(buf, sems, t, base):
        for i in range(1, NY):
            ref = buf.at[(y + NY - i) % NY]
            send(ref, ref, sems[0].at[t, base + i], sems[1].at[t, base + i], other_core).wait_recv()

    csem = (sc, rc)
    for t in range(ROUNDS - 1):
        if t > 0:
            g_send(t, grown)
        py, px = partner(t)
        xbufs[t][x] = carried(t)
        x_send(xbufs[t].at[x], csem, t, 0)
        if t == 0:
            affinities(1)
        x_wait(xbufs[t], csem, t, 0)
        ybufs[t][y] = xbufs[t][px]
        y_send(ybufs[t].at[y], csem, t, 4)
        if t == 0:
            affinities(2)
        y_wait(ybufs[t], csem, t, 4)
        grown = grown + ybufs[t][py].astype(jnp.float32)

    t = ROUNDS - 1
    py, px = partner(t)
    g_send(t, grown)
    gx[x] = grown
    x_send(gx.at[x], csem, ROUNDS, 0)

    @pl.when(stays)
    def _():
        gback[...] = grown

    @pl.when(moved)
    def _():
        gsend[1] = grown
        send(gsend.at[1], gback, s1.at[TRADE + 3], r1.at[TRADE + 3], twin).start()

    x_wait(gx, csem, ROUNDS, 0)
    gy[y] = gx[px]
    y_send(gy.at[y], csem, ROUNDS, 4)
    came = carried(t)
    xbufs[t][x] = came
    x_send(xbufs[t].at[x], csem, t, 0)
    y_wait(gy, csem, ROUNDS, 4)
    before = gy[py]
    after = before + came.astype(jnp.float32)

    top = jnp.where(lane < k, before, pltpu.roll(after, k, 1))
    bottom = jnp.where(lane < k, pltpu.roll(before, k, 1), after)
    prod[...] = (dot32(top, top, TN) + dot32(bottom, bottom, TN)).reshape(prod.shape)

    def total(ref, count):
        value = ref[0]
        for i in range(1, count):
            value = value + ref[i]
        return value

    def q_dev(i):
        there = (q + i) % nq
        return dev(x=there // 2, c=there % 2)

    @pl.loop(1, nq)
    def _(i):
        send(prod.at[(q + i) % nq], rs.at[q], sa.at[i], ra.at[i], q_dev(i)).start()

    rs[q] = prod[q]

    x_wait(xbufs[t], csem, t, 0)
    homeward[...] = xbufs[t][px]

    @pl.when(stays)
    def _():
        ybufs[t][y] = homeward[...]

    def home_copy(i):
        ty = (y + i) % NY
        device = dev(y=(ty // 2) * 2 + c, c=ty % 2)
        return send(homeward, ybufs[t].at[y], sc.at[t, 4 + i], rc.at[t, 4 + i], device)

    @pl.when(moved)
    def _():
        home_copy(0).start()

    for i in range(1, NY):
        home_copy(i).start()

    @pl.loop(1, nq)
    def _(i):
        send(prod.at[0], rs.at[(q + nq - i) % nq], sa.at[i], ra.at[i], other_core).wait_recv()

    ys[y] = total(rs, nq)

    @pl.loop(1, NY)
    def _(i):
        send(ys.at[y], ys.at[y], sa.at[8 + i], ra.at[8 + i], dev(y=(y + i) % NY)).start()

    @pl.loop(1, NY)
    def _(i):
        ref = ys.at[(y + NY - i) % NY]
        send(ref, ref, sa.at[8 + i], ra.at[8 + i], other_core).wait_recv()

    zs[z] = total(ys, NY)

    @pl.loop(1, NZ)
    def _(i):
        send(zs.at[z], zs.at[z], sa.at[12 + i], ra.at[12 + i], dev(z=(z + i) % NZ)).start()

    @pl.loop(1, NZ)
    def _(i):
        ref = zs.at[(z + NZ - i) % NZ]
        send(ref, ref, sa.at[12 + i], ra.at[12 + i], other_core).wait_recv()

    fin[q] = total(zs, NZ)

    @pl.loop(1, nq)
    def _(i):
        send(fin.at[q], fin.at[q], sa.at[20 + i], ra.at[20 + i], q_dev(i)).start()

    @pl.when(moved)
    def _():
        send(gsend.at[1], gback, s1.at[TRADE + 3], r1.at[TRADE + 3], twin).wait_recv()
        ref = ybufs[t].at[twin_y]
        send(ref, ref, sc.at[t, 4], rc.at[t, 4], other_core).wait_recv()

    for i in range(1, NY):
        ref = ybufs[t].at[(twin_y + NY - i) % NY]
        send(ref, ref, sc.at[t, 4 + i], rc.at[t, 4 + i], other_core).wait_recv()
    m = masks[t]
    grown_out[...] = gback[...] + ybufs[t][twin_y ^ ((m // 8) * 2 + m % 2)].astype(jnp.float32)

    @pl.loop(1, nq)
    def _(i):
        ref = fin.at[(q + nq - i) % nq]
        send(ref, ref, sa.at[20 + i], ra.at[20 + i], other_core).wait_recv()

    sums_out[...] = fin[...].reshape(sums_out.shape)

    for copy in pending:
        copy.wait_send()

    @pl.when(moved)
    def _():
        for copy in trades:
            copy.wait_send()
        send(gsend.at[1], gback, s1.at[TRADE + 3], r1.at[TRADE + 3], twin).wait_send()
        home_copy(0).wait_send()

    @pl.loop(1, NX)
    def _(i):
        for row in range(ROUNDS):
            ref = xbufs[row].at[x]
            send(ref, ref, sc.at[row, i], rc.at[row, i], other_core).wait_send()
            send(ref, ref, sc.at[row, 4 + i], rc.at[row, 4 + i], other_core).wait_send()
        ref = gx.at[x]
        send(ref, ref, sc.at[ROUNDS, i], rc.at[ROUNDS, i], other_core).wait_send()
        send(ref, ref, sc.at[ROUNDS, 4 + i], rc.at[ROUNDS, 4 + i], other_core).wait_send()
        send(ys.at[y], ys.at[y], sa.at[8 + i], ra.at[8 + i], other_core).wait_send()

    @pl.loop(1, NZ)
    def _(i):
        for row in range(ROUNDS):
            ref = gpart.at[row, z]
            send(ref, ref, sg.at[row, i], rg.at[row, i], other_core).wait_send()
        for base in (0, 12, 20):
            send(fin.at[q], fin.at[q], sa.at[base + i], ra.at[base + i], other_core).wait_send()

    for row in range(ROUNDS):
        send(wsend.at[row], wrecv.at[row], sw.at[row], rw.at[row], other_core).wait_send()


def inverse_factor(gram):
    k = gram.shape[0]
    row = lax.broadcasted_iota(jnp.int32, (k, 2 * k), 0)
    lane = lax.broadcasted_iota(jnp.int32, (k, 2 * k), 1)
    rows = lax.broadcasted_iota(jnp.int32, (k, 1), 0)
    work = jnp.concatenate([gram, jnp.where(lane == row, 1.0, 0.0)[:, :k]], axis=1)
    for i in range(k - 1):
        first = (i + 1) // 8 * 8
        pivot = work[i:i + 1, :] * (1.0 / work[i:i + 1, i:i + 1])
        rest = work[first:, :]
        factor = jnp.where(rows[first:] > i, rest[:, i:i + 1], 0.0)
        rest = rest - factor * pivot
        work = rest if first == 0 else jnp.concatenate([work[:first], rest], axis=0)
    diagonal = jnp.sum(jnp.where(lane == row, work, 0.0), axis=1, keepdims=True)
    return work[:, k:] * (1.0 / jnp.sqrt(diagonal))


def finish_kernel(total_rows, grown, sums, iterate_t, ritz):
    k = ritz.shape[0]
    half = grown.shape[0]
    every = sums[...] * (1.0 / total_rows)
    inv_before = inverse_factor(every[:k, :k])
    inv_last = inverse_factor(every[k:, k:])
    packed = grown[...]
    iterate_t[:, :half] = dot32(inv_last, packed[:, :k], NT)
    iterate_t[:, half:] = dot32(inv_last, packed[:, k:], NT)
    left = dot32(inv_before, every[:k, k:], (((1,), (0,)), ((), ())))
    ritz[...] = dot32(left, inv_before, NT)


def shards(shots, basis, round_masks):
    n, feat = shots.shape
    k = basis.shape[1]
    nrep, nown = lax.axis_size("rep"), lax.axis_size("owner")
    half = n // 2
    bf, f32 = jnp.bfloat16, jnp.float32
    vmem = pl.BlockSpec(memory_space=pltpu.VMEM)
    slab = (2 * k) // (2 * NX)
    dma = pltpu.SemaphoreType.DMA
    grown, sums = pl.pallas_call(
        functools.partial(rounds_kernel, SHARPNESS / math.sqrt(feat)),
        out_shape=(jax.ShapeDtypeStruct((half, 2 * k), f32), jax.ShapeDtypeStruct((2 * k, 2 * k), f32)),
        in_specs=[pl.BlockSpec(memory_space=pltpu.SMEM), vmem, vmem],
        out_specs=(vmem, vmem),
        scratch_shapes=[
            pltpu.VMEM((n, feat), bf),
            pltpu.VMEM((NY, NX, n, feat), bf),
            pltpu.VMEM((NZ, n, feat), bf),
            pltpu.VMEM((ROUNDS, n, feat), bf),
            pltpu.VMEM((ROUNDS, n, feat), bf),
            pltpu.VMEM((ROUNDS, 2 * n, NZ * n), bf),
            pltpu.VMEM((ROUNDS, NZ, half, 2 * k), bf),
            pltpu.VMEM((NZ * n, 2 * k), bf),
            pltpu.VMEM((ROUNDS, n, 2 * k), f32),
            pltpu.VMEM((ROUNDS, n, 2 * k), f32),
            [pltpu.VMEM((NX, half, 2 * k), bf)] * ROUNDS,
            [pltpu.VMEM((NY, half, 2 * k), bf)] * ROUNDS,
            pltpu.VMEM((half, 2 * k), bf),
            pltpu.VMEM((half, 2 * k), f32),
            pltpu.VMEM((2, half, 2 * k), f32),
            pltpu.VMEM((half, 2 * k), f32),
            pltpu.VMEM((NX, half, 2 * k), f32),
            pltpu.VMEM((NY, half, 2 * k), f32),
            pltpu.VMEM((2 * NX, slab, 2 * k), f32),
            pltpu.VMEM((NY, slab, 2 * k), f32),
            pltpu.VMEM((NZ, slab, 2 * k), f32),
            pltpu.VMEM((2 * NX, slab, 2 * k), f32),
            pltpu.VMEM((2 * NX, slab, 2 * k), f32),
            dma((61,)), dma((61,)),
            dma((ROUNDS, NZ)), dma((ROUNDS, NZ)),
            dma((ROUNDS + 1, 8)), dma((ROUNDS + 1, 8)),
            dma((ROUNDS,)), dma((ROUNDS,)),
            dma((28,)), dma((28,)),
        ],
        compiler_params=pltpu.CompilerParams(
            collective_id=0, has_side_effects=True, vmem_limit_bytes=48 * 1024 * 1024
        ),
        name="rounds",
    )(round_masks, shots, basis.T)
    iterate_t, ritz = pl.pallas_call(
        functools.partial(finish_kernel, float(nown * nrep * n)),
        out_shape=(jax.ShapeDtypeStruct((k, n), f32), jax.ShapeDtypeStruct((k, k), f32)),
        in_specs=[vmem, vmem],
        out_specs=(vmem, vmem),
        name="finish",
    )(grown, sums)
    return iterate_t.T, ritz


def solution(mesh):
    in_specs = (P(("owner", "rep"), None), P(("owner", "rep"), None), P())
    out_specs = (P(("owner", "rep"), None), P())
    return jax.shard_map(shards, mesh=mesh, in_specs=in_specs, out_specs=out_specs, check_vma=False)
```

```python
import functools
import math

import jax
import jax.numpy as jnp
from jax import lax
from jax.experimental import pallas as pl
from jax.experimental.pallas import tpu as pltpu
from jax.sharding import PartitionSpec as P

ROUNDS = 3
SHARPNESS = 1.6
MESH = pl.DeviceIdType.MESH
NT = (((1,), (1,)), ((), ()))
TN = (((0,), (0,)), ((), ()))
NX, NY, NZ = 4, 4, 8


def dot32(a, b, dims):
    return lax.dot_general(a, b, dims, precision=lax.Precision.HIGHEST, preferred_element_type=jnp.float32)


def pack(rows):
    half = rows.shape[0] // 2
    return jnp.concatenate([rows[:half], rows[half:]], axis=1)


def rounds_kernel(
    scale, masks_hbm, shots_hbm, basis_hbm, out,
    masks, shots, basis_t, oth, own, cands, aff, gpart, gfull, wsend, wrecv, xbufs, ybufs, homeward, ghome, gsend, gback, gx, gy,
    rs, ys, zs, fin, prod,
    s_in, s1, r1, sg, rg, sc, rc, sw, rw, sa, ra,
):
    n, feat = shots.shape
    half, quarter = n // 2, n // 4
    k = basis_t.shape[0]
    o, r = lax.axis_index("owner"), lax.axis_index("rep")
    c, x, yh = o % 2, (o // 2) % NX, o // (2 * NX)
    z, yl = r // 2, r % 2
    y = yh * 2 + yl
    nq = 2 * NX
    q = x * 2 + c

    def dev(y=y, x=x, c=c, z=z):
        return (((y // 2) * NX + x) * 2 + c, z * 2 + y % 2)

    twin_y = yh * 2 + c
    twin = dev(y=twin_y, c=yl)
    other_core = dev(c=1 - c)
    moved = c != yl
    stays = c == yl

    loads = [
        pltpu.make_async_copy(shots_hbm, shots, s_in.at[0]),
        pltpu.make_async_copy(basis_hbm, basis_t, s_in.at[1]),
        pltpu.make_async_copy(masks_hbm, masks, s_in.at[2]),
    ]
    for copy in loads:
        copy.start()

    bar = pltpu.get_barrier_semaphore()

    def hello(device):
        pl.semaphore_signal(bar, inc=1, device_id=device, device_id_type=MESH)

    @pl.loop(1, NZ)
    def _(i):
        hello(dev(z=(z + i) % NZ))

    @pl.loop(1, NX)
    def _(i):
        for core in range(2):
            hello(dev(x=(x + i) % NX, c=core))
            hello(dev(y=(y + i) % NY, c=core))

    hello(other_core)

    for copy in loads:
        copy.wait()
    values = shots[...].astype(jnp.float32)
    inv = lax.rsqrt(jnp.mean(values * values, axis=-1, keepdims=True) + 1e-06)
    oth[y, x] = (values * inv).astype(jnp.bfloat16)
    g0 = pack(basis_t[...].T)

    @pl.when(stays)
    def _():
        own[z] = oth[y, x]
        ghome[...] = g0

    @pl.when(moved)
    def _():
        gsend[0] = g0

    pl.semaphore_wait(bar, (NZ - 1) + 2 * (NX - 1) + 2 * (NY - 1) + 1)

    def send(src, dst, ssem, rsem, device):
        return pltpu.make_async_remote_copy(
            src_ref=src, dst_ref=dst, send_sem=ssem, recv_sem=rsem, device_id=device, device_id_type=MESH
        )

    pending = []

    def all_sent(numbers):
        for number, rows in numbers:
            ref = oth.at[0, 0, pl.ds(0, rows)]
            send(ref, ref, s1.at[number], r1.at[number], other_core).wait_send()

    def move(src, dst, number, device):
        send(src, dst, s1.at[number], r1.at[number], device).start()
        pending.append((number, src.shape[0]))

    def same(ref, number, device):
        move(ref, ref, number, device)

    def landed(ref, number):
        send(ref, ref, s1.at[number], r1.at[number], other_core).wait_recv()

    halves = (pl.ds(0, half), pl.ds(half, half))
    quarters = tuple((pl.ds(i * half, quarter), pl.ds(i * half + quarter, quarter)) for i in range(2))

    RING, UP, DN, CORE, TRADE = 0, 40, 47, 54, 57

    trade = send(gsend.at[0], ghome, s1.at[TRADE + 2], r1.at[TRADE + 2], twin)

    def step(axis, i):
        return dev(x=(x + i) % NX) if axis == 0 else dev(y=(y + i) % NY)

    def at(axis, i, j):
        dx, dy = (i, j) if axis == 0 else (j, i)
        return (y + dy) % NY, (x + dx) % NX

    def ring(axis, h, j, first):
        return RING + 4 * ((5 * h) + (0 if first else 1 + j % 4))

    def begin(axis, h, j, first=False):
        number = ring(axis, h, j, first)
        ref = oth.at[(*at(axis, 0, j), halves[h])]
        same(ref, number, step(axis, 1))
        same(ref, number + 1, step(axis, -1 % 4))

    def onward(axis, h, j, first=False):
        number = ring(axis, h, j, first)
        landed(oth.at[(*at(axis, 3, j), halves[h])], number)
        same(oth.at[(*at(axis, 3, j), quarters[h][0])], number + 2, step(axis, 1))
        landed(oth.at[(*at(axis, 1, j), halves[h])], number + 1)
        same(oth.at[(*at(axis, 1, j), quarters[h][1])], number + 3, step(axis, 3))

    def last(axis, h, j, first=False):
        number = ring(axis, h, j, first)
        landed(oth.at[(*at(axis, 2, j), quarters[h][0])], number + 2)
        landed(oth.at[(*at(axis, 2, j), quarters[h][1])], number + 3)

    up, down = dev(z=(z + 1) % NZ), dev(z=(z + NZ - 1) % NZ)

    def z_begin(h):
        same(own.at[z, halves[h]], UP + h, up)
        same(own.at[z, halves[h]], DN + h, down)

    def z_on(s, h):
        a, b = (z + NZ - s) % NZ, (z + s) % NZ
        landed(own.at[a, halves[h]], UP + 2 * (s - 1) + h)
        if s < 3 or h == 0:
            same(own.at[a, halves[h]], UP + 2 * s + (h if s < 3 else 0), up)
        landed(own.at[b, halves[h]], DN + 2 * (s - 1) + h)
        if s < 3 or h == 1:
            same(own.at[b, halves[h]], DN + 2 * s + (h if s < 3 else 0), down)

    def z_last():
        a = (z + 4) % NZ
        landed(own.at[a, halves[0]], UP + 6)
        landed(own.at[a, halves[1]], DN + 6)

    def hand_over(h):
        src = oth.at[yh * 2 + 1 - yl, x, halves[h]]
        move(src, own.at[z, halves[h]], TRADE + h, other_core)

    @pl.when(stays)
    def _():
        z_begin(0)
        z_begin(1)
        begin(0, 0, 0, first=True)
        begin(1, 1, 0, first=True)
        begin(0, 1, 0)
        begin(1, 0, 0)
        onward(1, 1, 0, first=True)
        hand_over(1)
        begin(0, 1, 3)
        begin(0, 1, 1)
        onward(0, 0, 0, first=True)
        begin(1, 0, 3)
        begin(1, 0, 1)
        z_on(1, 0)
        onward(1, 0, 0)
        hand_over(0)
        onward(0, 1, 0)
        z_on(1, 1)
        last(0, 0, 0, first=True)
        begin(1, 0, 2)
        last(1, 1, 0, first=True)
        begin(0, 1, 2)
        z_on(2, 0)
        z_on(2, 1)
        onward(1, 0, 3)
        onward(0, 1, 3)
        last(1, 0, 0)
        last(0, 1, 0)
        z_on(3, 0)
        z_on(3, 1)
        onward(1, 0, 1)
        onward(0, 1, 1)

    sent_if_stays = tuple(pending)
    pending.clear()

    @pl.when(moved)
    def _():
        trade.start()
        begin(1, 1, 0, first=True)
        begin(1, 0, 0)
        begin(0, 0, 0, first=True)
        begin(0, 1, 0)
        onward(1, 1, 0, first=True)
        begin(0, 1, 3)
        begin(0, 1, 1)
        onward(0, 0, 0, first=True)
        begin(1, 0, 3)
        begin(1, 0, 1)
        landed(own.at[z, halves[1]], TRADE + 1)
        z_begin(1)
        onward(1, 0, 0)
        onward(0, 1, 0)
        last(0, 0, 0, first=True)
        begin(1, 0, 2)
        last(1, 1, 0, first=True)
        begin(0, 1, 2)
        landed(own.at[z, halves[0]], TRADE)
        z_begin(0)
        z_on(1, 1)
        onward(1, 0, 3)
        onward(0, 1, 3)
        z_on(1, 0)
        last(1, 0, 0)
        last(0, 1, 0)
        z_on(2, 1)
        z_on(2, 0)
        onward(1, 0, 1)
        onward(0, 1, 1)
        z_on(3, 1)
        z_on(3, 0)

    sent_if_moved = tuple(pending)
    pending.clear()

    @pl.when(moved)
    def _():
        trade.wait_recv()

    def g_send(t, value):
        gpart[t, z] = value.astype(jnp.bfloat16)

        for i in (3, 5, 4, 2, 6, 1, 7):
            send(gpart.at[t, z], gpart.at[t, z], sg.at[t, i], rg.at[t, i], dev(z=(z + i) % NZ)).start()

    grown = ghome[...]
    g_send(0, grown)

    onward(1, 0, 2)
    onward(0, 1, 2)
    last(1, 0, 3)
    last(0, 1, 3)
    last(1, 0, 1)
    last(0, 1, 1)
    last(1, 0, 2)
    last(0, 1, 2)

    def partner(t):
        m = masks[t]
        return y ^ ((m // 8) * 2 + m % 2), x ^ ((m // 2) % 4)

    for t in range(ROUNDS):
        m = masks[t]
        for a in range(2):
            cands[t][c, a] = oth[(yh ^ (m // 8)) * 2 + a, x ^ ((m // 2) % 4)]
        send(cands[t].at[c], cands[t].at[c], s1.at[CORE + t], r1.at[CORE + t], other_core).start()

    def affinities(t):
        landed(cands[t].at[1 - c], CORE + t)
        holder = yl ^ (masks[t] % 2)

        @pl.loop(0, NZ)
        def _(item):
            columns = pl.ds(pl.multiple_of(item * n, n), n)
            for a in range(2):
                scores = lax.dot_general(cands[t][holder, a], own[item], NT, preferred_element_type=jnp.float32)
                aff[t, a, :, columns] = jnp.exp(scores * scale).astype(jnp.bfloat16)

    z_last()
    affinities(0)

    lane = lax.broadcasted_iota(jnp.int32, (half, 2 * k), 1)
    tail = jnp.where(lane == k, 1.0, 0.0)

    def unpack(t, item):
        p = gpart[t, item].astype(jnp.float32)
        start = pl.multiple_of(item * n, n)
        gfull[pl.ds(start, half), :] = jnp.where(lane < k, p, tail).astype(jnp.bfloat16)
        gfull[pl.ds(start + half, half), :] = jnp.where(lane < k, pltpu.roll(p, k, 1), tail).astype(jnp.bfloat16)

    def near(j):
        return (NZ + (1 - 2 * ((j + 1) % 2)) * ((j + 1) // 2)) % NZ

    def carried(t):
        unpack(t, z)

        @pl.loop(1, NZ)
        def _(j):
            i = near(j)
            item = (z + NZ - i) % NZ
            ref = gpart.at[t, item]
            send(ref, ref, sg.at[t, i], rg.at[t, i], other_core).wait_recv()
            unpack(t, item)

        wsend[t] = jnp.dot(aff[t, 1 - c], gfull[...], preferred_element_type=jnp.float32)
        copy = send(wsend.at[t], wrecv.at[t], sw.at[t], rw.at[t], other_core)
        copy.start()
        mine = jnp.dot(aff[t, c], gfull[...], preferred_element_type=jnp.float32)
        copy.wait_recv()
        product = mine + wrecv[t]
        return pack(product[:, :k] / product[:, k:k + 1]).astype(jnp.bfloat16)

    def x_send(ref, sems, t, base):
        for i in (2, 1, 3):
            send(ref, ref, sems[0].at[t, base + i], sems[1].at[t, base + i], dev(x=(x + i) % NX)).start()

    def x_wait(buf, sems, t, base):
        for i in range(1, NX):
            ref = buf.at[(x + NX - i) % NX]
            send(ref, ref, sems[0].at[t, base + i], sems[1].at[t, base + i], other_core).wait_recv()

    def y_send(ref, sems, t, base):
        for i in (2, 1, 3):
            send(ref, ref, sems[0].at[t, base + i], sems[1].at[t, base + i], dev(y=(y + i) % NY)).start()

    def y_wait(buf, sems, t, base):
        for i in range(1, NY):
            ref = buf.at[(y + NY - i) % NY]
            send(ref, ref, sems[0].at[t, base + i], sems[1].at[t, base + i], other_core).wait_recv()

    csem = (sc, rc)
    for t in range(ROUNDS - 1):
        if t > 0:
            g_send(t, grown)
        py, px = partner(t)
        xbufs[t][x] = carried(t)
        x_send(xbufs[t].at[x], csem, t, 0)
        if t == 0:
            affinities(1)
        x_wait(xbufs[t], csem, t, 0)
        ybufs[t][y] = xbufs[t][px]
        y_send(ybufs[t].at[y], csem, t, 4)
        if t == 0:
            affinities(2)
        y_wait(ybufs[t], csem, t, 4)
        grown = grown + ybufs[t][py].astype(jnp.float32)

    t = ROUNDS - 1
    py, px = partner(t)
    g_send(t, grown)
    gx[x] = grown
    x_send(gx.at[x], csem, ROUNDS, 0)

    @pl.when(stays)
    def _():
        gback[...] = grown

    @pl.when(moved)
    def _():
        gsend[1] = grown
        send(gsend.at[1], gback, s1.at[TRADE + 3], r1.at[TRADE + 3], twin).start()

    x_wait(gx, csem, ROUNDS, 0)
    gy[y] = gx[px]
    y_send(gy.at[y], csem, ROUNDS, 4)
    came = carried(t)
    xbufs[t][x] = came
    x_send(xbufs[t].at[x], csem, t, 0)
    y_wait(gy, csem, ROUNDS, 4)
    before = gy[py]
    after = before + came.astype(jnp.float32)

    top = jnp.where(lane < k, before, pltpu.roll(after, k, 1))
    bottom = jnp.where(lane < k, pltpu.roll(before, k, 1), after)
    prod[...] = (dot32(top, top, TN) + dot32(bottom, bottom, TN)).reshape(prod.shape)

    def total(ref, count):
        value = ref[0]
        for i in range(1, count):
            value = value + ref[i]
        return value

    def q_dev(i):
        there = (q + i) % nq
        return dev(x=there // 2, c=there % 2)

    @pl.loop(1, nq)
    def _(i):
        send(prod.at[(q + i) % nq], rs.at[q], sa.at[i], ra.at[i], q_dev(i)).start()

    rs[q] = prod[q]

    x_wait(xbufs[t], csem, t, 0)
    homeward[...] = xbufs[t][px]

    @pl.when(stays)
    def _():
        ybufs[t][y] = homeward[...]

    def home_copy(i):
        ty = (y + i) % NY
        device = dev(y=(ty // 2) * 2 + c, c=ty % 2)
        return send(homeward, ybufs[t].at[y], sc.at[t, 4 + i], rc.at[t, 4 + i], device)

    @pl.when(moved)
    def _():
        home_copy(0).start()

    for i in range(1, NY):
        home_copy(i).start()

    @pl.loop(1, nq)
    def _(i):
        send(prod.at[0], rs.at[(q + nq - i) % nq], sa.at[i], ra.at[i], other_core).wait_recv()

    ys[y] = total(rs, nq)

    @pl.loop(1, NY)
    def _(i):
        send(ys.at[y], ys.at[y], sa.at[8 + i], ra.at[8 + i], dev(y=(y + i) % NY)).start()

    @pl.loop(1, NY)
    def _(i):
        ref = ys.at[(y + NY - i) % NY]
        send(ref, ref, sa.at[8 + i], ra.at[8 + i], other_core).wait_recv()

    zs[z] = total(ys, NY)

    for i in (3, 5, 4, 2, 6, 1, 7):
        send(zs.at[z], zs.at[z], sa.at[12 + i], ra.at[12 + i], dev(z=(z + i) % NZ)).start()

    @pl.loop(1, NZ)
    def _(i):
        ref = zs.at[(z + NZ - i) % NZ]
        send(ref, ref, sa.at[12 + i], ra.at[12 + i], other_core).wait_recv()

    fin[q] = total(zs, NZ)

    @pl.loop(1, nq)
    def _(i):
        send(fin.at[q], fin.at[q], sa.at[20 + i], ra.at[20 + i], q_dev(i)).start()

    @pl.when(moved)
    def _():
        send(gsend.at[1], gback, s1.at[TRADE + 3], r1.at[TRADE + 3], twin).wait_recv()
        ref = ybufs[t].at[twin_y]
        send(ref, ref, sc.at[t, 4], rc.at[t, 4], other_core).wait_recv()

    for i in range(1, NY):
        ref = ybufs[t].at[(twin_y + NY - i) % NY]
        send(ref, ref, sc.at[t, 4 + i], rc.at[t, 4 + i], other_core).wait_recv()
    m = masks[t]
    out[:half, :] = gback[...] + ybufs[t][twin_y ^ ((m // 8) * 2 + m % 2)].astype(jnp.float32)

    @pl.loop(1, nq)
    def _(i):
        ref = fin.at[(q + nq - i) % nq]
        send(ref, ref, sa.at[20 + i], ra.at[20 + i], other_core).wait_recv()

    out[half:, :] = fin[...].reshape(2 * k, 2 * k)

    all_sent(pending)
    for t in range(ROUNDS):
        ref = cands[t].at[c]
        send(ref, ref, s1.at[CORE + t], r1.at[CORE + t], other_core).wait_send()

    @pl.when(stays)
    def _():
        all_sent(sent_if_stays)

    @pl.when(moved)
    def _():
        all_sent(sent_if_moved)
        trade.wait_send()
        send(gsend.at[1], gback, s1.at[TRADE + 3], r1.at[TRADE + 3], twin).wait_send()
        home_copy(0).wait_send()

    @pl.loop(1, NX)
    def _(i):
        for row in range(ROUNDS):
            ref = xbufs[row].at[x]
            send(ref, ref, sc.at[row, i], rc.at[row, i], other_core).wait_send()
            send(ref, ref, sc.at[row, 4 + i], rc.at[row, 4 + i], other_core).wait_send()
        ref = gx.at[x]
        send(ref, ref, sc.at[ROUNDS, i], rc.at[ROUNDS, i], other_core).wait_send()
        send(ref, ref, sc.at[ROUNDS, 4 + i], rc.at[ROUNDS, 4 + i], other_core).wait_send()
        send(ys.at[y], ys.at[y], sa.at[8 + i], ra.at[8 + i], other_core).wait_send()

    @pl.loop(1, NZ)
    def _(i):
        for row in range(ROUNDS):
            ref = gpart.at[row, z]
            send(ref, ref, sg.at[row, i], rg.at[row, i], other_core).wait_send()
        for base in (0, 12, 20):
            send(fin.at[q], fin.at[q], sa.at[base + i], ra.at[base + i], other_core).wait_send()

    for row in range(ROUNDS):
        send(wsend.at[row], wrecv.at[row], sw.at[row], rw.at[row], other_core).wait_send()


def inverse_factors(grams, outs):
    k = grams[0].shape[0]
    row = lax.broadcasted_iota(jnp.int32, (k, k), 0)
    lane = lax.broadcasted_iota(jnp.int32, (k, k), 1)
    identity = jnp.where(lane == row, 1.0, 0.0)
    for gram, out in zip(grams, outs):
        whole = jnp.concatenate([gram, identity], axis=1)
        work = [whole[8 * g:8 * g + 8] for g in range(k // 8)]
        for i in range(0, k, 4):
            block = work[i // 8]
            s = i % 8
            rows = [block[s + p:s + p + 1, :] for p in range(4)]
            u = {(p, j): block[s + p:s + p + 1, i + j:i + j + 1] for p in range(4) for j in range(p, 4)}
            inv = []
            for p in range(4):
                inv.append(1.0 / u[p, p])
                for j in range(p + 1, 4):
                    factor = u[p, j] * inv[p]
                    rows[j] = rows[j] - factor * rows[p]
                    for l in range(j, 4):
                        u[j, l] = u[j, l] - factor * u[p, l]
            for p in range(4):
                out[i + p:i + p + 1, :] = rows[p] * (1.0 / jnp.sqrt(u[p, p]))
            solved = [None] * 4
            for p in reversed(range(4)):
                value = rows[p]
                for j in range(p + 1, 4):
                    value = value - u[p, j] * solved[j]
                solved[p] = value * inv[p]
            for g in range((i + 4) // 8, k // 8):
                rest = work[g]
                for j in range(4):
                    rest = rest - work[g][:, i + j:i + j + 1] * solved[j]
                work[g] = rest


def finish_kernel(total_rows, both, iterate_t, ritz, work_a, work_b):
    k = ritz.shape[0]
    half = both.shape[0] - 2 * k
    every = both[half:, :] * (1.0 / total_rows)
    inverse_factors([every[:k, :k], every[k:, k:]], [work_a, work_b])
    inv_before, inv_last = work_a[:, k:], work_b[:, k:]
    packed = both[:half, :]
    iterate_t[:, :half] = dot32(inv_last, packed[:, :k], NT)
    iterate_t[:, half:] = dot32(inv_last, packed[:, k:], NT)
    left = dot32(inv_before, every[:k, k:], (((1,), (0,)), ((), ())))
    ritz[...] = dot32(left, inv_before, NT)


def shards(shots, basis, round_masks):
    n, feat = shots.shape
    k = basis.shape[1]
    nrep, nown = lax.axis_size("rep"), lax.axis_size("owner")
    half = n // 2
    bf, f32 = jnp.bfloat16, jnp.float32
    vmem = pl.BlockSpec(memory_space=pltpu.VMEM)
    slab = (2 * k) // (2 * NX)
    dma = pltpu.SemaphoreType.DMA
    both = pl.pallas_call(
        functools.partial(rounds_kernel, SHARPNESS / math.sqrt(feat)),
        out_shape=jax.ShapeDtypeStruct((half + 2 * k, 2 * k), f32),
        in_specs=[pl.BlockSpec(memory_space=pltpu.HBM)] * 3,
        out_specs=vmem,
        scratch_shapes=[
            pltpu.SMEM((ROUNDS,), jnp.int32),
            pltpu.VMEM((n, feat), bf),
            pltpu.VMEM((k, n), f32),
            pltpu.VMEM((NY, NX, n, feat), bf),
            pltpu.VMEM((NZ, n, feat), bf),
            [pltpu.VMEM((2, 2, n, feat), bf)] * ROUNDS,
            pltpu.VMEM((ROUNDS, 2, n, NZ * n), bf),
            pltpu.VMEM((ROUNDS, NZ, half, 2 * k), bf),
            pltpu.VMEM((NZ * n, 2 * k), bf),
            pltpu.VMEM((ROUNDS, n, 2 * k), f32),
            pltpu.VMEM((ROUNDS, n, 2 * k), f32),
            [pltpu.VMEM((NX, half, 2 * k), bf)] * ROUNDS,
            [pltpu.VMEM((NY, half, 2 * k), bf)] * ROUNDS,
            pltpu.VMEM((half, 2 * k), bf),
            pltpu.VMEM((half, 2 * k), f32),
            pltpu.VMEM((2, half, 2 * k), f32),
            pltpu.VMEM((half, 2 * k), f32),
            pltpu.VMEM((NX, half, 2 * k), f32),
            pltpu.VMEM((NY, half, 2 * k), f32),
            pltpu.VMEM((2 * NX, slab, 2 * k), f32),
            pltpu.VMEM((NY, slab, 2 * k), f32),
            pltpu.VMEM((NZ, slab, 2 * k), f32),
            pltpu.VMEM((2 * NX, slab, 2 * k), f32),
            pltpu.VMEM((2 * NX, slab, 2 * k), f32),
            dma((3,)),
            dma((61,)), dma((61,)),
            dma((ROUNDS, NZ)), dma((ROUNDS, NZ)),
            dma((ROUNDS + 1, 8)), dma((ROUNDS + 1, 8)),
            dma((ROUNDS,)), dma((ROUNDS,)),
            dma((28,)), dma((28,)),
        ],
        compiler_params=pltpu.CompilerParams(
            collective_id=0, has_side_effects=True, vmem_limit_bytes=60 * 1024 * 1024
        ),
        name="rounds",
    )(round_masks, shots, basis.T)
    iterate_t, ritz = pl.pallas_call(
        functools.partial(finish_kernel, float(nown * nrep * n)),
        out_shape=(jax.ShapeDtypeStruct((k, n), f32), jax.ShapeDtypeStruct((k, k), f32)),
        in_specs=[vmem],
        out_specs=(vmem, vmem),
        scratch_shapes=[pltpu.VMEM((k, 2 * k), f32)] * 2,
        name="finish",
    )(both)
    return iterate_t.T, ritz


def solution(mesh):
    in_specs = (P(("owner", "rep"), None), P(("owner", "rep"), None), P())
    out_specs = (P(("owner", "rep"), None), P())
    return jax.shard_map(shards, mesh=mesh, in_specs=in_specs, out_specs=out_specs, check_vma=False)
```

```python
import functools
import math

import jax
import jax.numpy as jnp
from jax import lax
from jax.experimental import pallas as pl
from jax.experimental.pallas import tpu as pltpu
from jax.sharding import PartitionSpec as P

ROUNDS = 3
SHARPNESS = 1.6
MESH = pl.DeviceIdType.MESH
NT = (((1,), (1,)), ((), ()))
TN = (((0,), (0,)), ((), ()))
NX, NY, NZ = 4, 4, 8

ORDER_STAYS = (
    ("G", 1, 0, 1), ("Y",), ("G", 1, 0, -1), ("F", 0, 0, 0, 1, 3), ("F", 0, 0, 0, 1, 1), ("F", 1, 1, 0, 1, 3),
    ("F", 1, 1, 0, 1, 1), ("Z", 1, 0, 1), ("Z", 1, 0, -1), ("F", 0, 1, 0, 0, 3), ("F", 0, 1, 0, 0, 1),
    ("F", 1, 0, 0, 0, 3), ("F", 1, 0, 0, 0, 1), ("Z", 1, 1, 1), ("Z", 1, 1, -1), ("G", 2, 0, 1), ("G", 2, 0, -1),
    ("Z", 2, 0, 1), ("Z", 2, 0, -1), ("Q", 0, 0, 0, 1, 0), ("Q", 0, 0, 0, 1, 1), ("F", 0, 1, 3, 0, 3),
    ("F", 0, 1, 3, 0, 1), ("Z", 2, 1, 1), ("Z", 2, 1, -1), ("G", 3, 0, 1), ("G", 3, 0, -1), ("F", 0, 1, 1, 0, 3),
    ("F", 0, 1, 1, 0, 1), ("Q", 0, 1, 0, 0, 0), ("Q", 0, 1, 0, 0, 1), ("Z", 3, 0, 1), ("F", 1, 0, 3, 0, 3),
    ("F", 1, 0, 3, 0, 1), ("Z", 3, 0, -1), ("F", 1, 0, 1, 0, 3), ("F", 1, 0, 1, 0, 1), ("Q", 1, 1, 0, 1, 0),
    ("Q", 1, 1, 0, 1, 1), ("Z", 3, 1, 1), ("Q", 1, 0, 0, 0, 0), ("Q", 1, 0, 0, 0, 1), ("Z", 3, 1, -1), ("G", 4, 0, 1),
    ("Q", 0, 1, 3, 0, 0), ("Q", 0, 1, 3, 0, 1), ("Q", 0, 1, 1, 0, 0), ("Q", 0, 1, 1, 0, 1), ("Q", 1, 0, 3, 0, 0),
    ("Q", 1, 0, 3, 0, 1), ("Q", 1, 0, 1, 0, 0), ("Q", 1, 0, 1, 0, 1), ("Z", 4, 0, 1), ("F", 1, 0, 2, 0, 3),
    ("F", 1, 0, 2, 0, 1), ("Z", 4, 1, -1), ("F", 0, 1, 2, 0, 3), ("F", 0, 1, 2, 0, 1), ("Q", 1, 0, 2, 0, 0),
    ("Q", 1, 0, 2, 0, 1), ("Q", 0, 1, 2, 0, 0), ("Q", 0, 1, 2, 0, 1),
)
ORDER_MOVED = (
    ("O", 1), ("T",), ("O", 0), ("F", 0, 0, 0, 1, 3), ("F", 0, 0, 0, 1, 1), ("F", 1, 1, 0, 1, 3),
    ("F", 1, 1, 0, 1, 1), ("F", 0, 1, 0, 0, 3), ("F", 0, 1, 0, 0, 1), ("F", 1, 0, 0, 0, 3), ("F", 1, 0, 0, 0, 1),
    ("Z", 1, 1, 1), ("Z", 1, 1, -1), ("F", 1, 0, 3, 0, 3), ("F", 1, 0, 3, 0, 1), ("G", 1, 0, 1), ("G", 1, 0, -1),
    ("F", 1, 0, 1, 0, 3), ("F", 1, 0, 1, 0, 1), ("Q", 1, 1, 0, 1, 0), ("Q", 1, 1, 0, 1, 1), ("Z", 1, 0, 1),
    ("Q", 1, 0, 0, 0, 0), ("Q", 1, 0, 0, 0, 1), ("Z", 1, 0, -1), ("Q", 0, 0, 0, 1, 0), ("Q", 0, 0, 0, 1, 1),
    ("F", 0, 1, 3, 0, 3), ("F", 0, 1, 3, 0, 1), ("Z", 2, 1, 1), ("Z", 2, 1, -1), ("F", 0, 1, 1, 0, 3),
    ("F", 0, 1, 1, 0, 1), ("Q", 0, 1, 0, 0, 0), ("Q", 0, 1, 0, 0, 1), ("G", 2, 0, 1), ("G", 2, 0, -1),
    ("F", 1, 0, 2, 0, 3), ("F", 1, 0, 2, 0, 1), ("Z", 2, 0, -1), ("Z", 2, 0, 1), ("F", 0, 1, 2, 0, 3),
    ("F", 0, 1, 2, 0, 1), ("Z", 3, 1, -1), ("Q", 0, 1, 3, 0, 0), ("Q", 0, 1, 3, 0, 1), ("Q", 0, 1, 1, 0, 0),
    ("Q", 0, 1, 1, 0, 1), ("Z", 3, 1, 1), ("G", 3, 0, -1), ("G", 3, 0, 1), ("Q", 1, 0, 3, 0, 0), ("Q", 1, 0, 3, 0, 1),
    ("Q", 1, 0, 1, 0, 0), ("Q", 1, 0, 1, 0, 1), ("Q", 0, 1, 2, 0, 0), ("Q", 0, 1, 2, 0, 1), ("Z", 3, 0, -1),
    ("Z", 3, 0, 1), ("G", 4, 0, 1), ("Q", 1, 0, 2, 0, 0), ("Q", 1, 0, 2, 0, 1), ("Z", 4, 1, -1), ("Z", 4, 0, 1),
)


def dot32(a, b, dims):
    return lax.dot_general(a, b, dims, precision=lax.Precision.HIGHEST, preferred_element_type=jnp.float32)


def pack(rows):
    half = rows.shape[0] // 2
    return jnp.concatenate([rows[:half], rows[half:]], axis=1)


def rounds_kernel(
    scale, masks_hbm, shots_hbm, basis_hbm, out,
    masks, shots, basis_t, oth, own, cands, aff, gpart, gfull, wsend, wrecv, xbufs, ybufs, homeward, ghome, gsend, gback, gx, gy,
    rs, ys, zs, fin, prod,
    s_in, s1, r1, sg, rg, sc, rc, sw, rw, sa, ra,
):
    n, feat = shots.shape
    half, quarter = n // 2, n // 4
    k = basis_t.shape[0]
    o, r = lax.axis_index("owner"), lax.axis_index("rep")
    c, x, yh = o % 2, (o // 2) % NX, o // (2 * NX)
    z, yl = r // 2, r % 2
    y = yh * 2 + yl
    nq = 2 * NX
    q = x * 2 + c

    def dev(y=y, x=x, c=c, z=z):
        return (((y // 2) * NX + x) * 2 + c, z * 2 + y % 2)

    twin_y = yh * 2 + c
    twin = dev(y=twin_y, c=yl)
    other_core = dev(c=1 - c)
    moved = c != yl
    stays = c == yl

    loads = [
        pltpu.make_async_copy(shots_hbm, shots, s_in.at[0]),
        pltpu.make_async_copy(basis_hbm, basis_t, s_in.at[1]),
        pltpu.make_async_copy(masks_hbm, masks, s_in.at[2]),
    ]
    for copy in loads:
        copy.start()

    bar = pltpu.get_barrier_semaphore()

    def hello(device):
        pl.semaphore_signal(bar, inc=1, device_id=device, device_id_type=MESH)

    @pl.loop(1, NZ)
    def _(i):
        hello(dev(z=(z + i) % NZ))

    @pl.loop(1, NX)
    def _(i):
        for core in range(2):
            hello(dev(x=(x + i) % NX, c=core))
            hello(dev(y=(y + i) % NY, c=core))

    hello(other_core)

    for copy in loads:
        copy.wait()
    values = shots[...].astype(jnp.float32)
    inv = lax.rsqrt(jnp.mean(values * values, axis=-1, keepdims=True) + 1e-06)
    oth[y, x] = (values * inv).astype(jnp.bfloat16)
    g0 = pack(basis_t[...].T)

    @pl.when(stays)
    def _():
        own[z] = oth[y, x]
        ghome[...] = g0

    @pl.when(moved)
    def _():
        gsend[0] = g0

    pl.semaphore_wait(bar, (NZ - 1) + 2 * (NX - 1) + 2 * (NY - 1) + 1)

    def send(src, dst, ssem, rsem, device):
        return pltpu.make_async_remote_copy(
            src_ref=src, dst_ref=dst, send_sem=ssem, recv_sem=rsem, device_id=device, device_id_type=MESH
        )

    pending = []

    def all_sent(numbers):
        for number, rows in numbers:
            ref = oth.at[0, 0, pl.ds(0, rows)]
            send(ref, ref, s1.at[number], r1.at[number], other_core).wait_send()

    def move(src, dst, number, device):
        send(src, dst, s1.at[number], r1.at[number], device).start()
        pending.append((number, src.shape[0]))

    def same(ref, number, device):
        move(ref, ref, number, device)

    def landed(ref, number):
        send(ref, ref, s1.at[number], r1.at[number], other_core).wait_recv()

    halves = (pl.ds(0, half), pl.ds(half, half))
    quarters = tuple((pl.ds(i * half, quarter), pl.ds(i * half + quarter, quarter)) for i in range(2))

    RING, UP, DN, CORE, TRADE = 0, 40, 47, 54, 57

    trade = send(gsend.at[0], ghome, s1.at[TRADE + 2], r1.at[TRADE + 2], twin)

    def step(axis, i):
        return dev(x=(x + i) % NX) if axis == 0 else dev(y=(y + i) % NY)

    def at(axis, i, j):
        dx, dy = (i, j) if axis == 0 else (j, i)
        return (y + dy) % NY, (x + dx) % NX

    def ring(axis, h, j, first):
        return RING + 4 * ((5 * h) + (0 if first else 1 + j % 4))

    def begin(axis, h, j, first=False):
        number = ring(axis, h, j, first)
        ref = oth.at[(*at(axis, 0, j), halves[h])]
        same(ref, number, step(axis, 1))
        same(ref, number + 1, step(axis, -1 % 4))

    def on_full(axis, h, j, first, k):
        number = ring(axis, h, j, first)
        part = 0 if k == 3 else 1
        landed(oth.at[(*at(axis, k, j), halves[h])], number + part)
        same(oth.at[(*at(axis, k, j), quarters[h][part])], number + 2 + part, step(axis, 4 - k))
        if first:
            begin(1 - axis, h, k)

    def on_quarter(axis, h, j, first, part):
        landed(oth.at[(*at(axis, 2, j), quarters[h][part])], ring(axis, h, j, first) + 2 + part)

    up, down = dev(z=(z + 1) % NZ), dev(z=(z + NZ - 1) % NZ)

    def z_begin(h):
        same(own.at[z, halves[h]], UP + h, up)
        same(own.at[z, halves[h]], DN + h, down)

    def on_z(s, h, direction):
        ref = own.at[(z + NZ - direction * s) % NZ, halves[h]]
        base = UP if direction == 1 else DN
        landed(ref, base + (2 * (s - 1) + h if s < 4 else 6))
        if s < 3 or (s == 3 and (h == 0) == (direction == 1)):
            same(ref, base + (2 * s + h if s < 3 else 6), up if direction == 1 else down)

    def g_begin():
        gpart[0, z] = ghome[...].astype(jnp.bfloat16)
        for i, device in ((1, up), (7, down)):
            send(gpart.at[0, z], gpart.at[0, z], sg.at[0, i], rg.at[0, i], device).start()

    def on_g(s, direction):
        ref = gpart.at[0, (z + NZ - direction * s) % NZ]
        i = s if direction == 1 else NZ - s
        send(ref, ref, sg.at[0, i], rg.at[0, i], other_core).wait_recv()
        if s < 3 or (s == 3 and direction == 1):
            send(ref, ref, sg.at[0, i + direction], rg.at[0, i + direction], up if direction == 1 else down).start()

    def hand_over(h):
        src = oth.at[yh * 2 + 1 - yl, x, halves[h]]
        move(src, own.at[z, halves[h]], TRADE + h, other_core)

    def gather(order):
        seen = set()
        for kind, *args in order:
            seen.add((kind, *args))
            if kind == "F":
                on_full(*args)
                axis, h, j, first, k = args
                if order is ORDER_STAYS and axis == 1 and j == 0 and ("F", axis, h, j, first, 4 - k) in seen:
                    hand_over(h)
            elif kind == "Q":
                on_quarter(*args)
                axis, h, j, first, part = args
                if first and ("Q", axis, h, j, first, 1 - part) in seen:
                    begin(1 - axis, h, 2)
            elif kind == "Z":
                on_z(*args)
            elif kind == "G":
                on_g(args[0], args[2])
            elif kind == "O":
                landed(own.at[z, halves[args[0]]], TRADE + args[0])
                z_begin(args[0])
            elif kind == "T":
                trade.wait_recv()
                g_begin()
            else:
                begin(1, 1, 0, first=True)
                begin(1, 0, 0)

    @pl.when(stays)
    def _():
        g_begin()
        z_begin(0)
        z_begin(1)
        begin(0, 0, 0, first=True)
        begin(0, 1, 0)
        gather(ORDER_STAYS)

    sent_if_stays = tuple(pending)
    pending.clear()

    @pl.when(moved)
    def _():
        begin(1, 1, 0, first=True)
        begin(1, 0, 0)
        trade.start()
        begin(0, 0, 0, first=True)
        begin(0, 1, 0)
        gather(ORDER_MOVED)

    sent_if_moved = tuple(pending)
    pending.clear()

    def g_send(t, value):
        gpart[t, z] = value.astype(jnp.bfloat16)

        for i in (3, 5, 4, 2, 6, 1, 7):
            send(gpart.at[t, z], gpart.at[t, z], sg.at[t, i], rg.at[t, i], dev(z=(z + i) % NZ)).start()

    grown = ghome[...]

    def partner(t):
        m = masks[t]
        return y ^ ((m // 8) * 2 + m % 2), x ^ ((m // 2) % 4)

    for t in range(ROUNDS):
        m = masks[t]
        for a in range(2):
            cands[t][c, a] = oth[(yh ^ (m // 8)) * 2 + a, x ^ ((m // 2) % 4)]
        send(cands[t].at[c], cands[t].at[c], s1.at[CORE + t], r1.at[CORE + t], other_core).start()

    def affinities(t):
        landed(cands[t].at[1 - c], CORE + t)
        holder = yl ^ (masks[t] % 2)

        @pl.loop(0, NZ)
        def _(item):
            columns = pl.ds(pl.multiple_of(item * n, n), n)
            for a in range(2):
                scores = lax.dot_general(cands[t][holder, a], own[item], NT, preferred_element_type=jnp.float32)
                aff[t, a, :, columns] = jnp.exp(scores * scale).astype(jnp.bfloat16)

    affinities(0)

    lane = lax.broadcasted_iota(jnp.int32, (half, 2 * k), 1)
    tail = jnp.where(lane == k, 1.0, 0.0)

    def unpack(t, item):
        p = gpart[t, item].astype(jnp.float32)
        start = pl.multiple_of(item * n, n)
        gfull[pl.ds(start, half), :] = jnp.where(lane < k, p, tail).astype(jnp.bfloat16)
        gfull[pl.ds(start + half, half), :] = jnp.where(lane < k, pltpu.roll(p, k, 1), tail).astype(jnp.bfloat16)

    def near(j):
        return (NZ + (1 - 2 * ((j + 1) % 2)) * ((j + 1) // 2)) % NZ

    def carried(t):
        unpack(t, z)

        @pl.loop(1, NZ)
        def _(j):
            i = near(j)
            item = (z + NZ - i) % NZ
            if t > 0:
                ref = gpart.at[t, item]
                send(ref, ref, sg.at[t, i], rg.at[t, i], other_core).wait_recv()
            unpack(t, item)

        wsend[t] = jnp.dot(aff[t, 1 - c], gfull[...], preferred_element_type=jnp.float32)
        copy = send(wsend.at[t], wrecv.at[t], sw.at[t], rw.at[t], other_core)
        copy.start()
        mine = jnp.dot(aff[t, c], gfull[...], preferred_element_type=jnp.float32)
        copy.wait_recv()
        product = mine + wrecv[t]
        return pack(product[:, :k] / product[:, k:k + 1]).astype(jnp.bfloat16)

    def x_send(ref, sems, t, base):
        for i in (2, 1, 3):
            send(ref, ref, sems[0].at[t, base + i], sems[1].at[t, base + i], dev(x=(x + i) % NX)).start()

    def x_wait(buf, sems, t, base):
        for i in range(1, NX):
            ref = buf.at[(x + NX - i) % NX]
            send(ref, ref, sems[0].at[t, base + i], sems[1].at[t, base + i], other_core).wait_recv()

    def y_send(ref, sems, t, base):
        for i in (2, 1, 3):
            send(ref, ref, sems[0].at[t, base + i], sems[1].at[t, base + i], dev(y=(y + i) % NY)).start()

    def y_wait(buf, sems, t, base):
        for i in range(1, NY):
            ref = buf.at[(y + NY - i) % NY]
            send(ref, ref, sems[0].at[t, base + i], sems[1].at[t, base + i], other_core).wait_recv()

    csem = (sc, rc)
    for t in range(ROUNDS - 1):
        if t > 0:
            g_send(t, grown)
        py, px = partner(t)
        xbufs[t][x] = carried(t)
        x_send(xbufs[t].at[x], csem, t, 0)
        if t == 0:
            affinities(1)
        x_wait(xbufs[t], csem, t, 0)
        ybufs[t][y] = xbufs[t][px]
        y_send(ybufs[t].at[y], csem, t, 4)
        if t == 0:
            affinities(2)
        y_wait(ybufs[t], csem, t, 4)
        grown = grown + ybufs[t][py].astype(jnp.float32)

    t = ROUNDS - 1
    py, px = partner(t)
    g_send(t, grown)
    gx[x] = grown
    x_send(gx.at[x], csem, ROUNDS, 0)

    @pl.when(stays)
    def _():
        gback[...] = grown

    @pl.when(moved)
    def _():
        gsend[1] = grown
        send(gsend.at[1], gback, s1.at[TRADE + 3], r1.at[TRADE + 3], twin).start()

    x_wait(gx, csem, ROUNDS, 0)
    gy[y] = gx[px]
    y_send(gy.at[y], csem, ROUNDS, 4)
    came = carried(t)
    xbufs[t][x] = came
    x_send(xbufs[t].at[x], csem, t, 0)
    y_wait(gy, csem, ROUNDS, 4)
    before = gy[py]
    after = before + came.astype(jnp.float32)

    top = jnp.where(lane < k, before, pltpu.roll(after, k, 1))
    bottom = jnp.where(lane < k, pltpu.roll(before, k, 1), after)
    prod[...] = (dot32(top, top, TN) + dot32(bottom, bottom, TN)).reshape(prod.shape)

    def total(ref, count):
        value = ref[0]
        for i in range(1, count):
            value = value + ref[i]
        return value

    def q_dev(i):
        there = (q + i) % nq
        return dev(x=there // 2, c=there % 2)

    @pl.loop(1, nq)
    def _(i):
        send(prod.at[(q + i) % nq], rs.at[q], sa.at[i], ra.at[i], q_dev(i)).start()

    rs[q] = prod[q]

    x_wait(xbufs[t], csem, t, 0)
    homeward[...] = xbufs[t][px]

    @pl.when(stays)
    def _():
        ybufs[t][y] = homeward[...]

    def home_copy(i):
        ty = (y + i) % NY
        device = dev(y=(ty // 2) * 2 + c, c=ty % 2)
        return send(homeward, ybufs[t].at[y], sc.at[t, 4 + i], rc.at[t, 4 + i], device)

    @pl.when(moved)
    def _():
        home_copy(0).start()

    for i in range(1, NY):
        home_copy(i).start()

    @pl.loop(1, nq)
    def _(i):
        send(prod.at[0], rs.at[(q + nq - i) % nq], sa.at[i], ra.at[i], other_core).wait_recv()

    ys[y] = total(rs, nq)

    @pl.loop(1, NY)
    def _(i):
        send(ys.at[y], ys.at[y], sa.at[8 + i], ra.at[8 + i], dev(y=(y + i) % NY)).start()

    @pl.loop(1, NY)
    def _(i):
        ref = ys.at[(y + NY - i) % NY]
        send(ref, ref, sa.at[8 + i], ra.at[8 + i], other_core).wait_recv()

    zs[z] = total(ys, NY)

    for i in (3, 5, 4, 2, 6, 1, 7):
        send(zs.at[z], zs.at[z], sa.at[12 + i], ra.at[12 + i], dev(z=(z + i) % NZ)).start()

    @pl.loop(1, NZ)
    def _(i):
        ref = zs.at[(z + NZ - i) % NZ]
        send(ref, ref, sa.at[12 + i], ra.at[12 + i], other_core).wait_recv()

    fin[q] = total(zs, NZ)

    @pl.loop(1, nq)
    def _(i):
        send(fin.at[q], fin.at[q], sa.at[20 + i], ra.at[20 + i], q_dev(i)).start()

    @pl.when(moved)
    def _():
        send(gsend.at[1], gback, s1.at[TRADE + 3], r1.at[TRADE + 3], twin).wait_recv()
        ref = ybufs[t].at[twin_y]
        send(ref, ref, sc.at[t, 4], rc.at[t, 4], other_core).wait_recv()

    for i in range(1, NY):
        ref = ybufs[t].at[(twin_y + NY - i) % NY]
        send(ref, ref, sc.at[t, 4 + i], rc.at[t, 4 + i], other_core).wait_recv()
    m = masks[t]
    out[:half, :] = gback[...] + ybufs[t][twin_y ^ ((m // 8) * 2 + m % 2)].astype(jnp.float32)

    @pl.loop(1, nq)
    def _(i):
        ref = fin.at[(q + nq - i) % nq]
        send(ref, ref, sa.at[20 + i], ra.at[20 + i], other_core).wait_recv()

    out[half:, :] = fin[...].reshape(2 * k, 2 * k)

    all_sent(pending)
    for t in range(ROUNDS):
        ref = cands[t].at[c]
        send(ref, ref, s1.at[CORE + t], r1.at[CORE + t], other_core).wait_send()

    @pl.when(stays)
    def _():
        all_sent(sent_if_stays)

    @pl.when(moved)
    def _():
        all_sent(sent_if_moved)
        trade.wait_send()
        send(gsend.at[1], gback, s1.at[TRADE + 3], r1.at[TRADE + 3], twin).wait_send()
        home_copy(0).wait_send()

    @pl.loop(1, NX)
    def _(i):
        for row in range(ROUNDS):
            ref = xbufs[row].at[x]
            send(ref, ref, sc.at[row, i], rc.at[row, i], other_core).wait_send()
            send(ref, ref, sc.at[row, 4 + i], rc.at[row, 4 + i], other_core).wait_send()
        ref = gx.at[x]
        send(ref, ref, sc.at[ROUNDS, i], rc.at[ROUNDS, i], other_core).wait_send()
        send(ref, ref, sc.at[ROUNDS, 4 + i], rc.at[ROUNDS, 4 + i], other_core).wait_send()
        send(ys.at[y], ys.at[y], sa.at[8 + i], ra.at[8 + i], other_core).wait_send()

    @pl.loop(1, NZ)
    def _(i):
        for row in range(ROUNDS):
            ref = gpart.at[row, z]
            send(ref, ref, sg.at[row, i], rg.at[row, i], other_core).wait_send()
        for base in (0, 12, 20):
            send(fin.at[q], fin.at[q], sa.at[base + i], ra.at[base + i], other_core).wait_send()

    for row in range(ROUNDS):
        send(wsend.at[row], wrecv.at[row], sw.at[row], rw.at[row], other_core).wait_send()


def inverse_factors(grams):
    k = grams[0].shape[0]
    row = lax.broadcasted_iota(jnp.int32, (k, 2 * k), 0)
    lane = lax.broadcasted_iota(jnp.int32, (k, 2 * k), 1)
    identity = jnp.where(lane == row, 1.0, 0.0)[:, :k]
    works = [jnp.concatenate([gram, identity], axis=1) for gram in grams]
    works = [[work[8 * g:8 * g + 8] for g in range(k // 8)] for work in works]
    below = lax.broadcasted_iota(jnp.int32, (8, 1), 0)
    for i in range(k - 1):
        own, s = i // 8, i % 8
        for work in works:
            pivot = work[own][s:s + 1, :] * (1.0 / work[own][s:s + 1, i:i + 1])
            for g in range(own, k // 8):
                factor = work[g][:, i:i + 1]
                if g == own:
                    factor = jnp.where(below > s, factor, 0.0)
                work[g] = work[g] - factor * pivot
    results = []
    for work in works:
        whole = jnp.concatenate(work, axis=0)
        diagonal = jnp.sum(jnp.where(lane == row, whole, 0.0), axis=1, keepdims=True)
        results.append(whole[:, k:] * (1.0 / jnp.sqrt(diagonal)))
    return results


def finish_kernel(total_rows, both, iterate_t, ritz):
    k = ritz.shape[0]
    half = both.shape[0] - 2 * k
    every = both[half:, :] * (1.0 / total_rows)
    inv_before, inv_last = inverse_factors([every[:k, :k], every[k:, k:]])
    packed = both[:half, :]
    iterate_t[:, :half] = dot32(inv_last, packed[:, :k], NT)
    iterate_t[:, half:] = dot32(inv_last, packed[:, k:], NT)
    left = dot32(inv_before, every[:k, k:], (((1,), (0,)), ((), ())))
    ritz[...] = dot32(left, inv_before, NT)


def shards(shots, basis, round_masks):
    n, feat = shots.shape
    k = basis.shape[1]
    nrep, nown = lax.axis_size("rep"), lax.axis_size("owner")
    half = n // 2
    bf, f32 = jnp.bfloat16, jnp.float32
    vmem = pl.BlockSpec(memory_space=pltpu.VMEM)
    slab = (2 * k) // (2 * NX)
    dma = pltpu.SemaphoreType.DMA
    both = pl.pallas_call(
        functools.partial(rounds_kernel, SHARPNESS / math.sqrt(feat)),
        out_shape=jax.ShapeDtypeStruct((half + 2 * k, 2 * k), f32),
        in_specs=[pl.BlockSpec(memory_space=pltpu.HBM)] * 3,
        out_specs=vmem,
        scratch_shapes=[
            pltpu.SMEM((ROUNDS,), jnp.int32),
            pltpu.VMEM((n, feat), bf),
            pltpu.VMEM((k, n), f32),
            pltpu.VMEM((NY, NX, n, feat), bf),
            pltpu.VMEM((NZ, n, feat), bf),
            [pltpu.VMEM((2, 2, n, feat), bf)] * ROUNDS,
            pltpu.VMEM((ROUNDS, 2, n, NZ * n), bf),
            pltpu.VMEM((ROUNDS, NZ, half, 2 * k), bf),
            pltpu.VMEM((NZ * n, 2 * k), bf),
            pltpu.VMEM((ROUNDS, n, 2 * k), f32),
            pltpu.VMEM((ROUNDS, n, 2 * k), f32),
            [pltpu.VMEM((NX, half, 2 * k), bf)] * ROUNDS,
            [pltpu.VMEM((NY, half, 2 * k), bf)] * ROUNDS,
            pltpu.VMEM((half, 2 * k), bf),
            pltpu.VMEM((half, 2 * k), f32),
            pltpu.VMEM((2, half, 2 * k), f32),
            pltpu.VMEM((half, 2 * k), f32),
            pltpu.VMEM((NX, half, 2 * k), f32),
            pltpu.VMEM((NY, half, 2 * k), f32),
            pltpu.VMEM((2 * NX, slab, 2 * k), f32),
            pltpu.VMEM((NY, slab, 2 * k), f32),
            pltpu.VMEM((NZ, slab, 2 * k), f32),
            pltpu.VMEM((2 * NX, slab, 2 * k), f32),
            pltpu.VMEM((2 * NX, slab, 2 * k), f32),
            dma((3,)),
            dma((61,)), dma((61,)),
            dma((ROUNDS, NZ)), dma((ROUNDS, NZ)),
            dma((ROUNDS + 1, 8)), dma((ROUNDS + 1, 8)),
            dma((ROUNDS,)), dma((ROUNDS,)),
            dma((28,)), dma((28,)),
        ],
        compiler_params=pltpu.CompilerParams(
            collective_id=0, has_side_effects=True, vmem_limit_bytes=60 * 1024 * 1024
        ),
        name="rounds",
    )(round_masks, shots, basis.T)
    iterate_t, ritz = pl.pallas_call(
        functools.partial(finish_kernel, float(nown * nrep * n)),
        out_shape=(jax.ShapeDtypeStruct((k, n), f32), jax.ShapeDtypeStruct((k, k), f32)),
        in_specs=[vmem],
        out_specs=(vmem, vmem),
        name="finish",
    )(both)
    return iterate_t.T, ritz


def solution(mesh):
    in_specs = (P(("owner", "rep"), None), P(("owner", "rep"), None), P())
    out_specs = (P(("owner", "rep"), None), P())
    return jax.shard_map(shards, mesh=mesh, in_specs=in_specs, out_specs=out_specs, check_vma=False)
```

```python
import functools
import math

import jax
import jax.numpy as jnp
from jax import lax
from jax.experimental import pallas as pl
from jax.experimental.pallas import tpu as pltpu
from jax.sharding import PartitionSpec as P

ROUNDS = 3
SHARPNESS = 1.6
MESH = pl.DeviceIdType.MESH
NT = (((1,), (1,)), ((), ()))
TN = (((0,), (0,)), ((), ()))
NX, NY, NZ = 4, 4, 8

ORDER_STAYS = (
    (
        ("G", 1, 1), ("G", 1, -1), ("F", 1, 1), ("Z", 1, 0, 1), ("Z", 1, 0, -1), ("Z", 1, 1, 1), ("Z", 1, 1, -1),
        ("G", 2, 1), ("G", 2, -1), ("Q", 1, 1), ("F", 0, 3), ("F", 0, 1), ("F", 1, 3), ("Q", 1, 0), ("Z", 2, 0, 1),
        ("Z", 2, 0, -1), ("Q", 0, 0), ("Q", 0, 1), ("Z", 2, 1, 1), ("Z", 2, 1, -1), ("G", 3, 1), ("G", 3, -1),
        ("Z", 3, 0, 1), ("Z", 3, 0, -1), ("F", 5, 3), ("F", 5, 1), ("F", 2, 3), ("F", 2, 1), ("Z", 3, 1, 1),
        ("Z", 3, 1, -1), ("G", 4, 1), ("Q", 5, 0), ("Q", 5, 1), ("Z", 4, 0, 1), ("Q", 2, 0), ("Q", 2, 1), ("F", 6, 3),
        ("F", 6, 1), ("Z", 4, 1, -1), ("X", 0),
    ),
    (
        ("Q", 6, 0), ("Q", 6, 1), ("F", 3, 3), ("F", 3, 1), ("F", 7, 3), ("F", 7, 1), ("Q", 3, 0), ("Q", 3, 1),
    ),
    (
        ("Q", 7, 0), ("X", 1),
    ),
    (
        ("Q", 7, 1), ("F", 4, 3), ("F", 4, 1), ("Q", 4, 0), ("Q", 4, 1),
    ),
    (
        ("X", 2),
    ),
)
ORDER_MOVED = (
    (
        ("T",), ("F", 1, 1), ("F", 1, 3), ("O", 0), ("G", 1, 1), ("G", 1, -1), ("Q", 1, 1), ("O", 1), ("F", 0, 3),
        ("F", 0, 1), ("Q", 1, 0), ("Z", 1, 0, 1), ("Z", 1, 0, -1), ("G", 2, 1), ("G", 2, -1), ("Q", 0, 0),
        ("Q", 0, 1), ("Z", 1, 1, 1), ("Z", 1, 1, -1), ("F", 5, 3), ("F", 5, 1), ("Z", 2, 0, 1), ("Z", 2, 0, -1),
        ("G", 3, 1), ("G", 3, -1), ("F", 2, 3), ("F", 2, 1), ("Z", 2, 1, -1), ("Q", 5, 0), ("Q", 5, 1),
        ("Z", 2, 1, 1), ("Z", 3, 0, -1), ("Q", 2, 0), ("Q", 2, 1), ("Z", 3, 0, 1), ("F", 6, 3), ("F", 6, 1),
        ("G", 4, 1), ("Z", 3, 1, -1), ("X", 0), ("Z", 3, 1, 1), ("Z", 4, 0, 1), ("Q", 6, 0), ("Q", 6, 1), ("F", 3, 3),
        ("F", 3, 1), ("Z", 4, 1, -1),
    ),
    (
        ("F", 7, 3), ("F", 7, 1), ("Q", 3, 0), ("Q", 3, 1),
    ),
    (
        ("Q", 7, 0), ("Q", 7, 1), ("X", 1),
    ),
    (
        ("F", 4, 3), ("F", 4, 1), ("Q", 4, 0), ("Q", 4, 1),
    ),
    (
        ("X", 2),
    ),
)


def dot32(a, b, dims):
    return lax.dot_general(a, b, dims, precision=lax.Precision.HIGHEST, preferred_element_type=jnp.float32)


def pack(rows):
    half = rows.shape[0] // 2
    return jnp.concatenate([rows[:half], rows[half:]], axis=1)


def rounds_kernel(
    scale, masks_hbm, shots_hbm, basis_hbm, out,
    masks, shots, basis_t, unit, rowbuf, colbuf, sel0, sel1, own, cands, aff, gpart, gfull, wsend, wrecv, xbufs, ybufs, homeward, ghome, gsend, gback, gx, gy,
    rs, ys, zs, fin, prod,
    s_in, s1, r1, sg, rg, sc, rc, sw, rw, sa, ra,
):
    n, feat = shots.shape
    half, n0 = n // 2, rowbuf.shape[1]
    n1 = n - n0
    k = basis_t.shape[0]
    o, r = lax.axis_index("owner"), lax.axis_index("rep")
    c, x, yh = o % 2, (o // 2) % NX, o // (2 * NX)
    z, yl = r // 2, r % 2
    y = yh * 2 + yl
    nq = 2 * NX
    q = x * 2 + c

    def dev(y=y, x=x, c=c, z=z):
        return (((y // 2) * NX + x) * 2 + c, z * 2 + y % 2)

    twin_y = yh * 2 + c
    twin = dev(y=twin_y, c=yl)
    other_core = dev(c=1 - c)
    moved = c != yl
    stays = c == yl

    loads = [
        pltpu.make_async_copy(shots_hbm, shots, s_in.at[0]),
        pltpu.make_async_copy(basis_hbm, basis_t, s_in.at[1]),
        pltpu.make_async_copy(masks_hbm, masks, s_in.at[2]),
    ]
    for copy in loads:
        copy.start()

    bar = pltpu.get_barrier_semaphore()

    def hello(device):
        pl.semaphore_signal(bar, inc=1, device_id=device, device_id_type=MESH)

    neighbours = [dev(x=(x + i) % NX) for i in (1, 3)] + [dev(y=(y + i) % NY) for i in (1, 3)]
    neighbours += [dev(z=(z + i) % NZ) for i in (1, 7)]
    for neighbour in neighbours:
        hello(neighbour)

    @pl.when(moved)
    def _():
        hello(twin)

    hello(other_core)

    for copy in loads:
        copy.wait()
    values = shots[...].astype(jnp.float32)
    inv = lax.rsqrt(jnp.mean(values * values, axis=-1, keepdims=True) + 1e-06)
    units = (values * inv).astype(jnp.bfloat16)
    rowbuf[x] = units[:n0]
    colbuf[y] = units[n0:]
    g0 = pack(basis_t[...].T)

    @pl.when(stays)
    def _():
        own[z] = units
        ghome[...] = g0

    @pl.when(moved)
    def _():
        unit[...] = units
        gsend[0] = g0

    pl.semaphore_wait(bar, len(neighbours) + 1 + (c + yl) % 2)

    def send(src, dst, ssem, rsem, device):
        return pltpu.make_async_remote_copy(
            src_ref=src, dst_ref=dst, send_sem=ssem, recv_sem=rsem, device_id=device, device_id_type=MESH
        )

    pending = []

    def all_sent(numbers):
        for number, rows in numbers:
            ref = own.at[0, pl.ds(0, rows)]
            send(ref, ref, s1.at[number], r1.at[number], other_core).wait_send()

    def move(src, dst, number, device):
        send(src, dst, s1.at[number], r1.at[number], device).start()
        pending.append((number, math.prod(src.shape[:-1])))

    def same(ref, number, device):
        move(ref, ref, number, device)

    def landed(ref, number):
        send(ref, ref, s1.at[number], r1.at[number], other_core).wait_recv()

    halves = (pl.ds(0, half), pl.ds(half, half))
    RING, UP, DN, CORE, TRADE = 0, 32, 39, 46, 52

    trade = send(gsend.at[0], ghome, s1.at[TRADE + 2], r1.at[TRADE + 2], twin)

    def leg(number, i):
        if number == 0:
            return rowbuf.at[(x + i) % NX]
        if number == 1:
            return colbuf.at[(y + i) % NY]
        if number < 5:
            return sel0[number - 2].at[(y + i) % NY]
        return sel1[number - 5].at[(x + i) % NX]

    def part_of(number, i, part):
        ref = leg(number, i)
        if number >= 5:
            return ref.at[part]
        size = ref.shape[0] // 2
        return ref.at[pl.ds(part * size, size)]

    def step(number, i):
        return dev(x=(x + i) % NX) if number in (0, 5, 6, 7) else dev(y=(y + i) % NY)

    def begin(number):
        same(leg(number, 0), RING + 4 * number, step(number, 1))
        same(leg(number, 0), RING + 4 * number + 1, step(number, 3))

    def on_full(number, k):
        part = 0 if k == 3 else 1
        landed(leg(number, k), RING + 4 * number + part)
        same(part_of(number, k, part), RING + 4 * number + 2 + part, step(number, 4 - k))

    def on_half(number, part):
        landed(part_of(number, 2, part), RING + 4 * number + 2 + part)

    def pick():
        for t in range(ROUNDS):
            m = masks[t]
            sel0[t][y] = rowbuf[x ^ ((m // 2) % 4)]
            for a in range(2):
                sel1[t][x, a] = colbuf[(yh ^ (m // 8)) * 2 + a]
        begin(2)
        begin(5)

    up, down = dev(z=(z + 1) % NZ), dev(z=(z + NZ - 1) % NZ)

    def z_begin(h):
        same(own.at[z, halves[h]], UP + h, up)
        same(own.at[z, halves[h]], DN + h, down)

    def on_z(s, h, direction):
        ref = own.at[(z + NZ - direction * s) % NZ, halves[h]]
        base = UP if direction == 1 else DN
        landed(ref, base + (2 * (s - 1) + h if s < 4 else 6))
        if s < 3 or (s == 3 and (h == 0) == (direction == 1)):
            same(ref, base + (2 * s + h if s < 3 else 6), up if direction == 1 else down)

    def g_begin():
        gpart[0, z] = ghome[...].astype(jnp.bfloat16)
        for i, device in ((1, up), (7, down)):
            send(gpart.at[0, z], gpart.at[0, z], sg.at[0, i], rg.at[0, i], device).start()

    def on_g(s, direction):
        ref = gpart.at[0, (z + NZ - direction * s) % NZ]
        i = s if direction == 1 else NZ - s
        send(ref, ref, sg.at[0, i], rg.at[0, i], other_core).wait_recv()
        if s < 3 or (s == 3 and direction == 1):
            send(ref, ref, sg.at[0, i + direction], rg.at[0, i + direction], up if direction == 1 else down).start()

    def choose(t):
        m = masks[t]
        for a in range(2):
            cands[t][c, a, :n0] = sel0[t][(yh ^ (m // 8)) * 2 + a]
            cands[t][c, a, n0:] = sel1[t][x ^ ((m // 2) % 4), a]
            number = CORE + 2 * t + a
            same(cands[t].at[c, a], number, other_core)

    def near(j):
        return (NZ + (1 - 2 * ((j + 1) % 2)) * ((j + 1) // 2)) % NZ

    def affinities(t, lo=0, hi=NZ):
        holder = yl ^ (masks[t] % 2)

        @pl.loop(lo, hi)
        def _(j):
            item = (z + near(j)) % NZ
            columns = pl.ds(pl.multiple_of(item * n, n), n)
            for a in range(2):
                scores = lax.dot_general(cands[t][holder, a], own[item], NT, preferred_element_type=jnp.float32)
                aff[t, a, :, columns] = jnp.exp(scores * scale).astype(jnp.bfloat16)

    def gather(order, seen, stays_here):
        def whole(number):
            return all(e in seen for e in (("F", number, 1), ("F", number, 3), ("Q", number, 0), ("Q", number, 1)))

        def z_here(s):
            if s == 0:
                return stays_here or (("O", 0) in seen and ("O", 1) in seen)
            if s == 4:
                return ("Z", 4, 0, 1) in seen and ("Z", 4, 1, -1) in seen
            return all(("Z", s, h, d) in seen for h in (0, 1) for d in (1, -1))

        for event in order:
            kind, *args = event
            seen.add(event)
            if kind == "F":
                on_full(*args)
                number, k = args
                if number in (2, 3, 5, 6) and ("F", number, 4 - k) in seen:
                    begin(number + 1)
            elif kind == "Q":
                on_half(*args)
            elif kind == "Z":
                on_z(*args)
            elif kind == "G":
                on_g(*args)
            elif kind == "O":
                landed(own.at[z, halves[args[0]]], TRADE + args[0])
                z_begin(args[0])
            elif kind == "T":
                trade.wait_recv()
                g_begin()
            else:
                for a in range(2):
                    landed(cands[args[0]].at[1 - c, a], CORE + 2 * args[0] + a)
            if kind in "FQ":
                if "picked" not in seen and whole(0) and whole(1):
                    seen.add("picked")
                    pick()
                for t in range(ROUNDS):
                    if ("chosen", t) not in seen and whole(2 + t) and whole(5 + t):
                        seen.add(("chosen", t))
                        choose(t)
            have = sum(("items", j) in seen for j in range(NZ))
            ready = have
            while ("X", 0) in seen and ready < NZ and z_here((ready + 1) // 2):
                seen.add(("items", ready))
                ready += 1
            if ready > have:
                affinities(0, have, ready)

    seen_stays, seen_moved = set(), set()

    @pl.when(stays)
    def _():
        g_begin()
        z_begin(0)
        z_begin(1)
        begin(0)
        begin(1)
        gather(ORDER_STAYS[0], seen_stays, True)

    sent_if_stays = list(pending)
    pending.clear()

    @pl.when(moved)
    def _():
        trade.start()
        for h in range(2):
            move(unit.at[halves[h]], own.at[z, halves[h]], TRADE + h, twin)
        begin(0)
        begin(1)
        gather(ORDER_MOVED[0], seen_moved, False)

    sent_if_moved = list(pending)
    pending.clear()

    def gather_rest(stage):
        @pl.when(stays)
        def _():
            gather(ORDER_STAYS[stage], seen_stays, True)

        sent_if_stays.extend(pending)
        pending.clear()

        @pl.when(moved)
        def _():
            gather(ORDER_MOVED[stage], seen_moved, False)

        sent_if_moved.extend(pending)
        pending.clear()

    def g_send(t, value):
        gpart[t, z] = value.astype(jnp.bfloat16)

        for i in (3, 5, 4, 2, 6, 1, 7):
            send(gpart.at[t, z], gpart.at[t, z], sg.at[t, i], rg.at[t, i], dev(z=(z + i) % NZ)).start()

    grown = ghome[...]

    def partner(t):
        m = masks[t]
        return y ^ ((m // 8) * 2 + m % 2), x ^ ((m // 2) % 4)

    lane = lax.broadcasted_iota(jnp.int32, (half, 2 * k), 1)
    tail = jnp.where(lane == k, 1.0, 0.0)

    def unpack(t, item):
        p = gpart[t, item].astype(jnp.float32)
        start = pl.multiple_of(item * n, n)
        gfull[pl.ds(start, half), :] = jnp.where(lane < k, p, tail).astype(jnp.bfloat16)
        gfull[pl.ds(start + half, half), :] = jnp.where(lane < k, pltpu.roll(p, k, 1), tail).astype(jnp.bfloat16)

    def carried(t):
        unpack(t, z)

        @pl.loop(1, NZ)
        def _(j):
            i = near(j)
            item = (z + NZ - i) % NZ
            if t > 0:
                ref = gpart.at[t, item]
                send(ref, ref, sg.at[t, i], rg.at[t, i], other_core).wait_recv()
            unpack(t, item)

        wsend[t] = jnp.dot(aff[t, 1 - c], gfull[...], preferred_element_type=jnp.float32)
        copy = send(wsend.at[t], wrecv.at[t], sw.at[t], rw.at[t], other_core)
        copy.start()
        mine = jnp.dot(aff[t, c], gfull[...], preferred_element_type=jnp.float32)
        copy.wait_recv()
        product = mine + wrecv[t]
        return pack(product[:, :k] / product[:, k:k + 1]).astype(jnp.bfloat16)

    def x_send(ref, sems, t, base):
        for i in (2, 1, 3):
            send(ref, ref, sems[0].at[t, base + i], sems[1].at[t, base + i], dev(x=(x + i) % NX)).start()

    def x_wait(buf, sems, t, base):
        for i in range(1, NX):
            ref = buf.at[(x + NX - i) % NX]
            send(ref, ref, sems[0].at[t, base + i], sems[1].at[t, base + i], other_core).wait_recv()

    def y_send(ref, sems, t, base):
        for i in (2, 1, 3):
            send(ref, ref, sems[0].at[t, base + i], sems[1].at[t, base + i], dev(y=(y + i) % NY)).start()

    def y_wait(buf, sems, t, base):
        for i in range(1, NY):
            ref = buf.at[(y + NY - i) % NY]
            send(ref, ref, sems[0].at[t, base + i], sems[1].at[t, base + i], other_core).wait_recv()

    csem = (sc, rc)
    for t in range(ROUNDS - 1):
        if t > 0:
            g_send(t, grown)
            gather_rest(3)
        py, px = partner(t)
        xbufs[t][x] = carried(t)
        x_send(xbufs[t].at[x], csem, t, 0)
        if t == 0:
            gather_rest(1)
        else:
            gather_rest(4)
            affinities(2)
        x_wait(xbufs[t], csem, t, 0)
        ybufs[t][y] = xbufs[t][px]
        y_send(ybufs[t].at[y], csem, t, 4)
        if t == 0:
            gather_rest(2)
            affinities(1)
        y_wait(ybufs[t], csem, t, 4)
        grown = grown + ybufs[t][py].astype(jnp.float32)

    t = ROUNDS - 1
    py, px = partner(t)
    g_send(t, grown)
    gx[x] = grown
    x_send(gx.at[x], csem, ROUNDS, 0)

    @pl.when(stays)
    def _():
        gback[...] = grown

    @pl.when(moved)
    def _():
        gsend[1] = grown
        send(gsend.at[1], gback, s1.at[TRADE + 3], r1.at[TRADE + 3], twin).start()

    x_wait(gx, csem, ROUNDS, 0)
    gy[y] = gx[px]
    y_send(gy.at[y], csem, ROUNDS, 4)
    came = carried(t)
    xbufs[t][x] = came
    x_send(xbufs[t].at[x], csem, t, 0)
    y_wait(gy, csem, ROUNDS, 4)
    before = gy[py]
    after = before + came.astype(jnp.float32)

    top = jnp.where(lane < k, before, pltpu.roll(after, k, 1))
    bottom = jnp.where(lane < k, pltpu.roll(before, k, 1), after)
    prod[...] = (dot32(top, top, TN) + dot32(bottom, bottom, TN)).reshape(prod.shape)

    def total(ref, count):
        value = ref[0]
        for i in range(1, count):
            value = value + ref[i]
        return value

    def q_dev(i):
        there = (q + i) % nq
        return dev(x=there // 2, c=there % 2)

    @pl.loop(1, nq)
    def _(i):
        send(prod.at[(q + i) % nq], rs.at[q], sa.at[i], ra.at[i], q_dev(i)).start()

    rs[q] = prod[q]

    x_wait(xbufs[t], csem, t, 0)
    homeward[...] = xbufs[t][px]

    @pl.when(stays)
    def _():
        ybufs[t][y] = homeward[...]

    def home_copy(i):
        ty = (y + i) % NY
        device = dev(y=(ty // 2) * 2 + c, c=ty % 2)
        return send(homeward, ybufs[t].at[y], sc.at[t, 4 + i], rc.at[t, 4 + i], device)

    @pl.when(moved)
    def _():
        home_copy(0).start()

    for i in range(1, NY):
        home_copy(i).start()

    @pl.loop(1, nq)
    def _(i):
        send(prod.at[0], rs.at[(q + nq - i) % nq], sa.at[i], ra.at[i], other_core).wait_recv()

    ys[y] = total(rs, nq)

    @pl.loop(1, NY)
    def _(i):
        send(ys.at[y], ys.at[y], sa.at[8 + i], ra.at[8 + i], dev(y=(y + i) % NY)).start()

    @pl.loop(1, NY)
    def _(i):
        ref = ys.at[(y + NY - i) % NY]
        send(ref, ref, sa.at[8 + i], ra.at[8 + i], other_core).wait_recv()

    zs[z] = total(ys, NY)

    for i in (3, 5, 4, 2, 6, 1, 7):
        send(zs.at[z], zs.at[z], sa.at[12 + i], ra.at[12 + i], dev(z=(z + i) % NZ)).start()

    @pl.loop(1, NZ)
    def _(i):
        ref = zs.at[(z + NZ - i) % NZ]
        send(ref, ref, sa.at[12 + i], ra.at[12 + i], other_core).wait_recv()

    fin[q] = total(zs, NZ)

    @pl.loop(1, nq)
    def _(i):
        send(fin.at[q], fin.at[q], sa.at[20 + i], ra.at[20 + i], q_dev(i)).start()

    @pl.when(moved)
    def _():
        send(gsend.at[1], gback, s1.at[TRADE + 3], r1.at[TRADE + 3], twin).wait_recv()
        ref = ybufs[t].at[twin_y]
        send(ref, ref, sc.at[t, 4], rc.at[t, 4], other_core).wait_recv()

    for i in range(1, NY):
        ref = ybufs[t].at[(twin_y + NY - i) % NY]
        send(ref, ref, sc.at[t, 4 + i], rc.at[t, 4 + i], other_core).wait_recv()
    m = masks[t]
    out[:half, :] = gback[...] + ybufs[t][twin_y ^ ((m // 8) * 2 + m % 2)].astype(jnp.float32)

    @pl.loop(1, nq)
    def _(i):
        ref = fin.at[(q + nq - i) % nq]
        send(ref, ref, sa.at[20 + i], ra.at[20 + i], other_core).wait_recv()

    out[half:, :] = fin[...].reshape(2 * k, 2 * k)

    assert not pending

    @pl.when(stays)
    def _():
        all_sent(sent_if_stays)

    @pl.when(moved)
    def _():
        all_sent(sent_if_moved)
        trade.wait_send()
        send(gsend.at[1], gback, s1.at[TRADE + 3], r1.at[TRADE + 3], twin).wait_send()
        home_copy(0).wait_send()

    @pl.loop(1, NX)
    def _(i):
        for row in range(ROUNDS):
            ref = xbufs[row].at[x]
            send(ref, ref, sc.at[row, i], rc.at[row, i], other_core).wait_send()
            send(ref, ref, sc.at[row, 4 + i], rc.at[row, 4 + i], other_core).wait_send()
        ref = gx.at[x]
        send(ref, ref, sc.at[ROUNDS, i], rc.at[ROUNDS, i], other_core).wait_send()
        send(ref, ref, sc.at[ROUNDS, 4 + i], rc.at[ROUNDS, 4 + i], other_core).wait_send()
        send(ys.at[y], ys.at[y], sa.at[8 + i], ra.at[8 + i], other_core).wait_send()

    @pl.loop(1, NZ)
    def _(i):
        for row in range(ROUNDS):
            ref = gpart.at[row, z]
            send(ref, ref, sg.at[row, i], rg.at[row, i], other_core).wait_send()
        for base in (0, 12, 20):
            send(fin.at[q], fin.at[q], sa.at[base + i], ra.at[base + i], other_core).wait_send()

    for row in range(ROUNDS):
        send(wsend.at[row], wrecv.at[row], sw.at[row], rw.at[row], other_core).wait_send()


def inverse_factors(grams):
    k = grams[0].shape[0]
    row = lax.broadcasted_iota(jnp.int32, (k, 2 * k), 0)
    lane = lax.broadcasted_iota(jnp.int32, (k, 2 * k), 1)
    identity = jnp.where(lane == row, 1.0, 0.0)[:, :k]
    works = [jnp.concatenate([gram, identity], axis=1) for gram in grams]
    works = [[work[8 * g:8 * g + 8] for g in range(k // 8)] for work in works]
    below = lax.broadcasted_iota(jnp.int32, (8, 1), 0)
    for i in range(k - 1):
        own, s = i // 8, i % 8
        for work in works:
            pivot = work[own][s:s + 1, :] * (1.0 / work[own][s:s + 1, i:i + 1])
            for g in range(own, k // 8):
                factor = work[g][:, i:i + 1]
                if g == own:
                    factor = jnp.where(below > s, factor, 0.0)
                work[g] = work[g] - factor * pivot
    results = []
    for work in works:
        whole = jnp.concatenate(work, axis=0)
        diagonal = jnp.sum(jnp.where(lane == row, whole, 0.0), axis=1, keepdims=True)
        results.append(whole[:, k:] * (1.0 / jnp.sqrt(diagonal)))
    return results


def finish_kernel(total_rows, both, iterate_t, ritz):
    k = ritz.shape[0]
    half = both.shape[0] - 2 * k
    every = both[half:, :] * (1.0 / total_rows)
    inv_before, inv_last = inverse_factors([every[:k, :k], every[k:, k:]])
    packed = both[:half, :]
    iterate_t[:, :half] = dot32(inv_last, packed[:, :k], NT)
    iterate_t[:, half:] = dot32(inv_last, packed[:, k:], NT)
    left = dot32(inv_before, every[:k, k:], (((1,), (0,)), ((), ())))
    ritz[...] = dot32(left, inv_before, NT)


def shards(shots, basis, round_masks):
    n, feat = shots.shape
    k = basis.shape[1]
    nrep, nown = lax.axis_size("rep"), lax.axis_size("owner")
    half, n0 = n // 2, n * 3 // 4
    bf, f32 = jnp.bfloat16, jnp.float32
    vmem = pl.BlockSpec(memory_space=pltpu.VMEM)
    slab = (2 * k) // (2 * NX)
    dma = pltpu.SemaphoreType.DMA
    both = pl.pallas_call(
        functools.partial(rounds_kernel, SHARPNESS / math.sqrt(feat)),
        out_shape=jax.ShapeDtypeStruct((half + 2 * k, 2 * k), f32),
        in_specs=[pl.BlockSpec(memory_space=pltpu.HBM)] * 3,
        out_specs=vmem,
        scratch_shapes=[
            pltpu.SMEM((ROUNDS,), jnp.int32),
            pltpu.VMEM((n, feat), bf),
            pltpu.VMEM((k, n), f32),
            pltpu.VMEM((n, feat), bf),
            pltpu.VMEM((NX, n0, feat), bf),
            pltpu.VMEM((NY, n - n0, feat), bf),
            [pltpu.VMEM((NY, n0, feat), bf)] * ROUNDS,
            [pltpu.VMEM((NX, 2, n - n0, feat), bf)] * ROUNDS,
            pltpu.VMEM((NZ, n, feat), bf),
            [pltpu.VMEM((2, 2, n, feat), bf)] * ROUNDS,
            pltpu.VMEM((ROUNDS, 2, n, NZ * n), bf),
            pltpu.VMEM((ROUNDS, NZ, half, 2 * k), bf),
            pltpu.VMEM((NZ * n, 2 * k), bf),
            pltpu.VMEM((ROUNDS, n, 2 * k), f32),
            pltpu.VMEM((ROUNDS, n, 2 * k), f32),
            [pltpu.VMEM((NX, half, 2 * k), bf)] * ROUNDS,
            [pltpu.VMEM((NY, half, 2 * k), bf)] * ROUNDS,
            pltpu.VMEM((half, 2 * k), bf),
            pltpu.VMEM((half, 2 * k), f32),
            pltpu.VMEM((2, half, 2 * k), f32),
            pltpu.VMEM((half, 2 * k), f32),
            pltpu.VMEM((NX, half, 2 * k), f32),
            pltpu.VMEM((NY, half, 2 * k), f32),
            pltpu.VMEM((2 * NX, slab, 2 * k), f32),
            pltpu.VMEM((NY, slab, 2 * k), f32),
            pltpu.VMEM((NZ, slab, 2 * k), f32),
            pltpu.VMEM((2 * NX, slab, 2 * k), f32),
            pltpu.VMEM((2 * NX, slab, 2 * k), f32),
            dma((3,)),
            dma((56,)), dma((56,)),
            dma((ROUNDS, NZ)), dma((ROUNDS, NZ)),
            dma((ROUNDS + 1, 8)), dma((ROUNDS + 1, 8)),
            dma((ROUNDS,)), dma((ROUNDS,)),
            dma((28,)), dma((28,)),
        ],
        compiler_params=pltpu.CompilerParams(
            collective_id=0, has_side_effects=True, vmem_limit_bytes=60 * 1024 * 1024
        ),
        name="rounds",
    )(round_masks, shots, basis.T)
    iterate_t, ritz = pl.pallas_call(
        functools.partial(finish_kernel, float(nown * nrep * n)),
        out_shape=(jax.ShapeDtypeStruct((k, n), f32), jax.ShapeDtypeStruct((k, k), f32)),
        in_specs=[vmem],
        out_specs=(vmem, vmem),
        name="finish",
    )(both)
    return iterate_t.T, ritz


def solution(mesh):
    in_specs = (P(("owner", "rep"), None), P(("owner", "rep"), None), P())
    out_specs = (P(("owner", "rep"), None), P())
    return jax.shard_map(shards, mesh=mesh, in_specs=in_specs, out_specs=out_specs, check_vma=False)
```

```python
import functools
import math

import jax
import jax.numpy as jnp
from jax import lax
from jax.experimental import pallas as pl
from jax.experimental.pallas import tpu as pltpu
from jax.sharding import PartitionSpec as P

ROUNDS = 3
SHARPNESS = 1.6
MESH = pl.DeviceIdType.MESH
NT = (((1,), (1,)), ((), ()))
TN = (((0,), (0,)), ((), ()))
NX, NY, NZ = 4, 4, 8

ORDER_STAYS = (
    (
        ("G", 1, 1), ("G", 1, -1), ("Z", 1, 0, 1), ("Z", 1, 0, -1), ("F", 1, 1), ("Z", 1, 1, 1), ("Z", 1, 1, -1),
        ("G", 2, 1), ("G", 2, -1), ("F", 0, 3), ("F", 0, 1), ("Q", 1, 1), ("F", 1, 3), ("Z", 2, 0, 1),
        ("Z", 2, 0, -1), ("Q", 1, 0), ("Q", 0, 0), ("Q", 0, 1), ("Z", 2, 1, 1), ("Z", 2, 1, -1), ("G", 3, 1),
        ("G", 3, -1), ("Z", 3, 0, 1), ("Z", 3, 0, -1), ("F", 5, 3), ("F", 5, 1), ("F", 2, 3), ("F", 2, 1),
        ("Z", 3, 1, 1), ("Z", 3, 1, -1), ("G", 4, 1), ("F", 6, 3), ("F", 6, 1), ("F", 3, 3), ("F", 3, 1),
        ("Z", 4, 0, 1), ("Q", 5, 0), ("Q", 5, 1), ("Z", 4, 1, -1), ("Q", 2, 0), ("Q", 2, 1), ("X", 0),
    ),
    (
        ("F", 7, 3), ("F", 7, 1), ("F", 4, 3), ("F", 4, 1), ("Q", 6, 0), ("Q", 6, 1), ("Q", 3, 0), ("Q", 3, 1),
    ),
    (
        ("Q", 7, 0), ("Q", 7, 1), ("X", 1),
    ),
    (
        ("Q", 4, 0), ("Q", 4, 1),
    ),
    (
        ("X", 2),
    ),
)
ORDER_MOVED = (
    (
        ("T",), ("F", 1, 1), ("F", 1, 3), ("O", 0), ("G", 1, 1), ("G", 1, -1), ("F", 0, 3), ("F", 0, 1), ("O", 1),
        ("Q", 1, 1), ("Q", 1, 0), ("Z", 1, 0, 1), ("Z", 1, 0, -1), ("Q", 0, 0), ("Q", 0, 1), ("G", 2, 1),
        ("G", 2, -1), ("Z", 1, 1, 1), ("Z", 1, 1, -1), ("F", 5, 3), ("F", 5, 1), ("Z", 2, 0, 1), ("Z", 2, 0, -1),
        ("F", 2, 3), ("F", 2, 1), ("G", 3, 1), ("G", 3, -1), ("Z", 2, 1, -1), ("Z", 2, 1, 1), ("F", 6, 3),
        ("F", 6, 1), ("F", 3, 3), ("F", 3, 1), ("Z", 3, 0, -1), ("Q", 5, 0), ("Q", 5, 1), ("Z", 3, 0, 1), ("G", 4, 1),
        ("Q", 2, 0), ("Q", 2, 1), ("Z", 3, 1, -1), ("Z", 3, 1, 1), ("X", 0), ("Z", 4, 0, 1), ("F", 7, 3), ("F", 7, 1),
        ("Z", 4, 1, -1),
    ),
    (
        ("F", 4, 3), ("F", 4, 1), ("Q", 6, 0), ("Q", 6, 1), ("Q", 3, 0), ("Q", 3, 1),
    ),
    (
        ("Q", 7, 0), ("Q", 7, 1), ("Q", 4, 0), ("Q", 4, 1), ("X", 1),
    ),
    (
    ),
    (
        ("X", 2),
    ),
)


def dot32(a, b, dims):
    return lax.dot_general(a, b, dims, precision=lax.Precision.HIGHEST, preferred_element_type=jnp.float32)


def pack(rows):
    half = rows.shape[0] // 2
    return jnp.concatenate([rows[:half], rows[half:]], axis=1)


def rounds_kernel(
    scale, masks_hbm, shots_hbm, basis_hbm, out,
    masks, shots, basis_t, unit, rowbuf, colbuf, sel0, sel1, own, cands, aff, gpart, gfull, wsend, wrecv, xbufs, ybufs, homeward, ghome, gsend, gback, gx, gy,
    rs, ys, zs, fin, prod,
    s_in, s1, r1, sg, rg, sc, rc, sw, rw, sa, ra,
):
    n, feat = shots.shape
    half, n0 = n // 2, rowbuf.shape[1]
    n1 = n - n0
    k = basis_t.shape[0]
    o, r = lax.axis_index("owner"), lax.axis_index("rep")
    c, x, yh = o % 2, (o // 2) % NX, o // (2 * NX)
    z, yl = r // 2, r % 2
    y = yh * 2 + yl
    nq = 2 * NX
    q = x * 2 + c

    def dev(y=y, x=x, c=c, z=z):
        return (((y // 2) * NX + x) * 2 + c, z * 2 + y % 2)

    twin_y = yh * 2 + c
    twin = dev(y=twin_y, c=yl)
    other_core = dev(c=1 - c)
    moved = c != yl
    stays = c == yl

    loads = [
        pltpu.make_async_copy(shots_hbm, shots, s_in.at[0]),
        pltpu.make_async_copy(basis_hbm, basis_t, s_in.at[1]),
        pltpu.make_async_copy(masks_hbm, masks, s_in.at[2]),
    ]
    for copy in loads:
        copy.start()

    bar = pltpu.get_barrier_semaphore()

    def hello(device):
        pl.semaphore_signal(bar, inc=1, device_id=device, device_id_type=MESH)

    neighbours = [dev(x=(x + i) % NX) for i in (1, 3)] + [dev(y=(y + i) % NY) for i in (1, 3)]
    neighbours += [dev(z=(z + i) % NZ) for i in (1, 7)]
    for neighbour in neighbours:
        hello(neighbour)

    @pl.when(moved)
    def _():
        hello(twin)

    hello(other_core)

    for copy in loads:
        copy.wait()
    values = shots[...].astype(jnp.float32)
    inv = lax.rsqrt(jnp.mean(values * values, axis=-1, keepdims=True) + 1e-06)
    units = (values * inv).astype(jnp.bfloat16)
    rowbuf[x] = units[:n0]
    colbuf[y] = units[n0:]
    g0 = pack(basis_t[...].T)

    @pl.when(stays)
    def _():
        own[z] = units
        ghome[...] = g0

    @pl.when(moved)
    def _():
        unit[...] = units
        gsend[0] = g0

    pl.semaphore_wait(bar, len(neighbours) + 1 + (c + yl) % 2)

    def send(src, dst, ssem, rsem, device):
        return pltpu.make_async_remote_copy(
            src_ref=src, dst_ref=dst, send_sem=ssem, recv_sem=rsem, device_id=device, device_id_type=MESH
        )

    pending = []

    def all_sent(numbers):
        for number, rows in numbers:
            ref = own.at[0, pl.ds(0, rows)]
            send(ref, ref, s1.at[number], r1.at[number], other_core).wait_send()

    def move(src, dst, number, device):
        send(src, dst, s1.at[number], r1.at[number], device).start()
        pending.append((number, math.prod(src.shape[:-1])))

    def same(ref, number, device):
        move(ref, ref, number, device)

    def landed(ref, number):
        send(ref, ref, s1.at[number], r1.at[number], other_core).wait_recv()

    halves = (pl.ds(0, half), pl.ds(half, half))
    RING, UP, DN, CORE, TRADE = 0, 32, 39, 46, 52

    trade = send(gsend.at[0], ghome, s1.at[TRADE + 2], r1.at[TRADE + 2], twin)

    def leg(number, i):
        if number == 0:
            return rowbuf.at[(x + i) % NX]
        if number == 1:
            return colbuf.at[(y + i) % NY]
        if number < 5:
            return sel0[number - 2].at[(y + i) % NY]
        return sel1[number - 5].at[(x + i) % NX]

    def part_of(number, i, part):
        ref = leg(number, i)
        if number >= 5:
            return ref.at[part]
        first = ref.shape[0] // 32 * 16 + 16
        return ref.at[pl.ds(0, first)] if part == 0 else ref.at[pl.ds(first, ref.shape[0] - first)]

    def step(number, i):
        return dev(x=(x + i) % NX) if number in (0, 5, 6, 7) else dev(y=(y + i) % NY)

    def begin(number):
        same(leg(number, 0), RING + 4 * number, step(number, 1))
        same(leg(number, 0), RING + 4 * number + 1, step(number, 3))

    def on_full(number, k):
        part = 0 if k == 3 else 1
        landed(leg(number, k), RING + 4 * number + part)
        same(part_of(number, k, part), RING + 4 * number + 2 + part, step(number, 4 - k))

    def on_half(number, part):
        landed(part_of(number, 2, part), RING + 4 * number + 2 + part)

    def pick():
        for t in range(ROUNDS):
            m = masks[t]
            sel0[t][y] = rowbuf[x ^ ((m // 2) % 4)]
            for a in range(2):
                sel1[t][x, a] = colbuf[(yh ^ (m // 8)) * 2 + a]
        for number in (2, 5, 3, 6):
            begin(number)

    up, down = dev(z=(z + 1) % NZ), dev(z=(z + NZ - 1) % NZ)

    def z_begin(h):
        same(own.at[z, halves[h]], UP + h, up)
        same(own.at[z, halves[h]], DN + h, down)

    def on_z(s, h, direction):
        ref = own.at[(z + NZ - direction * s) % NZ, halves[h]]
        base = UP if direction == 1 else DN
        landed(ref, base + (2 * (s - 1) + h if s < 4 else 6))
        if s < 3 or (s == 3 and (h == 0) == (direction == 1)):
            same(ref, base + (2 * s + h if s < 3 else 6), up if direction == 1 else down)

    def g_begin():
        gpart[0, z] = ghome[...].astype(jnp.bfloat16)
        for i, device in ((1, up), (7, down)):
            send(gpart.at[0, z], gpart.at[0, z], sg.at[0, i], rg.at[0, i], device).start()

    def on_g(s, direction):
        ref = gpart.at[0, (z + NZ - direction * s) % NZ]
        i = s if direction == 1 else NZ - s
        send(ref, ref, sg.at[0, i], rg.at[0, i], other_core).wait_recv()
        if s < 3 or (s == 3 and direction == 1):
            send(ref, ref, sg.at[0, i + direction], rg.at[0, i + direction], up if direction == 1 else down).start()

    def choose(t):
        m = masks[t]
        for a in range(2):
            cands[t][c, a, :n0] = sel0[t][(yh ^ (m // 8)) * 2 + a]
            cands[t][c, a, n0:] = sel1[t][x ^ ((m // 2) % 4), a]
            number = CORE + 2 * t + a
            same(cands[t].at[c, a], number, other_core)

    def near(j):
        return (NZ + (1 - 2 * ((j + 1) % 2)) * ((j + 1) // 2)) % NZ

    def affinities(t, lo=0, hi=NZ):
        holder = yl ^ (masks[t] % 2)

        @pl.loop(lo, hi)
        def _(j):
            item = (z + near(j)) % NZ
            columns = pl.ds(pl.multiple_of(item * n, n), n)
            for a in range(2):
                scores = lax.dot_general(cands[t][holder, a], own[item], NT, preferred_element_type=jnp.float32)
                aff[t, a, :, columns] = jnp.exp(scores * scale).astype(jnp.bfloat16)

    def gather(order, seen, stays_here):
        def whole(number):
            return all(e in seen for e in (("F", number, 1), ("F", number, 3), ("Q", number, 0), ("Q", number, 1)))

        def z_here(s):
            if s == 0:
                return stays_here or (("O", 0) in seen and ("O", 1) in seen)
            if s == 4:
                return ("Z", 4, 0, 1) in seen and ("Z", 4, 1, -1) in seen
            return all(("Z", s, h, d) in seen for h in (0, 1) for d in (1, -1))

        for event in order:
            kind, *args = event
            seen.add(event)
            if kind == "F":
                on_full(*args)
                number, k = args
                if number in (2, 5) and ("F", number, 4 - k) in seen:
                    begin(number + 2)
            elif kind == "Q":
                on_half(*args)
            elif kind == "Z":
                on_z(*args)
            elif kind == "G":
                on_g(*args)
            elif kind == "O":
                landed(own.at[z, halves[args[0]]], TRADE + args[0])
                z_begin(args[0])
            elif kind == "T":
                trade.wait_recv()
                g_begin()
            else:
                for a in range(2):
                    landed(cands[args[0]].at[1 - c, a], CORE + 2 * args[0] + a)
            if kind in "FQ":
                if "picked" not in seen and whole(0) and whole(1):
                    seen.add("picked")
                    pick()
                for t in range(ROUNDS):
                    if ("chosen", t) not in seen and whole(2 + t) and whole(5 + t):
                        seen.add(("chosen", t))
                        choose(t)
            have = sum(("items", j) in seen for j in range(NZ))
            ready = have
            while ("X", 0) in seen and ready < NZ and z_here((ready + 1) // 2):
                seen.add(("items", ready))
                ready += 1
            if ready > have:
                affinities(0, have, ready)

    seen_stays, seen_moved = set(), set()

    @pl.when(stays)
    def _():
        g_begin()
        z_begin(0)
        z_begin(1)
        begin(0)
        begin(1)
        gather(ORDER_STAYS[0], seen_stays, True)

    sent_if_stays = list(pending)
    pending.clear()

    @pl.when(moved)
    def _():
        trade.start()
        for h in range(2):
            move(unit.at[halves[h]], own.at[z, halves[h]], TRADE + h, twin)
        begin(0)
        begin(1)
        gather(ORDER_MOVED[0], seen_moved, False)

    sent_if_moved = list(pending)
    pending.clear()

    def gather_rest(stage):
        @pl.when(stays)
        def _():
            gather(ORDER_STAYS[stage], seen_stays, True)

        sent_if_stays.extend(pending)
        pending.clear()

        @pl.when(moved)
        def _():
            gather(ORDER_MOVED[stage], seen_moved, False)

        sent_if_moved.extend(pending)
        pending.clear()

    def g_send(t, value):
        gpart[t, z] = value.astype(jnp.bfloat16)

        for i in (3, 5, 4, 2, 6, 1, 7):
            send(gpart.at[t, z], gpart.at[t, z], sg.at[t, i], rg.at[t, i], dev(z=(z + i) % NZ)).start()

    grown = ghome[...]

    def partner(t):
        m = masks[t]
        return y ^ ((m // 8) * 2 + m % 2), x ^ ((m // 2) % 4)

    lane = lax.broadcasted_iota(jnp.int32, (half, 2 * k), 1)
    tail = jnp.where(lane == k, 1.0, 0.0)

    def unpack(t, item):
        p = gpart[t, item].astype(jnp.float32)
        start = pl.multiple_of(item * n, n)
        gfull[pl.ds(start, half), :] = jnp.where(lane < k, p, tail).astype(jnp.bfloat16)
        gfull[pl.ds(start + half, half), :] = jnp.where(lane < k, pltpu.roll(p, k, 1), tail).astype(jnp.bfloat16)

    def carried(t):
        unpack(t, z)

        @pl.loop(1, NZ)
        def _(j):
            i = near(j)
            item = (z + NZ - i) % NZ
            if t > 0:
                ref = gpart.at[t, item]
                send(ref, ref, sg.at[t, i], rg.at[t, i], other_core).wait_recv()
            unpack(t, item)

        wsend[t] = jnp.dot(aff[t, 1 - c], gfull[...], preferred_element_type=jnp.float32)
        copy = send(wsend.at[t], wrecv.at[t], sw.at[t], rw.at[t], other_core)
        copy.start()
        mine = jnp.dot(aff[t, c], gfull[...], preferred_element_type=jnp.float32)
        copy.wait_recv()
        product = mine + wrecv[t]
        return pack(product[:, :k] / product[:, k:k + 1]).astype(jnp.bfloat16)

    def x_send(ref, sems, t, base):
        for i in (2, 1, 3):
            send(ref, ref, sems[0].at[t, base + i], sems[1].at[t, base + i], dev(x=(x + i) % NX)).start()

    def x_wait(buf, sems, t, base):
        for i in range(1, NX):
            ref = buf.at[(x + NX - i) % NX]
            send(ref, ref, sems[0].at[t, base + i], sems[1].at[t, base + i], other_core).wait_recv()

    def y_send(ref, sems, t, base):
        for i in (2, 1, 3):
            send(ref, ref, sems[0].at[t, base + i], sems[1].at[t, base + i], dev(y=(y + i) % NY)).start()

    def y_wait(buf, sems, t, base):
        for i in range(1, NY):
            ref = buf.at[(y + NY - i) % NY]
            send(ref, ref, sems[0].at[t, base + i], sems[1].at[t, base + i], other_core).wait_recv()

    csem = (sc, rc)
    for t in range(ROUNDS - 1):
        if t > 0:
            g_send(t, grown)
            gather_rest(3)
        py, px = partner(t)
        xbufs[t][x] = carried(t)
        x_send(xbufs[t].at[x], csem, t, 0)
        if t == 0:
            gather_rest(1)
        else:
            gather_rest(4)
            affinities(2)
        x_wait(xbufs[t], csem, t, 0)
        ybufs[t][y] = xbufs[t][px]
        y_send(ybufs[t].at[y], csem, t, 4)
        if t == 0:
            gather_rest(2)
            affinities(1)
        y_wait(ybufs[t], csem, t, 4)
        grown = grown + ybufs[t][py].astype(jnp.float32)

    t = ROUNDS - 1
    py, px = partner(t)
    g_send(t, grown)
    gx[x] = grown
    x_send(gx.at[x], csem, ROUNDS, 0)

    @pl.when(stays)
    def _():
        gback[...] = grown

    @pl.when(moved)
    def _():
        gsend[1] = grown
        send(gsend.at[1], gback, s1.at[TRADE + 3], r1.at[TRADE + 3], twin).start()

    x_wait(gx, csem, ROUNDS, 0)
    gy[y] = gx[px]
    y_send(gy.at[y], csem, ROUNDS, 4)
    came = carried(t)
    xbufs[t][x] = came
    x_send(xbufs[t].at[x], csem, t, 0)
    y_wait(gy, csem, ROUNDS, 4)
    before = gy[py]
    after = before + came.astype(jnp.float32)

    top = jnp.where(lane < k, before, pltpu.roll(after, k, 1))
    bottom = jnp.where(lane < k, pltpu.roll(before, k, 1), after)
    prod[...] = (dot32(top, top, TN) + dot32(bottom, bottom, TN)).reshape(prod.shape)

    def total(ref, count):
        value = ref[0]
        for i in range(1, count):
            value = value + ref[i]
        return value

    def q_dev(i):
        there = (q + i) % nq
        return dev(x=there // 2, c=there % 2)

    @pl.loop(1, nq)
    def _(i):
        send(prod.at[(q + i) % nq], rs.at[q], sa.at[i], ra.at[i], q_dev(i)).start()

    rs[q] = prod[q]

    x_wait(xbufs[t], csem, t, 0)
    homeward[...] = xbufs[t][px]

    @pl.when(stays)
    def _():
        ybufs[t][y] = homeward[...]

    def home_copy(i):
        ty = (y + i) % NY
        device = dev(y=(ty // 2) * 2 + c, c=ty % 2)
        return send(homeward, ybufs[t].at[y], sc.at[t, 4 + i], rc.at[t, 4 + i], device)

    @pl.when(moved)
    def _():
        home_copy(0).start()

    for i in range(1, NY):
        home_copy(i).start()

    @pl.loop(1, nq)
    def _(i):
        send(prod.at[0], rs.at[(q + nq - i) % nq], sa.at[i], ra.at[i], other_core).wait_recv()

    ys[y] = total(rs, nq)

    @pl.loop(1, NY)
    def _(i):
        send(ys.at[y], ys.at[y], sa.at[8 + i], ra.at[8 + i], dev(y=(y + i) % NY)).start()

    @pl.loop(1, NY)
    def _(i):
        ref = ys.at[(y + NY - i) % NY]
        send(ref, ref, sa.at[8 + i], ra.at[8 + i], other_core).wait_recv()

    zs[z] = total(ys, NY)

    for i in (3, 5, 4, 2, 6, 1, 7):
        send(zs.at[z], zs.at[z], sa.at[12 + i], ra.at[12 + i], dev(z=(z + i) % NZ)).start()

    @pl.loop(1, NZ)
    def _(i):
        ref = zs.at[(z + NZ - i) % NZ]
        send(ref, ref, sa.at[12 + i], ra.at[12 + i], other_core).wait_recv()

    fin[q] = total(zs, NZ)

    @pl.loop(1, nq)
    def _(i):
        send(fin.at[q], fin.at[q], sa.at[20 + i], ra.at[20 + i], q_dev(i)).start()

    @pl.when(moved)
    def _():
        send(gsend.at[1], gback, s1.at[TRADE + 3], r1.at[TRADE + 3], twin).wait_recv()
        ref = ybufs[t].at[twin_y]
        send(ref, ref, sc.at[t, 4], rc.at[t, 4], other_core).wait_recv()

    for i in range(1, NY):
        ref = ybufs[t].at[(twin_y + NY - i) % NY]
        send(ref, ref, sc.at[t, 4 + i], rc.at[t, 4 + i], other_core).wait_recv()
    m = masks[t]
    out[:half, :] = gback[...] + ybufs[t][twin_y ^ ((m // 8) * 2 + m % 2)].astype(jnp.float32)

    @pl.loop(1, nq)
    def _(i):
        ref = fin.at[(q + nq - i) % nq]
        send(ref, ref, sa.at[20 + i], ra.at[20 + i], other_core).wait_recv()

    out[half:, :] = fin[...].reshape(2 * k, 2 * k)

    assert not pending

    @pl.when(stays)
    def _():
        all_sent(sent_if_stays)

    @pl.when(moved)
    def _():
        all_sent(sent_if_moved)
        trade.wait_send()
        send(gsend.at[1], gback, s1.at[TRADE + 3], r1.at[TRADE + 3], twin).wait_send()
        home_copy(0).wait_send()

    @pl.loop(1, NX)
    def _(i):
        for row in range(ROUNDS):
            ref = xbufs[row].at[x]
            send(ref, ref, sc.at[row, i], rc.at[row, i], other_core).wait_send()
            send(ref, ref, sc.at[row, 4 + i], rc.at[row, 4 + i], other_core).wait_send()
        ref = gx.at[x]
        send(ref, ref, sc.at[ROUNDS, i], rc.at[ROUNDS, i], other_core).wait_send()
        send(ref, ref, sc.at[ROUNDS, 4 + i], rc.at[ROUNDS, 4 + i], other_core).wait_send()
        send(ys.at[y], ys.at[y], sa.at[8 + i], ra.at[8 + i], other_core).wait_send()

    @pl.loop(1, NZ)
    def _(i):
        for row in range(ROUNDS):
            ref = gpart.at[row, z]
            send(ref, ref, sg.at[row, i], rg.at[row, i], other_core).wait_send()
        for base in (0, 12, 20):
            send(fin.at[q], fin.at[q], sa.at[base + i], ra.at[base + i], other_core).wait_send()

    for row in range(ROUNDS):
        send(wsend.at[row], wrecv.at[row], sw.at[row], rw.at[row], other_core).wait_send()


def inverse_factors(grams):
    k = grams[0].shape[0]
    row = lax.broadcasted_iota(jnp.int32, (k, 2 * k), 0)
    lane = lax.broadcasted_iota(jnp.int32, (k, 2 * k), 1)
    identity = jnp.where(lane == row, 1.0, 0.0)[:, :k]
    works = [jnp.concatenate([gram, identity], axis=1) for gram in grams]
    works = [[work[8 * g:8 * g + 8] for g in range(k // 8)] for work in works]
    below = lax.broadcasted_iota(jnp.int32, (8, 1), 0)
    for i in range(k - 1):
        own, s = i // 8, i % 8
        for work in works:
            pivot = work[own][s:s + 1, :] * (1.0 / work[own][s:s + 1, i:i + 1])
            for g in range(own, k // 8):
                factor = work[g][:, i:i + 1]
                if g == own:
                    factor = jnp.where(below > s, factor, 0.0)
                work[g] = work[g] - factor * pivot
    results = []
    for work in works:
        whole = jnp.concatenate(work, axis=0)
        diagonal = jnp.sum(jnp.where(lane == row, whole, 0.0), axis=1, keepdims=True)
        results.append(whole[:, k:] * (1.0 / jnp.sqrt(diagonal)))
    return results


def finish_kernel(total_rows, both, iterate_t, ritz):
    k = ritz.shape[0]
    half = both.shape[0] - 2 * k
    every = both[half:, :] * (1.0 / total_rows)
    inv_before, inv_last = inverse_factors([every[:k, :k], every[k:, k:]])
    packed = both[:half, :]
    iterate_t[:, :half] = dot32(inv_last, packed[:, :k], NT)
    iterate_t[:, half:] = dot32(inv_last, packed[:, k:], NT)
    left = dot32(inv_before, every[:k, k:], (((1,), (0,)), ((), ())))
    ritz[...] = dot32(left, inv_before, NT)


def shards(shots, basis, round_masks):
    n, feat = shots.shape
    k = basis.shape[1]
    nrep, nown = lax.axis_size("rep"), lax.axis_size("owner")
    half, n0 = n // 2, n * 11 // 16
    bf, f32 = jnp.bfloat16, jnp.float32
    vmem = pl.BlockSpec(memory_space=pltpu.VMEM)
    slab = (2 * k) // (2 * NX)
    dma = pltpu.SemaphoreType.DMA
    both = pl.pallas_call(
        functools.partial(rounds_kernel, SHARPNESS / math.sqrt(feat)),
        out_shape=jax.ShapeDtypeStruct((half + 2 * k, 2 * k), f32),
        in_specs=[pl.BlockSpec(memory_space=pltpu.HBM)] * 3,
        out_specs=vmem,
        scratch_shapes=[
            pltpu.SMEM((ROUNDS,), jnp.int32),
            pltpu.VMEM((n, feat), bf),
            pltpu.VMEM((k, n), f32),
            pltpu.VMEM((n, feat), bf),
            pltpu.VMEM((NX, n0, feat), bf),
            pltpu.VMEM((NY, n - n0, feat), bf),
            [pltpu.VMEM((NY, n0, feat), bf)] * ROUNDS,
            [pltpu.VMEM((NX, 2, n - n0, feat), bf)] * ROUNDS,
            pltpu.VMEM((NZ, n, feat), bf),
            [pltpu.VMEM((2, 2, n, feat), bf)] * ROUNDS,
            pltpu.VMEM((ROUNDS, 2, n, NZ * n), bf),
            pltpu.VMEM((ROUNDS, NZ, half, 2 * k), bf),
            pltpu.VMEM((NZ * n, 2 * k), bf),
            pltpu.VMEM((ROUNDS, n, 2 * k), f32),
            pltpu.VMEM((ROUNDS, n, 2 * k), f32),
            [pltpu.VMEM((NX, half, 2 * k), bf)] * ROUNDS,
            [pltpu.VMEM((NY, half, 2 * k), bf)] * ROUNDS,
            pltpu.VMEM((half, 2 * k), bf),
            pltpu.VMEM((half, 2 * k), f32),
            pltpu.VMEM((2, half, 2 * k), f32),
            pltpu.VMEM((half, 2 * k), f32),
            pltpu.VMEM((NX, half, 2 * k), f32),
            pltpu.VMEM((NY, half, 2 * k), f32),
            pltpu.VMEM((2 * NX, slab, 2 * k), f32),
            pltpu.VMEM((NY, slab, 2 * k), f32),
            pltpu.VMEM((NZ, slab, 2 * k), f32),
            pltpu.VMEM((2 * NX, slab, 2 * k), f32),
            pltpu.VMEM((2 * NX, slab, 2 * k), f32),
            dma((3,)),
            dma((56,)), dma((56,)),
            dma((ROUNDS, NZ)), dma((ROUNDS, NZ)),
            dma((ROUNDS + 1, 8)), dma((ROUNDS + 1, 8)),
            dma((ROUNDS,)), dma((ROUNDS,)),
            dma((28,)), dma((28,)),
        ],
        compiler_params=pltpu.CompilerParams(
            collective_id=0, has_side_effects=True, vmem_limit_bytes=60 * 1024 * 1024
        ),
        name="rounds",
    )(round_masks, shots, basis.T)
    iterate_t, ritz = pl.pallas_call(
        functools.partial(finish_kernel, float(nown * nrep * n)),
        out_shape=(jax.ShapeDtypeStruct((k, n), f32), jax.ShapeDtypeStruct((k, k), f32)),
        in_specs=[vmem],
        out_specs=(vmem, vmem),
        name="finish",
    )(both)
    return iterate_t.T, ritz


def solution(mesh):
    in_specs = (P(("owner", "rep"), None), P(("owner", "rep"), None), P())
    out_specs = (P(("owner", "rep"), None), P())
    return jax.shard_map(shards, mesh=mesh, in_specs=in_specs, out_specs=out_specs, check_vma=False)
```

```python
import functools
import math

import jax
import jax.numpy as jnp
from jax import lax
from jax.experimental import pallas as pl
from jax.experimental.pallas import tpu as pltpu
from jax.sharding import PartitionSpec as P

ROUNDS = 3
SHARPNESS = 1.6
MESH = pl.DeviceIdType.MESH
NT = (((1,), (1,)), ((), ()))
TN = (((0,), (0,)), ((), ()))
NX, NY, NZ = 4, 4, 8

ORDER_STAYS = (
    (
        ("G", 1, 1), ("G", 1, -1), ("Z", 1, 0, 1), ("Z", 1, 0, -1), ("F", 1, 1), ("Z", 1, 1, 1), ("Z", 1, 1, -1),
        ("G", 2, 1), ("G", 2, -1), ("F", 0, 3), ("F", 0, 1), ("Q", 1, 1), ("F", 1, 3), ("Z", 2, 0, 1), ("Q", 1, 0),
        ("Z", 2, 0, -1), ("Q", 0, 0), ("Q", 0, 1), ("Z", 2, 1, 1), ("Z", 2, 1, -1), ("G", 3, 1), ("G", 3, -1),
        ("Z", 3, 0, 1), ("Z", 3, 0, -1), ("F", 5, 3), ("F", 5, 1), ("F", 2, 3), ("F", 2, 1), ("Z", 3, 1, 1),
        ("Z", 3, 1, -1), ("G", 4, 1), ("F", 6, 3), ("Z", 4, 0, 1), ("F", 6, 1), ("F", 3, 3), ("F", 3, 1), ("Q", 5, 0),
        ("Q", 5, 1), ("Z", 4, 1, -1), ("Q", 2, 0), ("Q", 2, 1), ("X", 0),
    ),
    (
        ("F", 7, 3), ("F", 7, 1), ("F", 4, 3), ("F", 4, 1), ("Q", 6, 0), ("Q", 6, 1), ("Q", 3, 0), ("Q", 3, 1),
    ),
    (
        ("X", 1),
    ),
    (
        ("Q", 7, 0), ("Q", 7, 1), ("Q", 4, 0), ("Q", 4, 1),
    ),
    (
        ("X", 2),
    ),
)
ORDER_MOVED = (
    (
        ("T",), ("F", 1, 1), ("F", 1, 3), ("O", 0), ("G", 1, 1), ("G", 1, -1), ("F", 0, 3), ("F", 0, 1), ("O", 1),
        ("Q", 1, 1), ("Q", 1, 0), ("Z", 1, 0, 1), ("Z", 1, 0, -1), ("Q", 0, 0), ("Q", 0, 1), ("G", 2, 1),
        ("G", 2, -1), ("Z", 1, 1, 1), ("Z", 1, 1, -1), ("Z", 2, 0, 1), ("Z", 2, 0, -1), ("F", 5, 3), ("F", 5, 1),
        ("G", 3, 1), ("G", 3, -1), ("F", 2, 3), ("F", 2, 1), ("Z", 2, 1, -1), ("Z", 2, 1, 1), ("F", 6, 3),
        ("F", 6, 1), ("Z", 3, 0, -1), ("F", 3, 3), ("F", 3, 1), ("Z", 3, 0, 1), ("G", 4, 1), ("Q", 5, 0), ("Q", 5, 1),
        ("Q", 2, 0), ("Q", 2, 1), ("Z", 3, 1, -1), ("Z", 3, 1, 1), ("X", 0), ("Z", 4, 0, 1), ("F", 7, 3), ("F", 7, 1),
        ("F", 4, 3), ("F", 4, 1), ("Z", 4, 1, -1),
    ),
    (
        ("Q", 6, 0), ("Q", 6, 1), ("Q", 3, 0), ("Q", 3, 1),
    ),
    (
        ("Q", 7, 0), ("X", 1),
    ),
    (
        ("Q", 7, 1), ("Q", 4, 0), ("Q", 4, 1),
    ),
    (
        ("X", 2),
    ),
)


def dot32(a, b, dims):
    return lax.dot_general(a, b, dims, precision=lax.Precision.HIGHEST, preferred_element_type=jnp.float32)


def pack(rows):
    half = rows.shape[0] // 2
    return jnp.concatenate([rows[:half], rows[half:]], axis=1)


def rounds_kernel(
    scale, masks_hbm, shots_hbm, basis_hbm, out,
    masks, shots, basis_t, unit, rowbuf, colbuf, sel0, sel1, own, cands, aff, gpart, gfull, wsend, wrecv, xbufs, ybufs, homeward, ghome, gsend, gback, gx, gy,
    sums,
    s_in, s1, r1, sg, rg, sc, rc, sw, rw, sa, ra,
):
    n, feat = shots.shape
    half, n0 = n // 2, rowbuf.shape[1]
    rs, zs, fin, prod = sums
    n1 = n - n0
    k = basis_t.shape[0]
    o, r = lax.axis_index("owner"), lax.axis_index("rep")
    c, x, yh = o % 2, (o // 2) % NX, o // (2 * NX)
    z, yl = r // 2, r % 2
    y = yh * 2 + yl
    nq = 2 * NX
    q = x * 2 + c

    def dev(y=y, x=x, c=c, z=z):
        return (((y // 2) * NX + x) * 2 + c, z * 2 + y % 2)

    twin_y = yh * 2 + c
    twin = dev(y=twin_y, c=yl)
    other_core = dev(c=1 - c)
    moved = c != yl
    stays = c == yl

    loads = [
        pltpu.make_async_copy(shots_hbm, shots, s_in.at[0]),
        pltpu.make_async_copy(basis_hbm, basis_t, s_in.at[1]),
        pltpu.make_async_copy(masks_hbm, masks, s_in.at[2]),
    ]
    for copy in loads:
        copy.start()

    bar = pltpu.get_barrier_semaphore()

    def hello(device):
        pl.semaphore_signal(bar, inc=1, device_id=device, device_id_type=MESH)

    neighbours = [dev(x=(x + i) % NX) for i in (1, 3)] + [dev(y=(y + i) % NY) for i in (1, 3)]
    neighbours += [dev(z=(z + i) % NZ) for i in (1, 7)]
    for neighbour in neighbours:
        hello(neighbour)

    @pl.when(moved)
    def _():
        hello(twin)

    hello(other_core)

    for copy in loads:
        copy.wait()
    values = shots[...].astype(jnp.float32)
    inv = lax.rsqrt(jnp.mean(values * values, axis=-1, keepdims=True) + 1e-06)
    units = (values * inv).astype(jnp.bfloat16)
    rowbuf[x] = units[:n0]
    colbuf[y] = units[n0:]
    g0 = pack(basis_t[...].T)

    @pl.when(stays)
    def _():
        own[z] = units
        ghome[...] = g0

    @pl.when(moved)
    def _():
        unit[...] = units
        gsend[0] = g0

    pl.semaphore_wait(bar, len(neighbours) + 1 + (c + yl) % 2)

    def send(src, dst, ssem, rsem, device):
        return pltpu.make_async_remote_copy(
            src_ref=src, dst_ref=dst, send_sem=ssem, recv_sem=rsem, device_id=device, device_id_type=MESH
        )

    pending = []

    def all_sent(numbers):
        for number, rows in numbers:
            ref = own.at[0, pl.ds(0, rows)]
            send(ref, ref, s1.at[number], r1.at[number], other_core).wait_send()

    def move(src, dst, number, device):
        send(src, dst, s1.at[number], r1.at[number], device).start()
        pending.append((number, math.prod(src.shape[:-1])))

    def same(ref, number, device):
        move(ref, ref, number, device)

    def landed(ref, number):
        send(ref, ref, s1.at[number], r1.at[number], other_core).wait_recv()

    halves = (pl.ds(0, half), pl.ds(half, half))
    RING, UP, DN, CORE, TRADE = 0, 32, 39, 46, 52

    trade = send(gsend.at[0], ghome, s1.at[TRADE + 2], r1.at[TRADE + 2], twin)

    def leg(number, i):
        if number == 0:
            return rowbuf.at[(x + i) % NX]
        if number == 1:
            return colbuf.at[(y + i) % NY]
        if number < 5:
            return sel0[number - 2].at[(y + i) % NY]
        return sel1[number - 5].at[(x + i) % NX]

    def part_of(number, i, part):
        ref = leg(number, i)
        if number >= 5:
            return ref.at[part]
        first = ref.shape[0] // 32 * 16 + 16
        return ref.at[pl.ds(0, first)] if part == 0 else ref.at[pl.ds(first, ref.shape[0] - first)]

    def step(number, i):
        return dev(x=(x + i) % NX) if number in (0, 5, 6, 7) else dev(y=(y + i) % NY)

    def begin(number):
        same(leg(number, 0), RING + 4 * number, step(number, 1))
        same(leg(number, 0), RING + 4 * number + 1, step(number, 3))

    def on_full(number, k):
        part = 0 if k == 3 else 1
        landed(leg(number, k), RING + 4 * number + part)
        same(part_of(number, k, part), RING + 4 * number + 2 + part, step(number, 4 - k))

    def on_half(number, part):
        landed(part_of(number, 2, part), RING + 4 * number + 2 + part)

    def pick():
        for t in range(ROUNDS):
            m = masks[t]
            sel0[t][y] = rowbuf[x ^ ((m // 2) % 4)]
            for a in range(2):
                sel1[t][x, a] = colbuf[(yh ^ (m // 8)) * 2 + a]
        for number in (2, 5, 3, 6):
            begin(number)

    up, down = dev(z=(z + 1) % NZ), dev(z=(z + NZ - 1) % NZ)

    def z_begin(h):
        same(own.at[z, halves[h]], UP + h, up)
        same(own.at[z, halves[h]], DN + h, down)

    def on_z(s, h, direction):
        ref = own.at[(z + NZ - direction * s) % NZ, halves[h]]
        base = UP if direction == 1 else DN
        landed(ref, base + (2 * (s - 1) + h if s < 4 else 6))
        if s < 3 or (s == 3 and (h == 0) == (direction == 1)):
            same(ref, base + (2 * s + h if s < 3 else 6), up if direction == 1 else down)

    def g_begin():
        gpart[0, z] = ghome[...].astype(jnp.bfloat16)
        for i, device in ((1, up), (7, down)):
            send(gpart.at[0, z], gpart.at[0, z], sg.at[0, i], rg.at[0, i], device).start()

    def on_g(s, direction):
        ref = gpart.at[0, (z + NZ - direction * s) % NZ]
        i = s if direction == 1 else NZ - s
        send(ref, ref, sg.at[0, i], rg.at[0, i], other_core).wait_recv()
        if s < 3 or (s == 3 and direction == 1):
            send(ref, ref, sg.at[0, i + direction], rg.at[0, i + direction], up if direction == 1 else down).start()

    def choose(t):
        m = masks[t]
        for a in range(2):
            cands[t][c, a, :n0] = sel0[t][(yh ^ (m // 8)) * 2 + a]
            cands[t][c, a, n0:] = sel1[t][x ^ ((m // 2) % 4), a]
            number = CORE + 2 * t + a
            same(cands[t].at[c, a], number, other_core)

    def near(j):
        return (NZ + (1 - 2 * ((j + 1) % 2)) * ((j + 1) // 2)) % NZ

    def affinities(t, lo=0, hi=NZ):
        holder = yl ^ (masks[t] % 2)

        @pl.loop(lo, hi)
        def _(j):
            item = (z + near(j)) % NZ
            columns = pl.ds(pl.multiple_of(item * n, n), n)
            for a in range(2):
                scores = lax.dot_general(cands[t][holder, a], own[item], NT, preferred_element_type=jnp.float32)
                aff[t, a, :, columns] = jnp.exp(scores * scale).astype(jnp.bfloat16)

    def gather(order, seen, stays_here):
        def whole(number):
            return all(e in seen for e in (("F", number, 1), ("F", number, 3), ("Q", number, 0), ("Q", number, 1)))

        def z_here(s):
            if s == 0:
                return stays_here or (("O", 0) in seen and ("O", 1) in seen)
            if s == 4:
                return ("Z", 4, 0, 1) in seen and ("Z", 4, 1, -1) in seen
            return all(("Z", s, h, d) in seen for h in (0, 1) for d in (1, -1))

        for event in order:
            kind, *args = event
            seen.add(event)
            if kind == "F":
                on_full(*args)
                number, k = args
                if number in (2, 5) and ("F", number, 4 - k) in seen:
                    begin(number + 2)
            elif kind == "Q":
                on_half(*args)
            elif kind == "Z":
                on_z(*args)
            elif kind == "G":
                on_g(*args)
            elif kind == "O":
                landed(own.at[z, halves[args[0]]], TRADE + args[0])
                z_begin(args[0])
            elif kind == "T":
                trade.wait_recv()
                g_begin()
            else:
                for a in range(2):
                    landed(cands[args[0]].at[1 - c, a], CORE + 2 * args[0] + a)
            if kind in "FQ":
                if "picked" not in seen and whole(0) and whole(1):
                    seen.add("picked")
                    pick()
                for t in range(ROUNDS):
                    if ("chosen", t) not in seen and whole(2 + t) and whole(5 + t):
                        seen.add(("chosen", t))
                        choose(t)
            have = sum(("items", j) in seen for j in range(NZ))
            ready = have
            while ("X", 0) in seen and ready < NZ and z_here((ready + 1) // 2):
                seen.add(("items", ready))
                ready += 1
            if ready > have:
                affinities(0, have, ready)

    seen_stays, seen_moved = set(), set()

    @pl.when(stays)
    def _():
        g_begin()
        z_begin(0)
        z_begin(1)
        begin(0)
        begin(1)
        gather(ORDER_STAYS[0], seen_stays, True)

    sent_if_stays = list(pending)
    pending.clear()

    @pl.when(moved)
    def _():
        trade.start()
        for h in range(2):
            move(unit.at[halves[h]], own.at[z, halves[h]], TRADE + h, twin)
        begin(0)
        begin(1)
        gather(ORDER_MOVED[0], seen_moved, False)

    sent_if_moved = list(pending)
    pending.clear()

    def gather_rest(stage):
        @pl.when(stays)
        def _():
            gather(ORDER_STAYS[stage], seen_stays, True)

        sent_if_stays.extend(pending)
        pending.clear()

        @pl.when(moved)
        def _():
            gather(ORDER_MOVED[stage], seen_moved, False)

        sent_if_moved.extend(pending)
        pending.clear()

    def g_send(t, value):
        gpart[t, z] = value.astype(jnp.bfloat16)

        for i in (3, 5, 4, 2, 6, 1, 7):
            send(gpart.at[t, z], gpart.at[t, z], sg.at[t, i], rg.at[t, i], dev(z=(z + i) % NZ)).start()

    grown = ghome[...]

    def partner(t):
        m = masks[t]
        return y ^ ((m // 8) * 2 + m % 2), x ^ ((m // 2) % 4)

    lane = lax.broadcasted_iota(jnp.int32, (half, 2 * k), 1)
    tail = jnp.where(lane == k, 1.0, 0.0)

    def unpack(t, item):
        p = gpart[t, item].astype(jnp.float32)
        start = pl.multiple_of(item * n, n)
        gfull[pl.ds(start, half), :] = jnp.where(lane < k, p, tail).astype(jnp.bfloat16)
        gfull[pl.ds(start + half, half), :] = jnp.where(lane < k, pltpu.roll(p, k, 1), tail).astype(jnp.bfloat16)

    def carried(t):
        unpack(t, z)

        @pl.loop(1, NZ)
        def _(j):
            i = near(j)
            item = (z + NZ - i) % NZ
            if t > 0:
                ref = gpart.at[t, item]
                send(ref, ref, sg.at[t, i], rg.at[t, i], other_core).wait_recv()
            unpack(t, item)

        wsend[t] = jnp.dot(aff[t, 1 - c], gfull[...], preferred_element_type=jnp.float32)
        copy = send(wsend.at[t], wrecv.at[t], sw.at[t], rw.at[t], other_core)
        copy.start()
        mine = jnp.dot(aff[t, c], gfull[...], preferred_element_type=jnp.float32)
        copy.wait_recv()
        product = mine + wrecv[t]
        return pack(product[:, :k] / product[:, k:k + 1]).astype(jnp.bfloat16)

    def x_send(ref, sems, t, base):
        for i in (2, 1, 3):
            send(ref, ref, sems[0].at[t, base + i], sems[1].at[t, base + i], dev(x=(x + i) % NX)).start()

    def x_wait(buf, sems, t, base):
        for i in range(1, NX):
            ref = buf.at[(x + NX - i) % NX]
            send(ref, ref, sems[0].at[t, base + i], sems[1].at[t, base + i], other_core).wait_recv()

    def y_send(ref, sems, t, base):
        for i in (2, 1, 3):
            send(ref, ref, sems[0].at[t, base + i], sems[1].at[t, base + i], dev(y=(y + i) % NY)).start()

    def y_wait(buf, sems, t, base):
        for i in range(1, NY):
            ref = buf.at[(y + NY - i) % NY]
            send(ref, ref, sems[0].at[t, base + i], sems[1].at[t, base + i], other_core).wait_recv()

    csem = (sc, rc)
    for t in range(ROUNDS - 1):
        if t > 0:
            g_send(t, grown)
            gather_rest(3)
        py, px = partner(t)
        xbufs[t][x] = carried(t)
        x_send(xbufs[t].at[x], csem, t, 0)
        if t == 0:
            gather_rest(1)
        else:
            gather_rest(4)
            affinities(2)
        x_wait(xbufs[t], csem, t, 0)
        ybufs[t][y] = xbufs[t][px]
        y_send(ybufs[t].at[y], csem, t, 4)
        if t == 0:
            gather_rest(2)
            affinities(1)
        y_wait(ybufs[t], csem, t, 4)
        grown = grown + ybufs[t][py].astype(jnp.float32)

    t = ROUNDS - 1
    py, px = partner(t)
    g_send(t, grown)
    gx[x] = grown
    x_send(gx.at[x], csem, ROUNDS, 0)

    @pl.when(stays)
    def _():
        gback[...] = grown

    @pl.when(moved)
    def _():
        gsend[1] = grown
        send(gsend.at[1], gback, s1.at[TRADE + 3], r1.at[TRADE + 3], twin).start()

    x_wait(gx, csem, ROUNDS, 0)
    gy[y] = gx[px]
    y_send(gy.at[y], csem, ROUNDS, 4)
    came = carried(t)
    xbufs[t][x] = came
    x_send(xbufs[t].at[x], csem, t, 0)
    y_wait(gy, csem, ROUNDS, 4)
    before = gy[py]
    after = before + came.astype(jnp.float32)

    top = jnp.where(lane < k, before, pltpu.roll(after, k, 1))
    bottom = jnp.where(lane < k, pltpu.roll(before, k, 1), after)
    prod[...] = (dot32(top, top, TN) + dot32(bottom, bottom, TN)).reshape(prod.shape)

    def total(ref, count):
        value = ref[0]
        for i in range(1, count):
            value = value + ref[i]
        return value

    group = 2 * NX * 2
    place = q * 2 + yl
    line = (z * 2 + yh) % group

    def near_dev(i):
        there = (place + i) % group
        return there, dev(y=yh * 2 + there % 2, x=there // 4, c=there // 2 % 2)

    def far_dev(i):
        there = (line + i) % group
        return dev(y=there % 2 * 2 + yl, z=there // 2)

    for i in range(1, group):
        there, device = near_dev(i)
        send(prod.at[there], rs.at[place], sa.at[i], ra.at[i], device).start()
    rs[place] = prod[place]

    x_wait(xbufs[t], csem, t, 0)
    homeward[...] = xbufs[t][px]

    @pl.when(stays)
    def _():
        ybufs[t][y] = homeward[...]

    def home_copy(i):
        ty = (y + i) % NY
        device = dev(y=(ty // 2) * 2 + c, c=ty % 2)
        return send(homeward, ybufs[t].at[y], sc.at[t, 4 + i], rc.at[t, 4 + i], device)

    @pl.when(moved)
    def _():
        home_copy(0).start()

    for i in range(1, NY):
        home_copy(i).start()

    for i in range(1, group):
        send(prod.at[0], rs.at[(place + group - i) % group], sa.at[i], ra.at[i], other_core).wait_recv()
    zs[line] = total(rs, group)

    for i in (8, 7, 9, 6, 10, 5, 11, 4, 12, 3, 13, 2, 14, 1, 15):
        ref = zs.at[line]
        send(ref, ref, sa.at[group + i], ra.at[group + i], far_dev(i)).start()
    for i in range(1, group):
        ref = zs.at[(line + group - i) % group]
        send(ref, ref, sa.at[group + i], ra.at[group + i], other_core).wait_recv()
    fin[place] = total(zs, group)

    for i in range(1, group):
        ref = fin.at[place]
        send(ref, ref, sa.at[2 * group + i], ra.at[2 * group + i], near_dev(i)[1]).start()

    @pl.when(moved)
    def _():
        send(gsend.at[1], gback, s1.at[TRADE + 3], r1.at[TRADE + 3], twin).wait_recv()
        ref = ybufs[t].at[twin_y]
        send(ref, ref, sc.at[t, 4], rc.at[t, 4], other_core).wait_recv()

    for i in range(1, NY):
        ref = ybufs[t].at[(twin_y + NY - i) % NY]
        send(ref, ref, sc.at[t, 4 + i], rc.at[t, 4 + i], other_core).wait_recv()
    m = masks[t]
    out[:half, :] = gback[...] + ybufs[t][twin_y ^ ((m // 8) * 2 + m % 2)].astype(jnp.float32)

    for i in range(1, group):
        ref = fin.at[(place + group - i) % group]
        send(ref, ref, sa.at[2 * group + i], ra.at[2 * group + i], other_core).wait_recv()

    out[half:, :] = fin[...].reshape(2 * k, 2 * k)

    assert not pending

    @pl.when(stays)
    def _():
        all_sent(sent_if_stays)

    @pl.when(moved)
    def _():
        all_sent(sent_if_moved)
        trade.wait_send()
        send(gsend.at[1], gback, s1.at[TRADE + 3], r1.at[TRADE + 3], twin).wait_send()
        home_copy(0).wait_send()

    @pl.loop(1, NX)
    def _(i):
        for row in range(ROUNDS):
            ref = xbufs[row].at[x]
            send(ref, ref, sc.at[row, i], rc.at[row, i], other_core).wait_send()
            send(ref, ref, sc.at[row, 4 + i], rc.at[row, 4 + i], other_core).wait_send()
        ref = gx.at[x]
        send(ref, ref, sc.at[ROUNDS, i], rc.at[ROUNDS, i], other_core).wait_send()
        send(ref, ref, sc.at[ROUNDS, 4 + i], rc.at[ROUNDS, 4 + i], other_core).wait_send()

    @pl.loop(1, NZ)
    def _(i):
        for row in range(ROUNDS):
            ref = gpart.at[row, z]
            send(ref, ref, sg.at[row, i], rg.at[row, i], other_core).wait_send()

    @pl.loop(1, group)
    def _(i):
        for base in range(3):
            ref = fin.at[place]
            send(ref, ref, sa.at[base * group + i], ra.at[base * group + i], other_core).wait_send()

    for row in range(ROUNDS):
        send(wsend.at[row], wrecv.at[row], sw.at[row], rw.at[row], other_core).wait_send()


def inverse_factors(grams):
    k = grams[0].shape[0]
    row = lax.broadcasted_iota(jnp.int32, (k, 2 * k), 0)
    lane = lax.broadcasted_iota(jnp.int32, (k, 2 * k), 1)
    identity = jnp.where(lane == row, 1.0, 0.0)[:, :k]
    works = [jnp.concatenate([gram, identity], axis=1) for gram in grams]
    works = [[work[8 * g:8 * g + 8] for g in range(k // 8)] for work in works]
    below = lax.broadcasted_iota(jnp.int32, (8, 1), 0)
    for i in range(k - 1):
        own, s = i // 8, i % 8
        for work in works:
            pivot = work[own][s:s + 1, :] * (1.0 / work[own][s:s + 1, i:i + 1])
            for g in range(own, k // 8):
                factor = work[g][:, i:i + 1]
                if g == own:
                    factor = jnp.where(below > s, factor, 0.0)
                work[g] = work[g] - factor * pivot
    results = []
    for work in works:
        whole = jnp.concatenate(work, axis=0)
        diagonal = jnp.sum(jnp.where(lane == row, whole, 0.0), axis=1, keepdims=True)
        results.append(whole[:, k:] * (1.0 / jnp.sqrt(diagonal)))
    return results


def finish_kernel(total_rows, both, iterate_t, ritz):
    k = ritz.shape[0]
    half = both.shape[0] - 2 * k
    every = both[half:, :] * (1.0 / total_rows)
    inv_before, inv_last = inverse_factors([every[:k, :k], every[k:, k:]])
    packed = both[:half, :]
    iterate_t[:, :half] = dot32(inv_last, packed[:, :k], NT)
    iterate_t[:, half:] = dot32(inv_last, packed[:, k:], NT)
    left = dot32(inv_before, every[:k, k:], (((1,), (0,)), ((), ())))
    ritz[...] = dot32(left, inv_before, NT)


def shards(shots, basis, round_masks):
    n, feat = shots.shape
    k = basis.shape[1]
    nrep, nown = lax.axis_size("rep"), lax.axis_size("owner")
    half, n0 = n // 2, n * 11 // 16
    bf, f32 = jnp.bfloat16, jnp.float32
    vmem = pl.BlockSpec(memory_space=pltpu.VMEM)
    slab = (2 * k) // 16
    dma = pltpu.SemaphoreType.DMA
    both = pl.pallas_call(
        functools.partial(rounds_kernel, SHARPNESS / math.sqrt(feat)),
        out_shape=jax.ShapeDtypeStruct((half + 2 * k, 2 * k), f32),
        in_specs=[pl.BlockSpec(memory_space=pltpu.HBM)] * 3,
        out_specs=vmem,
        scratch_shapes=[
            pltpu.SMEM((ROUNDS,), jnp.int32),
            pltpu.VMEM((n, feat), bf),
            pltpu.VMEM((k, n), f32),
            pltpu.VMEM((n, feat), bf),
            pltpu.VMEM((NX, n0, feat), bf),
            pltpu.VMEM((NY, n - n0, feat), bf),
            [pltpu.VMEM((NY, n0, feat), bf)] * ROUNDS,
            [pltpu.VMEM((NX, 2, n - n0, feat), bf)] * ROUNDS,
            pltpu.VMEM((NZ, n, feat), bf),
            [pltpu.VMEM((2, 2, n, feat), bf)] * ROUNDS,
            pltpu.VMEM((ROUNDS, 2, n, NZ * n), bf),
            pltpu.VMEM((ROUNDS, NZ, half, 2 * k), bf),
            pltpu.VMEM((NZ * n, 2 * k), bf),
            pltpu.VMEM((ROUNDS, n, 2 * k), f32),
            pltpu.VMEM((ROUNDS, n, 2 * k), f32),
            [pltpu.VMEM((NX, half, 2 * k), bf)] * ROUNDS,
            [pltpu.VMEM((NY, half, 2 * k), bf)] * ROUNDS,
            pltpu.VMEM((half, 2 * k), bf),
            pltpu.VMEM((half, 2 * k), f32),
            pltpu.VMEM((2, half, 2 * k), f32),
            pltpu.VMEM((half, 2 * k), f32),
            pltpu.VMEM((NX, half, 2 * k), f32),
            pltpu.VMEM((NY, half, 2 * k), f32),
            [pltpu.VMEM((16, slab, 2 * k), f32)] * 4,
            dma((3,)),
            dma((56,)), dma((56,)),
            dma((ROUNDS, NZ)), dma((ROUNDS, NZ)),
            dma((ROUNDS + 1, 8)), dma((ROUNDS + 1, 8)),
            dma((ROUNDS,)), dma((ROUNDS,)),
            dma((48,)), dma((48,)),
        ],
        compiler_params=pltpu.CompilerParams(
            collective_id=0, has_side_effects=True, vmem_limit_bytes=60 * 1024 * 1024
        ),
        name="rounds",
    )(round_masks, shots, basis.T)
    iterate_t, ritz = pl.pallas_call(
        functools.partial(finish_kernel, float(nown * nrep * n)),
        out_shape=(jax.ShapeDtypeStruct((k, n), f32), jax.ShapeDtypeStruct((k, k), f32)),
        in_specs=[vmem],
        out_specs=(vmem, vmem),
        name="finish",
    )(both)
    return iterate_t.T, ritz


def solution(mesh):
    in_specs = (P(("owner", "rep"), None), P(("owner", "rep"), None), P())
    out_specs = (P(("owner", "rep"), None), P())
    return jax.shard_map(shards, mesh=mesh, in_specs=in_specs, out_specs=out_specs, check_vma=False)
```

```python
import functools
import math

import jax
import jax.numpy as jnp
from jax import lax
from jax.experimental import pallas as pl
from jax.experimental.pallas import tpu as pltpu
from jax.sharding import PartitionSpec as P

ROUNDS = 3
SHARPNESS = 1.6
MESH = pl.DeviceIdType.MESH
NT = (((1,), (1,)), ((), ()))
TN = (((0,), (0,)), ((), ()))
NX, NY, NZ = 4, 4, 8

ORDER_STAYS = (
    (
        ("G", 1, 1), ("G", 1, -1), ("Z", 1, 0, 1), ("Z", 1, 0, -1), ("F", 1, 1), ("Z", 1, 1, 1), ("Z", 1, 1, -1),
        ("G", 2, 1), ("G", 2, -1), ("F", 0, 3), ("F", 0, 1), ("Q", 1, 1), ("F", 1, 3), ("Z", 2, 0, 1), ("Q", 1, 0),
        ("Z", 2, 0, -1), ("Q", 0, 0), ("Q", 0, 1), ("Z", 2, 1, 1), ("Z", 2, 1, -1), ("G", 3, 1), ("G", 3, -1),
        ("Z", 3, 0, 1), ("Z", 3, 0, -1), ("F", 5, 3), ("F", 5, 1), ("F", 2, 3), ("F", 2, 1), ("Z", 3, 1, 1),
        ("Z", 3, 1, -1), ("G", 4, 1), ("F", 6, 3), ("Z", 4, 0, 1), ("F", 6, 1), ("F", 3, 3), ("F", 3, 1), ("Q", 5, 0),
        ("Q", 5, 1), ("Z", 4, 1, -1), ("Q", 2, 0), ("Q", 2, 1), ("X", 0),
    ),
    (
        ("F", 7, 3), ("F", 7, 1), ("F", 4, 3), ("F", 4, 1), ("Q", 6, 0), ("Q", 6, 1), ("Q", 3, 0), ("Q", 3, 1),
    ),
    (
        ("X", 1),
    ),
    (
        ("Q", 7, 0), ("Q", 7, 1), ("Q", 4, 0), ("Q", 4, 1),
    ),
    (
        ("X", 2),
    ),
)
ORDER_MOVED = (
    (
        ("T",), ("F", 1, 1), ("F", 1, 3), ("O", 0), ("G", 1, 1), ("G", 1, -1), ("F", 0, 3), ("F", 0, 1), ("O", 1),
        ("Q", 1, 1), ("Q", 1, 0), ("Z", 1, 0, 1), ("Z", 1, 0, -1), ("Q", 0, 0), ("Q", 0, 1), ("G", 2, 1),
        ("G", 2, -1), ("Z", 1, 1, 1), ("Z", 1, 1, -1), ("Z", 2, 0, 1), ("Z", 2, 0, -1), ("F", 5, 3), ("F", 5, 1),
        ("G", 3, 1), ("G", 3, -1), ("F", 2, 3), ("F", 2, 1), ("Z", 2, 1, -1), ("Z", 2, 1, 1), ("F", 6, 3),
        ("F", 6, 1), ("Z", 3, 0, -1), ("F", 3, 3), ("F", 3, 1), ("Z", 3, 0, 1), ("G", 4, 1), ("Q", 5, 0), ("Q", 5, 1),
        ("Q", 2, 0), ("Q", 2, 1), ("Z", 3, 1, -1), ("Z", 3, 1, 1), ("X", 0), ("Z", 4, 0, 1), ("F", 7, 3), ("F", 7, 1),
        ("F", 4, 3), ("F", 4, 1), ("Z", 4, 1, -1),
    ),
    (
        ("Q", 6, 0), ("Q", 6, 1), ("Q", 3, 0), ("Q", 3, 1),
    ),
    (
        ("Q", 7, 0), ("X", 1),
    ),
    (
        ("Q", 7, 1), ("Q", 4, 0), ("Q", 4, 1),
    ),
    (
        ("X", 2),
    ),
)


def dot32(a, b, dims):
    return lax.dot_general(a, b, dims, precision=lax.Precision.HIGHEST, preferred_element_type=jnp.float32)


def pack(rows):
    half = rows.shape[0] // 2
    return jnp.concatenate([rows[:half], rows[half:]], axis=1)


def rounds_kernel(
    scale, masks_hbm, shots_hbm, basis_hbm, rows_out, sums_out,
    masks, shots, basis_t, unit, rowbuf, colbuf, sel0, sel1, own, cands, aff, gpart, gfull, wsend, wrecv, xbufs, ybufs, homeward, ghome, gsend, gback, gx, gy,
    sums, result,
    s_in, s1, r1, sg, rg, sc, rc, sw, rw, sa, ra,
):
    n, feat = shots.shape
    half, n0 = n // 2, rowbuf.shape[1]
    rs, zs, fin, prod = sums
    n1 = n - n0
    k = basis_t.shape[0]
    o, r = lax.axis_index("owner"), lax.axis_index("rep")
    c, x, yh = o % 2, (o // 2) % NX, o // (2 * NX)
    z, yl = r // 2, r % 2
    y = yh * 2 + yl
    nq = 2 * NX
    q = x * 2 + c

    def dev(y=y, x=x, c=c, z=z):
        return (((y // 2) * NX + x) * 2 + c, z * 2 + y % 2)

    twin_y = yh * 2 + c
    twin = dev(y=twin_y, c=yl)
    other_core = dev(c=1 - c)
    moved = c != yl
    stays = c == yl

    loads = [
        pltpu.make_async_copy(shots_hbm, shots, s_in.at[0]),
        pltpu.make_async_copy(basis_hbm, basis_t, s_in.at[1]),
        pltpu.make_async_copy(masks_hbm, masks, s_in.at[2]),
    ]
    for copy in loads:
        copy.start()

    bar = pltpu.get_barrier_semaphore()

    def hello(device):
        pl.semaphore_signal(bar, inc=1, device_id=device, device_id_type=MESH)

    neighbours = [dev(x=(x + i) % NX) for i in (1, 3)] + [dev(y=(y + i) % NY) for i in (1, 3)]
    neighbours += [dev(z=(z + i) % NZ) for i in (1, 7)]
    for neighbour in neighbours:
        hello(neighbour)

    @pl.when(moved)
    def _():
        hello(twin)

    hello(other_core)

    for copy in loads:
        copy.wait()
    values = shots[...].astype(jnp.float32)
    inv = lax.rsqrt(jnp.mean(values * values, axis=-1, keepdims=True) + 1e-06)
    units = (values * inv).astype(jnp.bfloat16)
    rowbuf[x] = units[:n0]
    colbuf[y] = units[n0:]
    g0 = pack(basis_t[...].T)

    @pl.when(stays)
    def _():
        own[z] = units
        ghome[...] = g0

    @pl.when(moved)
    def _():
        unit[...] = units
        gsend[0] = g0

    pl.semaphore_wait(bar, len(neighbours) + 1 + (c + yl) % 2)

    def send(src, dst, ssem, rsem, device):
        return pltpu.make_async_remote_copy(
            src_ref=src, dst_ref=dst, send_sem=ssem, recv_sem=rsem, device_id=device, device_id_type=MESH
        )

    pending = []

    def all_sent(numbers):
        for number, rows in numbers:
            ref = own.at[0, pl.ds(0, rows)]
            send(ref, ref, s1.at[number], r1.at[number], other_core).wait_send()

    def move(src, dst, number, device):
        send(src, dst, s1.at[number], r1.at[number], device).start()
        pending.append((number, math.prod(src.shape[:-1])))

    def same(ref, number, device):
        move(ref, ref, number, device)

    def landed(ref, number):
        send(ref, ref, s1.at[number], r1.at[number], other_core).wait_recv()

    halves = (pl.ds(0, half), pl.ds(half, half))
    RING, UP, DN, CORE, TRADE = 0, 32, 39, 46, 52

    trade = send(gsend.at[0], ghome, s1.at[TRADE + 2], r1.at[TRADE + 2], twin)

    def leg(number, i):
        if number == 0:
            return rowbuf.at[(x + i) % NX]
        if number == 1:
            return colbuf.at[(y + i) % NY]
        if number < 5:
            return sel0[number - 2].at[(y + i) % NY]
        return sel1[number - 5].at[(x + i) % NX]

    def part_of(number, i, part):
        ref = leg(number, i)
        if number >= 5:
            return ref.at[part]
        first = ref.shape[0] // 32 * 16 + 16
        return ref.at[pl.ds(0, first)] if part == 0 else ref.at[pl.ds(first, ref.shape[0] - first)]

    def step(number, i):
        return dev(x=(x + i) % NX) if number in (0, 5, 6, 7) else dev(y=(y + i) % NY)

    def begin(number):
        same(leg(number, 0), RING + 4 * number, step(number, 1))
        same(leg(number, 0), RING + 4 * number + 1, step(number, 3))

    def on_full(number, k):
        part = 0 if k == 3 else 1
        landed(leg(number, k), RING + 4 * number + part)
        same(part_of(number, k, part), RING + 4 * number + 2 + part, step(number, 4 - k))

    def on_half(number, part):
        landed(part_of(number, 2, part), RING + 4 * number + 2 + part)

    def pick():
        for t in range(ROUNDS):
            m = masks[t]
            sel0[t][y] = rowbuf[x ^ ((m // 2) % 4)]
            for a in range(2):
                sel1[t][x, a] = colbuf[(yh ^ (m // 8)) * 2 + a]
        for number in (2, 5, 3, 6):
            begin(number)

    up, down = dev(z=(z + 1) % NZ), dev(z=(z + NZ - 1) % NZ)

    def z_begin(h):
        same(own.at[z, halves[h]], UP + h, up)
        same(own.at[z, halves[h]], DN + h, down)

    def on_z(s, h, direction):
        ref = own.at[(z + NZ - direction * s) % NZ, halves[h]]
        base = UP if direction == 1 else DN
        landed(ref, base + (2 * (s - 1) + h if s < 4 else 6))
        if s < 3 or (s == 3 and (h == 0) == (direction == 1)):
            same(ref, base + (2 * s + h if s < 3 else 6), up if direction == 1 else down)

    def g_begin():
        gpart[0, z] = ghome[...].astype(jnp.bfloat16)
        for i, device in ((1, up), (7, down)):
            send(gpart.at[0, z], gpart.at[0, z], sg.at[0, i], rg.at[0, i], device).start()

    def on_g(s, direction):
        ref = gpart.at[0, (z + NZ - direction * s) % NZ]
        i = s if direction == 1 else NZ - s
        send(ref, ref, sg.at[0, i], rg.at[0, i], other_core).wait_recv()
        if s < 3 or (s == 3 and direction == 1):
            send(ref, ref, sg.at[0, i + direction], rg.at[0, i + direction], up if direction == 1 else down).start()

    def choose(t):
        m = masks[t]
        for a in range(2):
            cands[t][c, a, :n0] = sel0[t][(yh ^ (m // 8)) * 2 + a]
            cands[t][c, a, n0:] = sel1[t][x ^ ((m // 2) % 4), a]
            number = CORE + 2 * t + a
            same(cands[t].at[c, a], number, other_core)

    def near(j):
        return (NZ + (1 - 2 * ((j + 1) % 2)) * ((j + 1) // 2)) % NZ

    def affinities(t, lo=0, hi=NZ):
        holder = yl ^ (masks[t] % 2)

        @pl.loop(lo, hi)
        def _(j):
            item = (z + near(j)) % NZ
            columns = pl.ds(pl.multiple_of(item * n, n), n)
            for a in range(2):
                scores = lax.dot_general(cands[t][holder, a], own[item], NT, preferred_element_type=jnp.float32)
                aff[t, a, :, columns] = jnp.exp(scores * scale).astype(jnp.bfloat16)

    def gather(order, seen, stays_here):
        def whole(number):
            return all(e in seen for e in (("F", number, 1), ("F", number, 3), ("Q", number, 0), ("Q", number, 1)))

        def z_here(s):
            if s == 0:
                return stays_here or (("O", 0) in seen and ("O", 1) in seen)
            if s == 4:
                return ("Z", 4, 0, 1) in seen and ("Z", 4, 1, -1) in seen
            return all(("Z", s, h, d) in seen for h in (0, 1) for d in (1, -1))

        for event in order:
            kind, *args = event
            seen.add(event)
            if kind == "F":
                on_full(*args)
                number, k = args
                if number in (2, 5) and ("F", number, 4 - k) in seen:
                    begin(number + 2)
            elif kind == "Q":
                on_half(*args)
            elif kind == "Z":
                on_z(*args)
            elif kind == "G":
                on_g(*args)
            elif kind == "O":
                landed(own.at[z, halves[args[0]]], TRADE + args[0])
                z_begin(args[0])
            elif kind == "T":
                trade.wait_recv()
                g_begin()
            else:
                for a in range(2):
                    landed(cands[args[0]].at[1 - c, a], CORE + 2 * args[0] + a)
            if kind in "FQ":
                if "picked" not in seen and whole(0) and whole(1):
                    seen.add("picked")
                    pick()
                for t in range(ROUNDS):
                    if ("chosen", t) not in seen and whole(2 + t) and whole(5 + t):
                        seen.add(("chosen", t))
                        choose(t)
            have = sum(("items", j) in seen for j in range(NZ))
            ready = have
            while ("X", 0) in seen and ready < NZ and z_here((ready + 1) // 2):
                seen.add(("items", ready))
                ready += 1
            if ready > have:
                affinities(0, have, ready)

    seen_stays, seen_moved = set(), set()

    @pl.when(stays)
    def _():
        g_begin()
        z_begin(0)
        z_begin(1)
        begin(0)
        begin(1)
        gather(ORDER_STAYS[0], seen_stays, True)

    sent_if_stays = list(pending)
    pending.clear()

    @pl.when(moved)
    def _():
        trade.start()
        for h in range(2):
            move(unit.at[halves[h]], own.at[z, halves[h]], TRADE + h, twin)
        begin(0)
        begin(1)
        gather(ORDER_MOVED[0], seen_moved, False)

    sent_if_moved = list(pending)
    pending.clear()

    def gather_rest(stage):
        @pl.when(stays)
        def _():
            gather(ORDER_STAYS[stage], seen_stays, True)

        sent_if_stays.extend(pending)
        pending.clear()

        @pl.when(moved)
        def _():
            gather(ORDER_MOVED[stage], seen_moved, False)

        sent_if_moved.extend(pending)
        pending.clear()

    def g_send(t, value):
        gpart[t, z] = value.astype(jnp.bfloat16)

        for i in (3, 5, 4, 2, 6, 1, 7):
            send(gpart.at[t, z], gpart.at[t, z], sg.at[t, i], rg.at[t, i], dev(z=(z + i) % NZ)).start()

    grown = ghome[...]

    def partner(t):
        m = masks[t]
        return y ^ ((m // 8) * 2 + m % 2), x ^ ((m // 2) % 4)

    lane = lax.broadcasted_iota(jnp.int32, (half, 2 * k), 1)
    tail = jnp.where(lane == k, 1.0, 0.0)

    def unpack(t, item):
        p = gpart[t, item].astype(jnp.float32)
        start = pl.multiple_of(item * n, n)
        gfull[pl.ds(start, half), :] = jnp.where(lane < k, p, tail).astype(jnp.bfloat16)
        gfull[pl.ds(start + half, half), :] = jnp.where(lane < k, pltpu.roll(p, k, 1), tail).astype(jnp.bfloat16)

    def carried(t):
        unpack(t, z)

        @pl.loop(1, NZ)
        def _(j):
            i = near(j)
            item = (z + NZ - i) % NZ
            if t > 0:
                ref = gpart.at[t, item]
                send(ref, ref, sg.at[t, i], rg.at[t, i], other_core).wait_recv()
            unpack(t, item)

        wsend[t] = jnp.dot(aff[t, 1 - c], gfull[...], preferred_element_type=jnp.float32)
        copy = send(wsend.at[t], wrecv.at[t], sw.at[t], rw.at[t], other_core)
        copy.start()
        mine = jnp.dot(aff[t, c], gfull[...], preferred_element_type=jnp.float32)
        copy.wait_recv()
        product = mine + wrecv[t]
        return pack(product[:, :k] / product[:, k:k + 1]).astype(jnp.bfloat16)

    def x_send(ref, sems, t, base):
        for i in (2, 1, 3):
            send(ref, ref, sems[0].at[t, base + i], sems[1].at[t, base + i], dev(x=(x + i) % NX)).start()

    def x_wait(buf, sems, t, base):
        for i in range(1, NX):
            ref = buf.at[(x + NX - i) % NX]
            send(ref, ref, sems[0].at[t, base + i], sems[1].at[t, base + i], other_core).wait_recv()

    def y_send(ref, sems, t, base):
        for i in (2, 1, 3):
            send(ref, ref, sems[0].at[t, base + i], sems[1].at[t, base + i], dev(y=(y + i) % NY)).start()

    def y_wait(buf, sems, t, base):
        for i in range(1, NY):
            ref = buf.at[(y + NY - i) % NY]
            send(ref, ref, sems[0].at[t, base + i], sems[1].at[t, base + i], other_core).wait_recv()

    csem = (sc, rc)
    for t in range(ROUNDS - 1):
        if t > 0:
            g_send(t, grown)
            gather_rest(3)
        py, px = partner(t)
        xbufs[t][x] = carried(t)
        x_send(xbufs[t].at[x], csem, t, 0)
        if t == 0:
            gather_rest(1)
        else:
            gather_rest(4)
            affinities(2)
        x_wait(xbufs[t], csem, t, 0)
        ybufs[t][y] = xbufs[t][px]
        y_send(ybufs[t].at[y], csem, t, 4)
        if t == 0:
            gather_rest(2)
            affinities(1)
        y_wait(ybufs[t], csem, t, 4)
        grown = grown + ybufs[t][py].astype(jnp.float32)

    t = ROUNDS - 1
    py, px = partner(t)
    g_send(t, grown)
    gx[x] = grown
    x_send(gx.at[x], csem, ROUNDS, 0)

    @pl.when(stays)
    def _():
        gback[...] = grown

    @pl.when(moved)
    def _():
        gsend[1] = grown
        send(gsend.at[1], gback, s1.at[TRADE + 3], r1.at[TRADE + 3], twin).start()

    x_wait(gx, csem, ROUNDS, 0)
    gy[y] = gx[px]
    y_send(gy.at[y], csem, ROUNDS, 4)
    came = carried(t)
    xbufs[t][x] = came
    x_send(xbufs[t].at[x], csem, t, 0)
    y_wait(gy, csem, ROUNDS, 4)
    before = gy[py]
    after = before + came.astype(jnp.float32)

    top = jnp.where(lane < k, before, pltpu.roll(after, k, 1))
    bottom = jnp.where(lane < k, pltpu.roll(before, k, 1), after)
    prod[...] = (dot32(top, top, TN) + dot32(bottom, bottom, TN)).reshape(prod.shape)

    def total(ref, count):
        value = ref[0]
        for i in range(1, count):
            value = value + ref[i]
        return value

    group = 2 * NX * 2
    place = q * 2 + yl
    line = (z * 2 + yh) % group

    def near_dev(i):
        there = (place + i) % group
        return there, dev(y=yh * 2 + there % 2, x=there // 4, c=there // 2 % 2)

    def far_dev(i):
        there = (line + i) % group
        return dev(y=there % 2 * 2 + yl, z=there // 2)

    for i in range(1, group):
        there, device = near_dev(i)
        send(prod.at[there], rs.at[place], sa.at[i], ra.at[i], device).start()
    rs[place] = prod[place]

    x_wait(xbufs[t], csem, t, 0)
    homeward[...] = xbufs[t][px]

    @pl.when(stays)
    def _():
        ybufs[t][y] = homeward[...]

    def home_copy(i):
        ty = (y + i) % NY
        device = dev(y=(ty // 2) * 2 + c, c=ty % 2)
        return send(homeward, ybufs[t].at[y], sc.at[t, 4 + i], rc.at[t, 4 + i], device)

    @pl.when(moved)
    def _():
        home_copy(0).start()

    for i in range(1, NY):
        home_copy(i).start()

    for i in range(1, group):
        send(prod.at[0], rs.at[(place + group - i) % group], sa.at[i], ra.at[i], other_core).wait_recv()
    zs[line] = total(rs, group)

    for i in (8, 7, 9, 6, 10, 5, 11, 4, 12, 3, 13, 2, 14, 1, 15):
        ref = zs.at[line]
        send(ref, ref, sa.at[group + i], ra.at[group + i], far_dev(i)).start()
    for i in range(1, group):
        ref = zs.at[(line + group - i) % group]
        send(ref, ref, sa.at[group + i], ra.at[group + i], other_core).wait_recv()
    fin[place] = total(zs, group)

    for i in range(1, group):
        ref = fin.at[place]
        send(ref, ref, sa.at[2 * group + i], ra.at[2 * group + i], near_dev(i)[1]).start()

    @pl.when(moved)
    def _():
        send(gsend.at[1], gback, s1.at[TRADE + 3], r1.at[TRADE + 3], twin).wait_recv()
        ref = ybufs[t].at[twin_y]
        send(ref, ref, sc.at[t, 4], rc.at[t, 4], other_core).wait_recv()

    for i in range(1, NY):
        ref = ybufs[t].at[(twin_y + NY - i) % NY]
        send(ref, ref, sc.at[t, 4 + i], rc.at[t, 4 + i], other_core).wait_recv()
    m = masks[t]
    result[...] = gback[...] + ybufs[t][twin_y ^ ((m // 8) * 2 + m % 2)].astype(jnp.float32)
    rows_copy = pltpu.make_async_copy(result, rows_out, s_in.at[3])
    rows_copy.start()

    for i in range(1, group):
        ref = fin.at[(place + group - i) % group]
        send(ref, ref, sa.at[2 * group + i], ra.at[2 * group + i], other_core).wait_recv()

    sums_copy = pltpu.make_async_copy(fin, sums_out, s_in.at[4])
    sums_copy.start()

    assert not pending

    @pl.when(stays)
    def _():
        all_sent(sent_if_stays)

    @pl.when(moved)
    def _():
        all_sent(sent_if_moved)
        trade.wait_send()
        send(gsend.at[1], gback, s1.at[TRADE + 3], r1.at[TRADE + 3], twin).wait_send()
        home_copy(0).wait_send()

    @pl.loop(1, NX)
    def _(i):
        for row in range(ROUNDS):
            ref = xbufs[row].at[x]
            send(ref, ref, sc.at[row, i], rc.at[row, i], other_core).wait_send()
            send(ref, ref, sc.at[row, 4 + i], rc.at[row, 4 + i], other_core).wait_send()
        ref = gx.at[x]
        send(ref, ref, sc.at[ROUNDS, i], rc.at[ROUNDS, i], other_core).wait_send()
        send(ref, ref, sc.at[ROUNDS, 4 + i], rc.at[ROUNDS, 4 + i], other_core).wait_send()

    @pl.loop(1, NZ)
    def _(i):
        for row in range(ROUNDS):
            ref = gpart.at[row, z]
            send(ref, ref, sg.at[row, i], rg.at[row, i], other_core).wait_send()

    @pl.loop(1, group)
    def _(i):
        for base in range(3):
            ref = fin.at[place]
            send(ref, ref, sa.at[base * group + i], ra.at[base * group + i], other_core).wait_send()

    for row in range(ROUNDS):
        send(wsend.at[row], wrecv.at[row], sw.at[row], rw.at[row], other_core).wait_send()
    rows_copy.wait()
    sums_copy.wait()


def inverse_factors(grams):
    k = grams[0].shape[0]
    row = lax.broadcasted_iota(jnp.int32, (k, 2 * k), 0)
    lane = lax.broadcasted_iota(jnp.int32, (k, 2 * k), 1)
    identity = jnp.where(lane == row, 1.0, 0.0)[:, :k]
    works = [jnp.concatenate([gram, identity], axis=1) for gram in grams]
    works = [[work[8 * g:8 * g + 8] for g in range(k // 8)] for work in works]
    below = lax.broadcasted_iota(jnp.int32, (8, 1), 0)
    for i in range(k - 1):
        own, s = i // 8, i % 8
        for work in works:
            pivot = work[own][s:s + 1, :] * (1.0 / work[own][s:s + 1, i:i + 1])
            for g in range(own, k // 8):
                factor = work[g][:, i:i + 1]
                if g == own:
                    factor = jnp.where(below > s, factor, 0.0)
                work[g] = work[g] - factor * pivot
    results = []
    for work in works:
        whole = jnp.concatenate(work, axis=0)
        diagonal = jnp.sum(jnp.where(lane == row, whole, 0.0), axis=1, keepdims=True)
        results.append(whole[:, k:] * (1.0 / jnp.sqrt(diagonal)))
    return results


def finish_kernel(total_rows, grown_hbm, sums, iterate_t, ritz, grown, sem):
    k = ritz.shape[0]
    half = grown.shape[0]
    copy = pltpu.make_async_copy(grown_hbm, grown, sem)
    copy.start()
    every = sums[...].reshape(2 * k, 2 * k) * (1.0 / total_rows)
    inv_before, inv_last = inverse_factors([every[:k, :k], every[k:, k:]])
    copy.wait()
    packed = grown[...]
    iterate_t[:, :half] = dot32(inv_last, packed[:, :k], NT)
    iterate_t[:, half:] = dot32(inv_last, packed[:, k:], NT)
    left = dot32(inv_before, every[:k, k:], (((1,), (0,)), ((), ())))
    ritz[...] = dot32(left, inv_before, NT)


def shards(shots, basis, round_masks):
    n, feat = shots.shape
    k = basis.shape[1]
    nrep, nown = lax.axis_size("rep"), lax.axis_size("owner")
    half, n0 = n // 2, n * 11 // 16
    bf, f32 = jnp.bfloat16, jnp.float32
    vmem, hbm = pl.BlockSpec(memory_space=pltpu.VMEM), pl.BlockSpec(memory_space=pltpu.HBM)
    slab = (2 * k) // 16
    dma = pltpu.SemaphoreType.DMA
    grown, total_sums = pl.pallas_call(
        functools.partial(rounds_kernel, SHARPNESS / math.sqrt(feat)),
        out_shape=(jax.ShapeDtypeStruct((half, 2 * k), f32), jax.ShapeDtypeStruct((16, slab, 2 * k), f32)),
        in_specs=[hbm] * 3,
        out_specs=(hbm, hbm),
        scratch_shapes=[
            pltpu.SMEM((ROUNDS,), jnp.int32),
            pltpu.VMEM((n, feat), bf),
            pltpu.VMEM((k, n), f32),
            pltpu.VMEM((n, feat), bf),
            pltpu.VMEM((NX, n0, feat), bf),
            pltpu.VMEM((NY, n - n0, feat), bf),
            [pltpu.VMEM((NY, n0, feat), bf)] * ROUNDS,
            [pltpu.VMEM((NX, 2, n - n0, feat), bf)] * ROUNDS,
            pltpu.VMEM((NZ, n, feat), bf),
            [pltpu.VMEM((2, 2, n, feat), bf)] * ROUNDS,
            pltpu.VMEM((ROUNDS, 2, n, NZ * n), bf),
            pltpu.VMEM((ROUNDS, NZ, half, 2 * k), bf),
            pltpu.VMEM((NZ * n, 2 * k), bf),
            pltpu.VMEM((ROUNDS, n, 2 * k), f32),
            pltpu.VMEM((ROUNDS, n, 2 * k), f32),
            [pltpu.VMEM((NX, half, 2 * k), bf)] * ROUNDS,
            [pltpu.VMEM((NY, half, 2 * k), bf)] * ROUNDS,
            pltpu.VMEM((half, 2 * k), bf),
            pltpu.VMEM((half, 2 * k), f32),
            pltpu.VMEM((2, half, 2 * k), f32),
            pltpu.VMEM((half, 2 * k), f32),
            pltpu.VMEM((NX, half, 2 * k), f32),
            pltpu.VMEM((NY, half, 2 * k), f32),
            [pltpu.VMEM((16, slab, 2 * k), f32)] * 4,
            pltpu.VMEM((half, 2 * k), f32),
            dma((5,)),
            dma((56,)), dma((56,)),
            dma((ROUNDS, NZ)), dma((ROUNDS, NZ)),
            dma((ROUNDS + 1, 8)), dma((ROUNDS + 1, 8)),
            dma((ROUNDS,)), dma((ROUNDS,)),
            dma((48,)), dma((48,)),
        ],
        compiler_params=pltpu.CompilerParams(
            collective_id=0, has_side_effects=True, vmem_limit_bytes=60 * 1024 * 1024
        ),
        name="rounds",
    )(round_masks, shots, basis.T)
    iterate_t, ritz = pl.pallas_call(
        functools.partial(finish_kernel, float(nown * nrep * n)),
        out_shape=(jax.ShapeDtypeStruct((k, n), f32), jax.ShapeDtypeStruct((k, k), f32)),
        in_specs=[hbm, vmem],
        out_specs=(vmem, vmem),
        scratch_shapes=[pltpu.VMEM((half, 2 * k), f32), pltpu.SemaphoreType.DMA],
        name="finish",
    )(grown, total_sums)
    return iterate_t.T, ritz


def solution(mesh):
    in_specs = (P(("owner", "rep"), None), P(("owner", "rep"), None), P())
    out_specs = (P(("owner", "rep"), None), P())
    return jax.shard_map(shards, mesh=mesh, in_specs=in_specs, out_specs=out_specs, check_vma=False)
```

```python
import functools
import math

import jax
import jax.numpy as jnp
from jax import lax
from jax.experimental import pallas as pl
from jax.experimental.pallas import tpu as pltpu
from jax.sharding import PartitionSpec as P

ROUNDS = 3
SHARPNESS = 1.6
MESH = pl.DeviceIdType.MESH
NT = (((1,), (1,)), ((), ()))
TN = (((0,), (0,)), ((), ()))
NX, NY, NZ = 4, 4, 8

ORDER_STAYS = (
    (
        ("G", 1, 1), ("G", 1, -1), ("Z", 1, 0, 1), ("Z", 1, 0, -1), ("F", 1, 1), ("Z", 1, 1, 1), ("Z", 1, 1, -1),
        ("G", 2, 1), ("G", 2, -1), ("F", 0, 3), ("F", 0, 1), ("Q", 1, 1), ("F", 1, 3), ("Z", 2, 0, 1), ("Q", 1, 0),
        ("Z", 2, 0, -1), ("Q", 0, 0), ("Q", 0, 1), ("Z", 2, 1, 1), ("Z", 2, 1, -1), ("G", 3, 1), ("G", 3, -1),
        ("Z", 3, 0, 1), ("Z", 3, 0, -1), ("F", 5, 3), ("F", 5, 1), ("F", 2, 3), ("F", 2, 1), ("Z", 3, 1, 1),
        ("Z", 3, 1, -1), ("G", 4, 1), ("F", 6, 3), ("Z", 4, 0, 1), ("F", 6, 1), ("F", 3, 3), ("F", 3, 1), ("Q", 5, 0),
        ("Q", 5, 1), ("Z", 4, 1, -1), ("Q", 2, 0), ("Q", 2, 1), ("X", 0),
    ),
    (
        ("F", 7, 3), ("F", 7, 1), ("F", 4, 3), ("F", 4, 1), ("Q", 6, 0), ("Q", 6, 1), ("Q", 3, 0), ("Q", 3, 1),
    ),
    (
        ("X", 1),
    ),
    (
        ("Q", 7, 0), ("Q", 7, 1), ("Q", 4, 0), ("Q", 4, 1),
    ),
    (
        ("X", 2),
    ),
)
ORDER_MOVED = (
    (
        ("T",), ("F", 1, 1), ("F", 1, 3), ("O", 0), ("G", 1, 1), ("G", 1, -1), ("F", 0, 3), ("F", 0, 1), ("O", 1),
        ("Q", 1, 1), ("Q", 1, 0), ("Z", 1, 0, 1), ("Z", 1, 0, -1), ("Q", 0, 0), ("Q", 0, 1), ("G", 2, 1),
        ("G", 2, -1), ("Z", 1, 1, 1), ("Z", 1, 1, -1), ("Z", 2, 0, 1), ("Z", 2, 0, -1), ("F", 5, 3), ("F", 5, 1),
        ("G", 3, 1), ("G", 3, -1), ("F", 2, 3), ("F", 2, 1), ("Z", 2, 1, -1), ("Z", 2, 1, 1), ("F", 6, 3),
        ("F", 6, 1), ("Z", 3, 0, -1), ("F", 3, 3), ("F", 3, 1), ("Z", 3, 0, 1), ("G", 4, 1), ("Q", 5, 0), ("Q", 5, 1),
        ("Q", 2, 0), ("Q", 2, 1), ("Z", 3, 1, -1), ("Z", 3, 1, 1), ("X", 0), ("Z", 4, 0, 1), ("F", 7, 3), ("F", 7, 1),
        ("F", 4, 3), ("F", 4, 1), ("Z", 4, 1, -1),
    ),
    (
        ("Q", 6, 0), ("Q", 6, 1), ("Q", 3, 0), ("Q", 3, 1),
    ),
    (
        ("Q", 7, 0), ("X", 1),
    ),
    (
        ("Q", 7, 1), ("Q", 4, 0), ("Q", 4, 1),
    ),
    (
        ("X", 2),
    ),
)


def dot32(a, b, dims):
    return lax.dot_general(a, b, dims, precision=lax.Precision.HIGHEST, preferred_element_type=jnp.float32)


def pack(rows):
    half = rows.shape[0] // 2
    return jnp.concatenate([rows[:half], rows[half:]], axis=1)


def rounds_kernel(
    scale, masks_hbm, shots_hbm, basis_hbm, rows_out, sums_out,
    masks, shots, basis_t, unit, rowbuf, colbuf, sel0, sel1, own, cands, aff, gpart, gfull, wsend, wrecv, xbufs, ybufs, homeward, ghome, gsend, gback, gx, gy,
    sums, result,
    s_in, s1, r1, sg, rg, sc, rc, sw, rw, sa, ra,
):
    n, feat = shots.shape
    half, n0 = n // 2, rowbuf.shape[1]
    rs, zs, fin, prod = sums
    n1 = n - n0
    k = basis_t.shape[0]
    o, r = lax.axis_index("owner"), lax.axis_index("rep")
    c, x, yh = o % 2, (o // 2) % NX, o // (2 * NX)
    z, yl = r // 2, r % 2
    y = yh * 2 + yl
    nq = 2 * NX
    q = x * 2 + c

    def dev(y=y, x=x, c=c, z=z):
        return (((y // 2) * NX + x) * 2 + c, z * 2 + y % 2)

    twin_y = yh * 2 + c
    twin = dev(y=twin_y, c=yl)
    other_core = dev(c=1 - c)
    moved = c != yl
    stays = c == yl

    loads = [
        pltpu.make_async_copy(shots_hbm, shots, s_in.at[0]),
        pltpu.make_async_copy(basis_hbm, basis_t, s_in.at[1]),
        pltpu.make_async_copy(masks_hbm, masks, s_in.at[2]),
    ]
    for copy in loads:
        copy.start()

    bar = pltpu.get_barrier_semaphore()

    def hello(device):
        pl.semaphore_signal(bar, inc=1, device_id=device, device_id_type=MESH)

    neighbours = [dev(x=(x + i) % NX) for i in (1, 3)] + [dev(y=(y + i) % NY) for i in (1, 3)]
    neighbours += [dev(z=(z + i) % NZ) for i in (1, 7)]
    for neighbour in neighbours:
        hello(neighbour)

    @pl.when(moved)
    def _():
        hello(twin)

    hello(other_core)

    for copy in loads:
        copy.wait()
    values = shots[...].astype(jnp.float32)
    inv = lax.rsqrt(jnp.mean(values * values, axis=-1, keepdims=True) + 1e-06)
    units = (values * inv).astype(jnp.bfloat16)
    rowbuf[x] = units[:n0]
    colbuf[y] = units[n0:]
    g0 = pack(basis_t[...].T) * 0.25

    @pl.when(stays)
    def _():
        own[z] = units
        ghome[...] = g0

    @pl.when(moved)
    def _():
        unit[...] = units
        gsend[0] = g0

    pl.semaphore_wait(bar, len(neighbours) + 1 + (c + yl) % 2)

    def send(src, dst, ssem, rsem, device):
        return pltpu.make_async_remote_copy(
            src_ref=src, dst_ref=dst, send_sem=ssem, recv_sem=rsem, device_id=device, device_id_type=MESH
        )

    pending = []

    def all_sent(numbers):
        for number, rows in numbers:
            ref = own.at[0, pl.ds(0, rows)]
            send(ref, ref, s1.at[number], r1.at[number], other_core).wait_send()

    def move(src, dst, number, device):
        send(src, dst, s1.at[number], r1.at[number], device).start()
        pending.append((number, math.prod(src.shape[:-1])))

    def same(ref, number, device):
        move(ref, ref, number, device)

    def landed(ref, number):
        send(ref, ref, s1.at[number], r1.at[number], other_core).wait_recv()

    halves = (pl.ds(0, half), pl.ds(half, half))
    RING, UP, DN, CORE, TRADE = 0, 32, 39, 46, 52

    trade = send(gsend.at[0], ghome, s1.at[TRADE + 2], r1.at[TRADE + 2], twin)

    def leg(number, i):
        if number == 0:
            return rowbuf.at[(x + i) % NX]
        if number == 1:
            return colbuf.at[(y + i) % NY]
        if number < 5:
            return sel0[number - 2].at[(y + i) % NY]
        return sel1[number - 5].at[(x + i) % NX]

    def part_of(number, i, part):
        ref = leg(number, i)
        if number >= 5:
            return ref.at[part]
        first = ref.shape[0] // 32 * 16 + 16
        return ref.at[pl.ds(0, first)] if part == 0 else ref.at[pl.ds(first, ref.shape[0] - first)]

    def step(number, i):
        return dev(x=(x + i) % NX) if number in (0, 5, 6, 7) else dev(y=(y + i) % NY)

    def begin(number):
        same(leg(number, 0), RING + 4 * number, step(number, 1))
        same(leg(number, 0), RING + 4 * number + 1, step(number, 3))

    def on_full(number, k):
        part = 0 if k == 3 else 1
        landed(leg(number, k), RING + 4 * number + part)
        same(part_of(number, k, part), RING + 4 * number + 2 + part, step(number, 4 - k))

    def on_half(number, part):
        landed(part_of(number, 2, part), RING + 4 * number + 2 + part)

    def pick():
        for t in range(ROUNDS):
            m = masks[t]
            sel0[t][y] = rowbuf[x ^ ((m // 2) % 4)]
            for a in range(2):
                sel1[t][x, a] = colbuf[(yh ^ (m // 8)) * 2 + a]
        for number in (2, 5, 3, 6):
            begin(number)

    up, down = dev(z=(z + 1) % NZ), dev(z=(z + NZ - 1) % NZ)

    def z_begin(h):
        same(own.at[z, halves[h]], UP + h, up)
        same(own.at[z, halves[h]], DN + h, down)

    def on_z(s, h, direction):
        ref = own.at[(z + NZ - direction * s) % NZ, halves[h]]
        base = UP if direction == 1 else DN
        landed(ref, base + (2 * (s - 1) + h if s < 4 else 6))
        if s < 3 or (s == 3 and (h == 0) == (direction == 1)):
            same(ref, base + (2 * s + h if s < 3 else 6), up if direction == 1 else down)

    def g_begin():
        gpart[0, z] = ghome[...].astype(jnp.bfloat16)
        for i, device in ((1, up), (7, down)):
            send(gpart.at[0, z], gpart.at[0, z], sg.at[0, i], rg.at[0, i], device).start()

    def on_g(s, direction):
        ref = gpart.at[0, (z + NZ - direction * s) % NZ]
        i = s if direction == 1 else NZ - s
        send(ref, ref, sg.at[0, i], rg.at[0, i], other_core).wait_recv()
        if s < 3 or (s == 3 and direction == 1):
            send(ref, ref, sg.at[0, i + direction], rg.at[0, i + direction], up if direction == 1 else down).start()

    def choose(t):
        m = masks[t]
        for a in range(2):
            cands[t][c, a, :n0] = sel0[t][(yh ^ (m // 8)) * 2 + a]
            cands[t][c, a, n0:] = sel1[t][x ^ ((m // 2) % 4), a]
            number = CORE + 2 * t + a
            same(cands[t].at[c, a], number, other_core)

    def near(j):
        return (NZ + (1 - 2 * ((j + 1) % 2)) * ((j + 1) // 2)) % NZ

    def affinities(t, lo=0, hi=NZ):
        holder = yl ^ (masks[t] % 2)

        @pl.loop(lo, hi)
        def _(j):
            item = (z + near(j)) % NZ
            columns = pl.ds(pl.multiple_of(item * n, n), n)
            for a in range(2):
                scores = lax.dot_general(cands[t][holder, a], own[item], NT, preferred_element_type=jnp.float32)
                aff[t, a, :, columns] = jnp.exp(scores * scale).astype(jnp.bfloat16)

    def gather(order, seen, stays_here):
        def whole(number):
            return all(e in seen for e in (("F", number, 1), ("F", number, 3), ("Q", number, 0), ("Q", number, 1)))

        def z_here(s):
            if s == 0:
                return stays_here or (("O", 0) in seen and ("O", 1) in seen)
            if s == 4:
                return ("Z", 4, 0, 1) in seen and ("Z", 4, 1, -1) in seen
            return all(("Z", s, h, d) in seen for h in (0, 1) for d in (1, -1))

        for event in order:
            kind, *args = event
            seen.add(event)
            if kind == "F":
                on_full(*args)
                number, k = args
                if number in (2, 5) and ("F", number, 4 - k) in seen:
                    begin(number + 2)
            elif kind == "Q":
                on_half(*args)
            elif kind == "Z":
                on_z(*args)
            elif kind == "G":
                on_g(*args)
            elif kind == "O":
                landed(own.at[z, halves[args[0]]], TRADE + args[0])
                z_begin(args[0])
            elif kind == "T":
                trade.wait_recv()
                g_begin()
            else:
                for a in range(2):
                    landed(cands[args[0]].at[1 - c, a], CORE + 2 * args[0] + a)
            if kind in "FQ":
                if "picked" not in seen and whole(0) and whole(1):
                    seen.add("picked")
                    pick()
                for t in range(ROUNDS):
                    if ("chosen", t) not in seen and whole(2 + t) and whole(5 + t):
                        seen.add(("chosen", t))
                        choose(t)
            have = sum(("items", j) in seen for j in range(NZ))
            ready = have
            while ("X", 0) in seen and ready < NZ and z_here((ready + 1) // 2):
                seen.add(("items", ready))
                ready += 1
            if ready > have:
                affinities(0, have, ready)

    seen_stays, seen_moved = set(), set()

    @pl.when(stays)
    def _():
        g_begin()
        z_begin(0)
        z_begin(1)
        begin(0)
        begin(1)
        gather(ORDER_STAYS[0], seen_stays, True)

    sent_if_stays = list(pending)
    pending.clear()

    @pl.when(moved)
    def _():
        trade.start()
        for h in range(2):
            move(unit.at[halves[h]], own.at[z, halves[h]], TRADE + h, twin)
        begin(0)
        begin(1)
        gather(ORDER_MOVED[0], seen_moved, False)

    sent_if_moved = list(pending)
    pending.clear()

    def gather_rest(stage):
        @pl.when(stays)
        def _():
            gather(ORDER_STAYS[stage], seen_stays, True)

        sent_if_stays.extend(pending)
        pending.clear()

        @pl.when(moved)
        def _():
            gather(ORDER_MOVED[stage], seen_moved, False)

        sent_if_moved.extend(pending)
        pending.clear()

    def g_send(t, value):
        gpart[t, z] = value.astype(jnp.bfloat16)

        for i in (3, 5, 4, 2, 6, 1, 7):
            send(gpart.at[t, z], gpart.at[t, z], sg.at[t, i], rg.at[t, i], dev(z=(z + i) % NZ)).start()

    grown = ghome[...]

    def partner(t):
        m = masks[t]
        return y ^ ((m // 8) * 2 + m % 2), x ^ ((m // 2) % 4)

    lane = lax.broadcasted_iota(jnp.int32, (half, 2 * k), 1)
    tail = jnp.where(lane == k, 1.0, 0.0)

    def unpack(t, item):
        p = gpart[t, item].astype(jnp.float32)
        start = pl.multiple_of(item * n, n)
        gfull[pl.ds(start, half), :] = jnp.where(lane < k, p, tail).astype(jnp.bfloat16)
        gfull[pl.ds(start + half, half), :] = jnp.where(lane < k, pltpu.roll(p, k, 1), tail).astype(jnp.bfloat16)

    def carried(t):
        unpack(t, z)

        @pl.loop(1, NZ)
        def _(j):
            i = near(j)
            item = (z + NZ - i) % NZ
            if t > 0:
                ref = gpart.at[t, item]
                send(ref, ref, sg.at[t, i], rg.at[t, i], other_core).wait_recv()
            unpack(t, item)

        wsend[t] = jnp.dot(aff[t, 1 - c], gfull[...], preferred_element_type=jnp.float32)
        copy = send(wsend.at[t], wrecv.at[t], sw.at[t], rw.at[t], other_core)
        copy.start()
        mine = jnp.dot(aff[t, c], gfull[...], preferred_element_type=jnp.float32)
        copy.wait_recv()
        product = mine + wrecv[t]
        return pack(product[:, :k] / product[:, k:k + 1]).astype(jnp.bfloat16)

    def x_send(ref, sems, t, base):
        for i in (2, 1, 3):
            send(ref, ref, sems[0].at[t, base + i], sems[1].at[t, base + i], dev(x=(x + i) % NX)).start()

    def x_wait(buf, sems, t, base):
        for i in range(1, NX):
            ref = buf.at[(x + NX - i) % NX]
            send(ref, ref, sems[0].at[t, base + i], sems[1].at[t, base + i], other_core).wait_recv()

    def y_send(ref, sems, t, base):
        for i in (2, 1, 3):
            send(ref, ref, sems[0].at[t, base + i], sems[1].at[t, base + i], dev(y=(y + i) % NY)).start()

    def y_wait(buf, sems, t, base):
        for i in range(1, NY):
            ref = buf.at[(y + NY - i) % NY]
            send(ref, ref, sems[0].at[t, base + i], sems[1].at[t, base + i], other_core).wait_recv()

    csem = (sc, rc)
    for t in range(ROUNDS - 1):
        if t > 0:
            g_send(t, grown)
            gather_rest(3)
        py, px = partner(t)
        xbufs[t][x] = carried(t)
        x_send(xbufs[t].at[x], csem, t, 0)
        if t == 0:
            gather_rest(1)
        else:
            gather_rest(4)
            affinities(2)
        x_wait(xbufs[t], csem, t, 0)
        ybufs[t][y] = xbufs[t][px]
        y_send(ybufs[t].at[y], csem, t, 4)
        if t == 0:
            gather_rest(2)
            affinities(1)
        y_wait(ybufs[t], csem, t, 4)
        grown = grown + ybufs[t][py].astype(jnp.float32)

    t = ROUNDS - 1
    py, px = partner(t)
    g_send(t, grown)
    gx[x] = grown
    x_send(gx.at[x], csem, ROUNDS, 0)

    @pl.when(stays)
    def _():
        gback[...] = grown

    @pl.when(moved)
    def _():
        gsend[1] = grown
        send(gsend.at[1], gback, s1.at[TRADE + 3], r1.at[TRADE + 3], twin).start()

    x_wait(gx, csem, ROUNDS, 0)
    gy[y] = gx[px]
    y_send(gy.at[y], csem, ROUNDS, 4)
    came = carried(t)
    xbufs[t][x] = came
    x_send(xbufs[t].at[x], csem, t, 0)
    y_wait(gy, csem, ROUNDS, 4)
    before = gy[py]
    after = before + came.astype(jnp.float32)

    top = jnp.where(lane < k, before, pltpu.roll(after, k, 1))
    bottom = jnp.where(lane < k, pltpu.roll(before, k, 1), after)
    prod[...] = (dot32(top, top, TN) + dot32(bottom, bottom, TN)).reshape(prod.shape)

    def total(ref, count):
        value = ref[0]
        for i in range(1, count):
            value = value + ref[i]
        return value

    group = 2 * NX * 2
    place = q * 2 + yl
    line = (z * 2 + yh) % group

    def near_dev(i):
        there = (place + i) % group
        return there, dev(y=yh * 2 + there % 2, x=there // 4, c=there // 2 % 2)

    def far_dev(i):
        there = (line + i) % group
        return dev(y=there % 2 * 2 + yl, z=there // 2)

    for i in range(1, group):
        there, device = near_dev(i)
        send(prod.at[there], rs.at[place], sa.at[i], ra.at[i], device).start()
    rs[place] = prod[place]

    x_wait(xbufs[t], csem, t, 0)
    homeward[...] = xbufs[t][px]

    @pl.when(stays)
    def _():
        ybufs[t][y] = homeward[...]

    def home_copy(i):
        ty = (y + i) % NY
        device = dev(y=(ty // 2) * 2 + c, c=ty % 2)
        return send(homeward, ybufs[t].at[y], sc.at[t, 4 + i], rc.at[t, 4 + i], device)

    @pl.when(moved)
    def _():
        home_copy(0).start()

    for i in range(1, NY):
        home_copy(i).start()

    for i in range(1, group):
        send(prod.at[0], rs.at[(place + group - i) % group], sa.at[i], ra.at[i], other_core).wait_recv()
    zs[line] = total(rs, group)

    for i in (8, 7, 9, 6, 10, 5, 11, 4, 12, 3, 13, 2, 14, 1, 15):
        ref = zs.at[line]
        send(ref, ref, sa.at[group + i], ra.at[group + i], far_dev(i)).start()
    for i in range(1, group):
        ref = zs.at[(line + group - i) % group]
        send(ref, ref, sa.at[group + i], ra.at[group + i], other_core).wait_recv()
    fin[place] = total(zs, group)

    for i in range(1, group):
        ref = fin.at[place]
        send(ref, ref, sa.at[2 * group + i], ra.at[2 * group + i], near_dev(i)[1]).start()

    @pl.when(moved)
    def _():
        send(gsend.at[1], gback, s1.at[TRADE + 3], r1.at[TRADE + 3], twin).wait_recv()
        ref = ybufs[t].at[twin_y]
        send(ref, ref, sc.at[t, 4], rc.at[t, 4], other_core).wait_recv()

    for i in range(1, NY):
        ref = ybufs[t].at[(twin_y + NY - i) % NY]
        send(ref, ref, sc.at[t, 4 + i], rc.at[t, 4 + i], other_core).wait_recv()
    m = masks[t]
    result[...] = gback[...] + ybufs[t][twin_y ^ ((m // 8) * 2 + m % 2)].astype(jnp.float32)
    rows_copy = pltpu.make_async_copy(result, rows_out, s_in.at[3])
    rows_copy.start()

    for i in range(1, group):
        ref = fin.at[(place + group - i) % group]
        send(ref, ref, sa.at[2 * group + i], ra.at[2 * group + i], other_core).wait_recv()

    sums_copy = pltpu.make_async_copy(fin, sums_out, s_in.at[4])
    sums_copy.start()

    assert not pending

    @pl.when(stays)
    def _():
        all_sent(sent_if_stays)

    @pl.when(moved)
    def _():
        all_sent(sent_if_moved)
        trade.wait_send()
        send(gsend.at[1], gback, s1.at[TRADE + 3], r1.at[TRADE + 3], twin).wait_send()
        home_copy(0).wait_send()

    @pl.loop(1, NX)
    def _(i):
        for row in range(ROUNDS):
            ref = xbufs[row].at[x]
            send(ref, ref, sc.at[row, i], rc.at[row, i], other_core).wait_send()
            send(ref, ref, sc.at[row, 4 + i], rc.at[row, 4 + i], other_core).wait_send()
        ref = gx.at[x]
        send(ref, ref, sc.at[ROUNDS, i], rc.at[ROUNDS, i], other_core).wait_send()
        send(ref, ref, sc.at[ROUNDS, 4 + i], rc.at[ROUNDS, 4 + i], other_core).wait_send()

    @pl.loop(1, NZ)
    def _(i):
        for row in range(ROUNDS):
            ref = gpart.at[row, z]
            send(ref, ref, sg.at[row, i], rg.at[row, i], other_core).wait_send()

    @pl.loop(1, group)
    def _(i):
        for base in range(3):
            ref = fin.at[place]
            send(ref, ref, sa.at[base * group + i], ra.at[base * group + i], other_core).wait_send()

    for row in range(ROUNDS):
        send(wsend.at[row], wrecv.at[row], sw.at[row], rw.at[row], other_core).wait_send()
    rows_copy.wait()
    sums_copy.wait()


def inverse_factors(grams):
    k = grams[0].shape[0]
    row = lax.broadcasted_iota(jnp.int32, (k, 2 * k), 0)
    lane = lax.broadcasted_iota(jnp.int32, (k, 2 * k), 1)
    identity = jnp.where(lane == row, 1.0, 0.0)[:, :k]
    works = [jnp.concatenate([gram, identity], axis=1) for gram in grams]
    works = [[work[8 * g:8 * g + 8] for g in range(k // 8)] for work in works]
    below = lax.broadcasted_iota(jnp.int32, (8, 1), 0)
    for i in range(k - 1):
        own, s = i // 8, i % 8
        for work in works:
            pivot = work[own][s:s + 1, :] * (1.0 / work[own][s:s + 1, i:i + 1])
            for g in range(own, k // 8):
                factor = work[g][:, i:i + 1]
                if g == own:
                    factor = jnp.where(below > s, factor, 0.0)
                work[g] = work[g] - factor * pivot
    results = []
    for work in works:
        whole = jnp.concatenate(work, axis=0)
        diagonal = jnp.sum(jnp.where(lane == row, whole, 0.0), axis=1, keepdims=True)
        results.append(whole[:, k:] * (1.0 / jnp.sqrt(diagonal)))
    return results


def finish_kernel(total_rows, grown_hbm, sums, iterate_t, ritz, grown, sem):
    k = ritz.shape[0]
    half = grown.shape[0]
    copy = pltpu.make_async_copy(grown_hbm, grown, sem)
    copy.start()
    every = sums[...].reshape(2 * k, 2 * k) * (1.0 / total_rows)
    inv_before, inv_last = inverse_factors([every[:k, :k], every[k:, k:]])
    copy.wait()
    packed = grown[...]
    iterate_t[:, :half] = dot32(inv_last, packed[:, :k], NT)
    iterate_t[:, half:] = dot32(inv_last, packed[:, k:], NT)
    left = dot32(inv_before, every[:k, k:], (((1,), (0,)), ((), ())))
    ritz[...] = dot32(left, inv_before, NT)


def shards(shots, basis, round_masks):
    n, feat = shots.shape
    k = basis.shape[1]
    nrep, nown = lax.axis_size("rep"), lax.axis_size("owner")
    half, n0 = n // 2, n * 11 // 16
    bf, f32 = jnp.bfloat16, jnp.float32
    vmem, hbm = pl.BlockSpec(memory_space=pltpu.VMEM), pl.BlockSpec(memory_space=pltpu.HBM)
    slab = (2 * k) // 16
    dma = pltpu.SemaphoreType.DMA
    grown, total_sums = pl.pallas_call(
        functools.partial(rounds_kernel, SHARPNESS / math.sqrt(feat)),
        out_shape=(jax.ShapeDtypeStruct((half, 2 * k), f32), jax.ShapeDtypeStruct((16, slab, 2 * k), f32)),
        in_specs=[hbm] * 3,
        out_specs=(hbm, hbm),
        scratch_shapes=[
            pltpu.SMEM((ROUNDS,), jnp.int32),
            pltpu.VMEM((n, feat), bf),
            pltpu.VMEM((k, n), f32),
            pltpu.VMEM((n, feat), bf),
            pltpu.VMEM((NX, n0, feat), bf),
            pltpu.VMEM((NY, n - n0, feat), bf),
            [pltpu.VMEM((NY, n0, feat), bf)] * ROUNDS,
            [pltpu.VMEM((NX, 2, n - n0, feat), bf)] * ROUNDS,
            pltpu.VMEM((NZ, n, feat), bf),
            [pltpu.VMEM((2, 2, n, feat), bf)] * ROUNDS,
            pltpu.VMEM((ROUNDS, 2, n, NZ * n), bf),
            pltpu.VMEM((ROUNDS, NZ, half, 2 * k), bf),
            pltpu.VMEM((NZ * n, 2 * k), bf),
            pltpu.VMEM((ROUNDS, n, 2 * k), f32),
            pltpu.VMEM((ROUNDS, n, 2 * k), f32),
            [pltpu.VMEM((NX, half, 2 * k), bf)] * ROUNDS,
            [pltpu.VMEM((NY, half, 2 * k), bf)] * ROUNDS,
            pltpu.VMEM((half, 2 * k), bf),
            pltpu.VMEM((half, 2 * k), f32),
            pltpu.VMEM((2, half, 2 * k), f32),
            pltpu.VMEM((half, 2 * k), f32),
            pltpu.VMEM((NX, half, 2 * k), f32),
            pltpu.VMEM((NY, half, 2 * k), f32),
            [pltpu.VMEM((16, slab, 2 * k), f32)] * 4,
            pltpu.VMEM((half, 2 * k), f32),
            dma((5,)),
            dma((56,)), dma((56,)),
            dma((ROUNDS, NZ)), dma((ROUNDS, NZ)),
            dma((ROUNDS + 1, 8)), dma((ROUNDS + 1, 8)),
            dma((ROUNDS,)), dma((ROUNDS,)),
            dma((48,)), dma((48,)),
        ],
        compiler_params=pltpu.CompilerParams(
            collective_id=0, has_side_effects=True, vmem_limit_bytes=60 * 1024 * 1024
        ),
        name="rounds",
    )(round_masks, shots, basis.T)
    iterate_t, ritz = pl.pallas_call(
        functools.partial(finish_kernel, float(nown * nrep * n)),
        out_shape=(jax.ShapeDtypeStruct((k, n), f32), jax.ShapeDtypeStruct((k, k), f32)),
        in_specs=[hbm, vmem],
        out_specs=(vmem, vmem),
        scratch_shapes=[pltpu.VMEM((half, 2 * k), f32), pltpu.SemaphoreType.DMA],
        name="finish",
    )(grown, total_sums)
    return iterate_t.T, ritz


def solution(mesh):
    in_specs = (P(("owner", "rep"), None), P(("owner", "rep"), None), P())
    out_specs = (P(("owner", "rep"), None), P())
    return jax.shard_map(shards, mesh=mesh, in_specs=in_specs, out_specs=out_specs, check_vma=False)
```

```python
import functools
import math

import jax
import jax.numpy as jnp
from jax import lax
from jax.experimental import pallas as pl
from jax.experimental.pallas import tpu as pltpu
from jax.sharding import PartitionSpec as P

ROUNDS = 3
SHARPNESS = 1.6
MESH = pl.DeviceIdType.MESH
NT = (((1,), (1,)), ((), ()))
TN = (((0,), (0,)), ((), ()))
NX, NY, NZ = 4, 4, 8

ORDER_STAYS = (
    (
        ("G", 1, 1), ("G", 1, -1), ("Z", 1, 0, 1), ("Z", 1, 0, -1), ("F", 1, 1), ("Z", 1, 1, 1), ("Z", 1, 1, -1),
        ("G", 2, 1), ("G", 2, -1), ("F", 0, 3), ("F", 0, 1), ("Q", 1, 1), ("F", 1, 3), ("Z", 2, 0, 1), ("Q", 1, 0),
        ("Z", 2, 0, -1), ("Q", 0, 0), ("Q", 0, 1), ("Z", 2, 1, 1), ("Z", 2, 1, -1), ("G", 3, 1), ("G", 3, -1),
        ("Z", 3, 0, 1), ("Z", 3, 0, -1), ("F", 5, 3), ("F", 5, 1), ("F", 2, 3), ("F", 2, 1), ("Z", 3, 1, 1),
        ("Z", 3, 1, -1), ("G", 4, 1), ("F", 6, 3), ("Z", 4, 0, 1), ("F", 6, 1), ("F", 3, 3), ("F", 3, 1), ("Q", 5, 0),
        ("Q", 5, 1), ("Z", 4, 1, -1), ("Q", 2, 0), ("Q", 2, 1), ("X", 0),
    ),
    (
        ("F", 7, 3), ("F", 7, 1), ("F", 4, 3), ("F", 4, 1), ("Q", 6, 0), ("Q", 6, 1), ("Q", 3, 0), ("Q", 3, 1),
    ),
    (
        ("X", 1),
    ),
    (
        ("Q", 7, 0), ("Q", 7, 1), ("Q", 4, 0), ("Q", 4, 1),
    ),
    (
        ("X", 2),
    ),
)
ORDER_MOVED = (
    (
        ("T",), ("F", 1, 1), ("F", 1, 3), ("O", 0), ("G", 1, 1), ("G", 1, -1), ("F", 0, 3), ("F", 0, 1), ("O", 1),
        ("Q", 1, 1), ("Q", 1, 0), ("Z", 1, 0, 1), ("Z", 1, 0, -1), ("Q", 0, 0), ("Q", 0, 1), ("G", 2, 1),
        ("G", 2, -1), ("Z", 1, 1, 1), ("Z", 1, 1, -1), ("Z", 2, 0, 1), ("Z", 2, 0, -1), ("F", 5, 3), ("F", 5, 1),
        ("G", 3, 1), ("G", 3, -1), ("F", 2, 3), ("F", 2, 1), ("Z", 2, 1, -1), ("Z", 2, 1, 1), ("F", 6, 3),
        ("F", 6, 1), ("Z", 3, 0, -1), ("F", 3, 3), ("F", 3, 1), ("Z", 3, 0, 1), ("G", 4, 1), ("Q", 5, 0), ("Q", 5, 1),
        ("Q", 2, 0), ("Q", 2, 1), ("Z", 3, 1, -1), ("Z", 3, 1, 1), ("X", 0), ("Z", 4, 0, 1), ("F", 7, 3), ("F", 7, 1),
        ("F", 4, 3), ("F", 4, 1), ("Z", 4, 1, -1),
    ),
    (
        ("Q", 6, 0), ("Q", 6, 1), ("Q", 3, 0), ("Q", 3, 1),
    ),
    (
        ("Q", 7, 0), ("X", 1),
    ),
    (
        ("Q", 7, 1), ("Q", 4, 0), ("Q", 4, 1),
    ),
    (
        ("X", 2),
    ),
)


def dot32(a, b, dims):
    return lax.dot_general(a, b, dims, precision=lax.Precision.HIGHEST, preferred_element_type=jnp.float32)


def pack(rows):
    half = rows.shape[0] // 2
    return jnp.concatenate([rows[:half], rows[half:]], axis=1)


def rounds_kernel(
    scale, masks_hbm, shots_hbm, basis_hbm, rows_out, sums_out,
    masks, shots, basis_t, unit, rowbuf, colbuf, sel0, sel1, own, cands, aff, gpart, gfull, wsend, wrecv, xbufs, ybufs, homeward, ghome, gsend, gback, gx, gy,
    sums, result,
    s_in, s1, r1, sg, rg, sc, rc, sw, rw, sa, ra,
):
    n, feat = shots.shape
    half, n0 = n // 2, rowbuf.shape[1]
    rs, zs, fin, prod = sums
    n1 = n - n0
    k = basis_t.shape[0]
    o, r = lax.axis_index("owner"), lax.axis_index("rep")
    c, x, yh = o % 2, (o // 2) % NX, o // (2 * NX)
    z, yl = r // 2, r % 2
    y = yh * 2 + yl
    nq = 2 * NX
    q = x * 2 + c

    def dev(y=y, x=x, c=c, z=z):
        return (((y // 2) * NX + x) * 2 + c, z * 2 + y % 2)

    twin_y = yh * 2 + c
    twin = dev(y=twin_y, c=yl)
    other_core = dev(c=1 - c)
    moved = c != yl
    stays = c == yl

    loads = [
        pltpu.make_async_copy(shots_hbm, shots, s_in.at[0]),
        pltpu.make_async_copy(basis_hbm, basis_t, s_in.at[1]),
        pltpu.make_async_copy(masks_hbm, masks, s_in.at[2]),
    ]
    for copy in loads:
        copy.start()

    bar = pltpu.get_barrier_semaphore()

    def hello(device):
        pl.semaphore_signal(bar, inc=1, device_id=device, device_id_type=MESH)

    neighbours = [dev(x=(x + i) % NX) for i in (1, 3)] + [dev(y=(y + i) % NY) for i in (1, 3)]
    neighbours += [dev(z=(z + i) % NZ) for i in (1, 7)]
    for neighbour in neighbours:
        hello(neighbour)

    @pl.when(moved)
    def _():
        hello(twin)

    hello(other_core)

    for copy in loads:
        copy.wait()
    values = shots[...].astype(jnp.float32)
    inv = lax.rsqrt(jnp.mean(values * values, axis=-1, keepdims=True) + 1e-06)
    units = (values * inv).astype(jnp.bfloat16)
    rowbuf[x] = units[:n0]
    colbuf[y] = units[n0:]
    g0 = pack(basis_t[...].T) * 0.25

    @pl.when(stays)
    def _():
        own[z] = units
        ghome[...] = g0

    @pl.when(moved)
    def _():
        unit[...] = units
        gsend[0] = g0

    pl.semaphore_wait(bar, len(neighbours) + 1 + (c + yl) % 2)

    def send(src, dst, ssem, rsem, device):
        return pltpu.make_async_remote_copy(
            src_ref=src, dst_ref=dst, send_sem=ssem, recv_sem=rsem, device_id=device, device_id_type=MESH
        )

    pending = []

    def all_sent(numbers):
        for number, rows in numbers:
            ref = own.at[0, pl.ds(0, rows)]
            send(ref, ref, s1.at[number], r1.at[number], other_core).wait_send()

    def move(src, dst, number, device):
        send(src, dst, s1.at[number], r1.at[number], device).start()
        pending.append((number, math.prod(src.shape[:-1])))

    def same(ref, number, device):
        move(ref, ref, number, device)

    def landed(ref, number):
        send(ref, ref, s1.at[number], r1.at[number], other_core).wait_recv()

    halves = (pl.ds(0, half), pl.ds(half, half))
    RING, UP, DN, CORE, TRADE = 0, 32, 39, 46, 52

    trade = send(gsend.at[0], ghome, s1.at[TRADE + 2], r1.at[TRADE + 2], twin)

    def leg(number, i):
        if number == 0:
            return rowbuf.at[(x + i) % NX]
        if number == 1:
            return colbuf.at[(y + i) % NY]
        if number < 5:
            return sel0[number - 2].at[(y + i) % NY]
        return sel1[number - 5].at[(x + i) % NX]

    def part_of(number, i, part):
        ref = leg(number, i)
        if number >= 5:
            return ref.at[part]
        first = ref.shape[0] // 32 * 16 + 16
        return ref.at[pl.ds(0, first)] if part == 0 else ref.at[pl.ds(first, ref.shape[0] - first)]

    def step(number, i):
        return dev(x=(x + i) % NX) if number in (0, 5, 6, 7) else dev(y=(y + i) % NY)

    def begin(number):
        same(leg(number, 0), RING + 4 * number, step(number, 1))
        same(leg(number, 0), RING + 4 * number + 1, step(number, 3))

    def on_full(number, k):
        part = 0 if k == 3 else 1
        landed(leg(number, k), RING + 4 * number + part)
        same(part_of(number, k, part), RING + 4 * number + 2 + part, step(number, 4 - k))

    def on_half(number, part):
        landed(part_of(number, 2, part), RING + 4 * number + 2 + part)

    def pick():
        for t in range(ROUNDS):
            m = masks[t]
            sel0[t][y] = rowbuf[x ^ ((m // 2) % 4)]
            for a in range(2):
                sel1[t][x, a] = colbuf[(yh ^ (m // 8)) * 2 + a]
        for number in (2, 5, 3, 6):
            begin(number)

    lane = lax.broadcasted_iota(jnp.int32, (half, 2 * k), 1)
    tail = jnp.where(lane == k, 1.0, 0.0)

    def unpack(t, item):
        p = gpart[t, item].astype(jnp.float32)
        start = pl.multiple_of(item * n, n)
        gfull[pl.ds(start, half), :] = jnp.where(lane < k, p, tail).astype(jnp.bfloat16)
        gfull[pl.ds(start + half, half), :] = jnp.where(lane < k, pltpu.roll(p, k, 1), tail).astype(jnp.bfloat16)

    up, down = dev(z=(z + 1) % NZ), dev(z=(z + NZ - 1) % NZ)

    def z_begin(h):
        same(own.at[z, halves[h]], UP + h, up)
        same(own.at[z, halves[h]], DN + h, down)

    def on_z(s, h, direction):
        ref = own.at[(z + NZ - direction * s) % NZ, halves[h]]
        base = UP if direction == 1 else DN
        landed(ref, base + (2 * (s - 1) + h if s < 4 else 6))
        if s < 3 or (s == 3 and (h == 0) == (direction == 1)):
            same(ref, base + (2 * s + h if s < 3 else 6), up if direction == 1 else down)

    def g_begin():
        gpart[0, z] = ghome[...].astype(jnp.bfloat16)
        unpack(0, z)
        for i, device in ((1, up), (7, down)):
            send(gpart.at[0, z], gpart.at[0, z], sg.at[0, i], rg.at[0, i], device).start()

    def on_g(s, direction):
        ref = gpart.at[0, (z + NZ - direction * s) % NZ]
        i = s if direction == 1 else NZ - s
        send(ref, ref, sg.at[0, i], rg.at[0, i], other_core).wait_recv()
        if s < 3 or (s == 3 and direction == 1):
            send(ref, ref, sg.at[0, i + direction], rg.at[0, i + direction], up if direction == 1 else down).start()
        unpack(0, (z + NZ - direction * s) % NZ)

    def choose(t):
        m = masks[t]
        for a in range(2):
            cands[t][c, a, :n0] = sel0[t][(yh ^ (m // 8)) * 2 + a]
            cands[t][c, a, n0:] = sel1[t][x ^ ((m // 2) % 4), a]
            number = CORE + 2 * t + a
            same(cands[t].at[c, a], number, other_core)

    def near(j):
        return (NZ + (1 - 2 * ((j + 1) % 2)) * ((j + 1) // 2)) % NZ

    def affinities(t, lo=0, hi=NZ):
        holder = yl ^ (masks[t] % 2)

        @pl.loop(lo, hi)
        def _(j):
            item = (z + near(j)) % NZ
            columns = pl.ds(pl.multiple_of(item * n, n), n)
            for a in range(2):
                scores = lax.dot_general(cands[t][holder, a], own[item], NT, preferred_element_type=jnp.float32)
                aff[t, a, :, columns] = jnp.exp(scores * scale).astype(jnp.bfloat16)

    def gather(order, seen, stays_here):
        def whole(number):
            return all(e in seen for e in (("F", number, 1), ("F", number, 3), ("Q", number, 0), ("Q", number, 1)))

        def z_here(s):
            if s == 0:
                return stays_here or (("O", 0) in seen and ("O", 1) in seen)
            if s == 4:
                return ("Z", 4, 0, 1) in seen and ("Z", 4, 1, -1) in seen
            return all(("Z", s, h, d) in seen for h in (0, 1) for d in (1, -1))

        for event in order:
            kind, *args = event
            seen.add(event)
            if kind == "F":
                on_full(*args)
                number, k = args
                if number in (2, 5) and ("F", number, 4 - k) in seen:
                    begin(number + 2)
            elif kind == "Q":
                on_half(*args)
            elif kind == "Z":
                on_z(*args)
            elif kind == "G":
                on_g(*args)
            elif kind == "O":
                landed(own.at[z, halves[args[0]]], TRADE + args[0])
                z_begin(args[0])
            elif kind == "T":
                trade.wait_recv()
                g_begin()
            else:
                for a in range(2):
                    landed(cands[args[0]].at[1 - c, a], CORE + 2 * args[0] + a)
            if kind in "FQ":
                if "picked" not in seen and whole(0) and whole(1):
                    seen.add("picked")
                    pick()
                for t in range(ROUNDS):
                    if ("chosen", t) not in seen and whole(2 + t) and whole(5 + t):
                        seen.add(("chosen", t))
                        choose(t)
            have = sum(("items", j) in seen for j in range(NZ))
            ready = have
            while ("X", 0) in seen and ready < NZ and z_here((ready + 1) // 2):
                seen.add(("items", ready))
                ready += 1
            if ready > have:
                affinities(0, have, ready)

    seen_stays, seen_moved = set(), set()

    @pl.when(stays)
    def _():
        g_begin()
        z_begin(0)
        z_begin(1)
        begin(0)
        begin(1)
        gather(ORDER_STAYS[0], seen_stays, True)

    sent_if_stays = list(pending)
    pending.clear()

    @pl.when(moved)
    def _():
        trade.start()
        for h in range(2):
            move(unit.at[halves[h]], own.at[z, halves[h]], TRADE + h, twin)
        begin(0)
        begin(1)
        gather(ORDER_MOVED[0], seen_moved, False)

    sent_if_moved = list(pending)
    pending.clear()

    def gather_rest(stage):
        @pl.when(stays)
        def _():
            gather(ORDER_STAYS[stage], seen_stays, True)

        sent_if_stays.extend(pending)
        pending.clear()

        @pl.when(moved)
        def _():
            gather(ORDER_MOVED[stage], seen_moved, False)

        sent_if_moved.extend(pending)
        pending.clear()

    def g_send(t, value):
        gpart[t, z] = value.astype(jnp.bfloat16)

        for i in (3, 5, 4, 2, 6, 1, 7):
            send(gpart.at[t, z], gpart.at[t, z], sg.at[t, i], rg.at[t, i], dev(z=(z + i) % NZ)).start()

    grown = ghome[...]

    def partner(t):
        m = masks[t]
        return y ^ ((m // 8) * 2 + m % 2), x ^ ((m // 2) % 4)

    def carried(t):
        if t > 0:
            unpack(t, z)

            @pl.loop(1, NZ)
            def _(j):
                i = near(j)
                item = (z + NZ - i) % NZ
                ref = gpart.at[t, item]
                send(ref, ref, sg.at[t, i], rg.at[t, i], other_core).wait_recv()
                unpack(t, item)

        wsend[t] = jnp.dot(aff[t, 1 - c], gfull[...], preferred_element_type=jnp.float32)
        copy = send(wsend.at[t], wrecv.at[t], sw.at[t], rw.at[t], other_core)
        copy.start()
        mine = jnp.dot(aff[t, c], gfull[...], preferred_element_type=jnp.float32)
        copy.wait_recv()
        product = mine + wrecv[t]
        return pack(product[:, :k] / product[:, k:k + 1]).astype(jnp.bfloat16)

    def x_send(ref, sems, t, base):
        for i in (2, 1, 3):
            send(ref, ref, sems[0].at[t, base + i], sems[1].at[t, base + i], dev(x=(x + i) % NX)).start()

    def x_wait(buf, sems, t, base):
        for i in range(1, NX):
            ref = buf.at[(x + NX - i) % NX]
            send(ref, ref, sems[0].at[t, base + i], sems[1].at[t, base + i], other_core).wait_recv()

    def y_send(ref, sems, t, base):
        for i in (2, 1, 3):
            send(ref, ref, sems[0].at[t, base + i], sems[1].at[t, base + i], dev(y=(y + i) % NY)).start()

    def y_wait(buf, sems, t, base):
        for i in range(1, NY):
            ref = buf.at[(y + NY - i) % NY]
            send(ref, ref, sems[0].at[t, base + i], sems[1].at[t, base + i], other_core).wait_recv()

    csem = (sc, rc)
    for t in range(ROUNDS - 1):
        if t > 0:
            g_send(t, grown)
            gather_rest(3)
        py, px = partner(t)
        xbufs[t][x] = carried(t)
        x_send(xbufs[t].at[x], csem, t, 0)
        if t == 0:
            gather_rest(1)
        else:
            gather_rest(4)
            affinities(2)
        x_wait(xbufs[t], csem, t, 0)
        ybufs[t][y] = xbufs[t][px]
        y_send(ybufs[t].at[y], csem, t, 4)
        if t == 0:
            gather_rest(2)
            affinities(1)
        y_wait(ybufs[t], csem, t, 4)
        grown = grown + ybufs[t][py].astype(jnp.float32)

    t = ROUNDS - 1
    py, px = partner(t)
    g_send(t, grown)
    gx[x] = grown
    x_send(gx.at[x], csem, ROUNDS, 0)

    @pl.when(stays)
    def _():
        gback[...] = grown

    @pl.when(moved)
    def _():
        gsend[1] = grown
        send(gsend.at[1], gback, s1.at[TRADE + 3], r1.at[TRADE + 3], twin).start()

    x_wait(gx, csem, ROUNDS, 0)
    gy[y] = gx[px]
    y_send(gy.at[y], csem, ROUNDS, 4)
    came = carried(t)
    xbufs[t][x] = came
    x_send(xbufs[t].at[x], csem, t, 0)
    y_wait(gy, csem, ROUNDS, 4)
    before = gy[py]
    after = before + came.astype(jnp.float32)

    top = jnp.where(lane < k, before, pltpu.roll(after, k, 1))
    bottom = jnp.where(lane < k, pltpu.roll(before, k, 1), after)
    prod[...] = (dot32(top, top, TN) + dot32(bottom, bottom, TN)).reshape(prod.shape)

    def total(ref, count):
        value = ref[0]
        for i in range(1, count):
            value = value + ref[i]
        return value

    group = 2 * NX * 2
    place = q * 2 + yl
    line = (z * 2 + yh) % group

    def near_dev(i):
        there = (place + i) % group
        return there, dev(y=yh * 2 + there % 2, x=there // 4, c=there // 2 % 2)

    def far_dev(i):
        there = (line + i) % group
        return dev(y=there % 2 * 2 + yl, z=there // 2)

    for i in range(1, group):
        there, device = near_dev(i)
        send(prod.at[there], rs.at[place], sa.at[i], ra.at[i], device).start()
    rs[place] = prod[place]

    x_wait(xbufs[t], csem, t, 0)
    homeward[...] = xbufs[t][px]

    @pl.when(stays)
    def _():
        ybufs[t][y] = homeward[...]

    def home_copy(i):
        ty = (y + i) % NY
        device = dev(y=(ty // 2) * 2 + c, c=ty % 2)
        return send(homeward, ybufs[t].at[y], sc.at[t, 4 + i], rc.at[t, 4 + i], device)

    @pl.when(moved)
    def _():
        home_copy(0).start()

    for i in range(1, NY):
        home_copy(i).start()

    for i in range(1, group):
        send(prod.at[0], rs.at[(place + group - i) % group], sa.at[i], ra.at[i], other_core).wait_recv()
    zs[line] = total(rs, group)

    for i in (8, 7, 9, 6, 10, 5, 11, 4, 12, 3, 13, 2, 14, 1, 15):
        ref = zs.at[line]
        send(ref, ref, sa.at[group + i], ra.at[group + i], far_dev(i)).start()
    for i in range(1, group):
        ref = zs.at[(line + group - i) % group]
        send(ref, ref, sa.at[group + i], ra.at[group + i], other_core).wait_recv()
    fin[place] = total(zs, group)

    for i in range(1, group):
        ref = fin.at[place]
        send(ref, ref, sa.at[2 * group + i], ra.at[2 * group + i], near_dev(i)[1]).start()

    @pl.when(moved)
    def _():
        send(gsend.at[1], gback, s1.at[TRADE + 3], r1.at[TRADE + 3], twin).wait_recv()
        ref = ybufs[t].at[twin_y]
        send(ref, ref, sc.at[t, 4], rc.at[t, 4], other_core).wait_recv()

    for i in range(1, NY):
        ref = ybufs[t].at[(twin_y + NY - i) % NY]
        send(ref, ref, sc.at[t, 4 + i], rc.at[t, 4 + i], other_core).wait_recv()
    m = masks[t]
    result[...] = gback[...] + ybufs[t][twin_y ^ ((m // 8) * 2 + m % 2)].astype(jnp.float32)
    rows_copy = pltpu.make_async_copy(result, rows_out, s_in.at[3])
    rows_copy.start()

    for i in range(1, group):
        ref = fin.at[(place + group - i) % group]
        send(ref, ref, sa.at[2 * group + i], ra.at[2 * group + i], other_core).wait_recv()

    sums_copy = pltpu.make_async_copy(fin, sums_out, s_in.at[4])
    sums_copy.start()

    assert not pending

    @pl.when(stays)
    def _():
        all_sent(sent_if_stays)

    @pl.when(moved)
    def _():
        all_sent(sent_if_moved)
        trade.wait_send()
        send(gsend.at[1], gback, s1.at[TRADE + 3], r1.at[TRADE + 3], twin).wait_send()
        home_copy(0).wait_send()

    @pl.loop(1, NX)
    def _(i):
        for row in range(ROUNDS):
            ref = xbufs[row].at[x]
            send(ref, ref, sc.at[row, i], rc.at[row, i], other_core).wait_send()
            send(ref, ref, sc.at[row, 4 + i], rc.at[row, 4 + i], other_core).wait_send()
        ref = gx.at[x]
        send(ref, ref, sc.at[ROUNDS, i], rc.at[ROUNDS, i], other_core).wait_send()
        send(ref, ref, sc.at[ROUNDS, 4 + i], rc.at[ROUNDS, 4 + i], other_core).wait_send()

    @pl.loop(1, NZ)
    def _(i):
        for row in range(ROUNDS):
            ref = gpart.at[row, z]
            send(ref, ref, sg.at[row, i], rg.at[row, i], other_core).wait_send()

    @pl.loop(1, group)
    def _(i):
        for base in range(3):
            ref = fin.at[place]
            send(ref, ref, sa.at[base * group + i], ra.at[base * group + i], other_core).wait_send()

    for row in range(ROUNDS):
        send(wsend.at[row], wrecv.at[row], sw.at[row], rw.at[row], other_core).wait_send()
    rows_copy.wait()
    sums_copy.wait()


def inverse_factors(grams):
    k = grams[0].shape[0]
    row = lax.broadcasted_iota(jnp.int32, (k, 2 * k), 0)
    lane = lax.broadcasted_iota(jnp.int32, (k, 2 * k), 1)
    identity = jnp.where(lane == row, 1.0, 0.0)[:, :k]
    works = [jnp.concatenate([gram, identity], axis=1) for gram in grams]
    works = [[work[8 * g:8 * g + 8] for g in range(k // 8)] for work in works]
    below = lax.broadcasted_iota(jnp.int32, (8, 1), 0)
    for i in range(k - 1):
        own, s = i // 8, i % 8
        for work in works:
            pivot = work[own][s:s + 1, :] * (1.0 / work[own][s:s + 1, i:i + 1])
            for g in range(own, k // 8):
                factor = work[g][:, i:i + 1]
                if g == own:
                    factor = jnp.where(below > s, factor, 0.0)
                work[g] = work[g] - factor * pivot
    results = []
    for work in works:
        whole = jnp.concatenate(work, axis=0)
        diagonal = jnp.sum(jnp.where(lane == row, whole, 0.0), axis=1, keepdims=True)
        results.append(whole[:, k:] * (1.0 / jnp.sqrt(diagonal)))
    return results


def finish_kernel(total_rows, grown_hbm, sums, iterate_t, ritz, grown, sem):
    k = ritz.shape[0]
    half = grown.shape[0]
    copy = pltpu.make_async_copy(grown_hbm, grown, sem)
    copy.start()
    every = sums[...].reshape(2 * k, 2 * k) * (1.0 / total_rows)
    inv_before, inv_last = inverse_factors([every[:k, :k], every[k:, k:]])
    copy.wait()
    packed = grown[...]
    iterate_t[:, :half] = dot32(inv_last, packed[:, :k], NT)
    iterate_t[:, half:] = dot32(inv_last, packed[:, k:], NT)
    left = dot32(inv_before, every[:k, k:], (((1,), (0,)), ((), ())))
    ritz[...] = dot32(left, inv_before, NT)


def shards(shots, basis, round_masks):
    n, feat = shots.shape
    k = basis.shape[1]
    nrep, nown = lax.axis_size("rep"), lax.axis_size("owner")
    half, n0 = n // 2, n * 11 // 16
    bf, f32 = jnp.bfloat16, jnp.float32
    vmem, hbm = pl.BlockSpec(memory_space=pltpu.VMEM), pl.BlockSpec(memory_space=pltpu.HBM)
    slab = (2 * k) // 16
    dma = pltpu.SemaphoreType.DMA
    grown, total_sums = pl.pallas_call(
        functools.partial(rounds_kernel, SHARPNESS / math.sqrt(feat)),
        out_shape=(jax.ShapeDtypeStruct((half, 2 * k), f32), jax.ShapeDtypeStruct((16, slab, 2 * k), f32)),
        in_specs=[hbm] * 3,
        out_specs=(hbm, hbm),
        scratch_shapes=[
            pltpu.SMEM((ROUNDS,), jnp.int32),
            pltpu.VMEM((n, feat), bf),
            pltpu.VMEM((k, n), f32),
            pltpu.VMEM((n, feat), bf),
            pltpu.VMEM((NX, n0, feat), bf),
            pltpu.VMEM((NY, n - n0, feat), bf),
            [pltpu.VMEM((NY, n0, feat), bf)] * ROUNDS,
            [pltpu.VMEM((NX, 2, n - n0, feat), bf)] * ROUNDS,
            pltpu.VMEM((NZ, n, feat), bf),
            [pltpu.VMEM((2, 2, n, feat), bf)] * ROUNDS,
            pltpu.VMEM((ROUNDS, 2, n, NZ * n), bf),
            pltpu.VMEM((ROUNDS, NZ, half, 2 * k), bf),
            pltpu.VMEM((NZ * n, 2 * k), bf),
            pltpu.VMEM((ROUNDS, n, 2 * k), f32),
            pltpu.VMEM((ROUNDS, n, 2 * k), f32),
            [pltpu.VMEM((NX, half, 2 * k), bf)] * ROUNDS,
            [pltpu.VMEM((NY, half, 2 * k), bf)] * ROUNDS,
            pltpu.VMEM((half, 2 * k), bf),
            pltpu.VMEM((half, 2 * k), f32),
            pltpu.VMEM((2, half, 2 * k), f32),
            pltpu.VMEM((half, 2 * k), f32),
            pltpu.VMEM((NX, half, 2 * k), f32),
            pltpu.VMEM((NY, half, 2 * k), f32),
            [pltpu.VMEM((16, slab, 2 * k), f32)] * 4,
            pltpu.VMEM((half, 2 * k), f32),
            dma((5,)),
            dma((56,)), dma((56,)),
            dma((ROUNDS, NZ)), dma((ROUNDS, NZ)),
            dma((ROUNDS + 1, 8)), dma((ROUNDS + 1, 8)),
            dma((ROUNDS,)), dma((ROUNDS,)),
            dma((48,)), dma((48,)),
        ],
        compiler_params=pltpu.CompilerParams(
            collective_id=0, has_side_effects=True, vmem_limit_bytes=60 * 1024 * 1024
        ),
        name="rounds",
    )(round_masks, shots, basis.T)
    iterate_t, ritz = pl.pallas_call(
        functools.partial(finish_kernel, float(nown * nrep * n)),
        out_shape=(jax.ShapeDtypeStruct((k, n), f32), jax.ShapeDtypeStruct((k, k), f32)),
        in_specs=[hbm, vmem],
        out_specs=(vmem, vmem),
        scratch_shapes=[pltpu.VMEM((half, 2 * k), f32), pltpu.SemaphoreType.DMA],
        name="finish",
    )(grown, total_sums)
    return iterate_t.T, ritz


def solution(mesh):
    in_specs = (P(("owner", "rep"), None), P(("owner", "rep"), None), P())
    out_specs = (P(("owner", "rep"), None), P())
    return jax.shard_map(shards, mesh=mesh, in_specs=in_specs, out_specs=out_specs, check_vma=False)
```
